32 devices in a mesh: rep: 2 (over y), fsdp: 16 (over z, x, core).
Axes of the slice: x: 2, y: 2, z: 4, core: 2. Of those that a mesh axis runs over, the one named last changes fastest.
Arguments:
- tokens: bfloat16 [8192, 1536], P(('rep', 'fsdp')), may hold values from -6 to 6
- doc_ids: int32 [8192], P(('rep', 'fsdp')), may hold values from 0 to 127, never falling along the last dimension, each value on 1 to 256 neighbouring positions
- norm_gain: bfloat16 [1536], P('fsdp'), may hold values from 0.5 to 1.5
- qkv_weight: bfloat16 [1536, 4608], P(None, 'fsdp'), may hold values from -0.15625 to 0.15625
- group_gain: bfloat16 [1536], P('fsdp'), may hold values from 0.5 to 1.5
- out_weight: bfloat16 [1536, 1536], P(None, 'fsdp'), may hold values from -0.15625 to 0.15625
- ffn_gain: bfloat16 [1536], P('fsdp'), may hold values from 0.5 to 1.5
- gate_weight: bfloat16 [1536, 4096], P(None, 'fsdp'), may hold values from -0.15625 to 0.15625
- up_weight: bfloat16 [1536, 4096], P(None, 'fsdp'), may hold values from -0.15625 to 0.15625
- down_weight: bfloat16 [4096, 1536], P('fsdp'), may hold values from -0.09375 to 0.09375
- conv_kernel: float32 [16, 66], replicated, may hold values from -1.5 to 1.5
- head_mix: float32 [8, 2, 2], replicated, may hold values from 0.25 to 1
- out_grad: float32 [8192, 1536], P(('rep', 'fsdp')), may hold values from -6 to 6
Outputs:
- layer_out: bfloat16 [8192, 1536], P(('rep', 'fsdp'))
- input_grad: float32 [8192, 1536], P(('rep', 'fsdp'))
- norm_gain_grad: float32 [1536], P('fsdp')
- qkv_weight_grad: float32 [1536, 4608], P(None, 'fsdp')
- group_gain_grad: float32 [1536], P('fsdp')
- out_weight_grad: float32 [1536, 1536], P(None, 'fsdp')
- ffn_gain_grad: float32 [1536], P('fsdp')
- gate_weight_grad: float32 [1536, 4096], P(None, 'fsdp')
- up_weight_grad: float32 [1536, 4096], P(None, 'fsdp')
- down_weight_grad: float32 [4096, 1536], P('fsdp')
- conv_kernel_grad: float32 [16, 66], replicated
- head_mix_grad: float32 [8, 2, 2], replicated
The draws below stay inside these ranges and needn't reach their ends.
Inputs may be any that keep to these rules, and one draw needn't show every extreme that they name: `doc_ids`: document numbers never fall along the tokens; each document has 1 to 256 tokens.
All inputs are finite; a program needn't handle non-finite values.
Results may differ from the reference program's by a relative error of at most 0.018.
The reference program's roundings to bfloat16 on the way count: a program that leaves them out, or rounds other values in their place, can miss the bound.
Values may be sent and summed in bfloat16 or wider, within the bound.
No kernel may reach another device: no remote copies, remote signals or barrier semaphores. Data moves between devices by JAX's collectives and lax.ppermute only.
A program may use at most 320 MiB of HBM per device.

```python
import math
import jax
import jax.numpy as jnp
import numpy as np
from jax import lax

D = 1536
H = 16
HD = 96
FF = 4096
CQ = 6
CK = 11
SEQ = 256
TOKENS = 8192
DOCS = 128
N_REP = 2
N_FSDP = 16


def block_levels(own_key, shape, cuts, low, top_value):
    loudness, own = 1.0, jax.random.fold_in(own_key, 6)
    for position, parts in cuts:
        steps = jnp.exp(jax.random.uniform(jax.random.fold_in(own, position), (parts,), jnp.float32, low / len(cuts), top_value / len(cuts)))
        loudness = loudness * jnp.repeat(steps, shape[position] // parts).reshape([-1 if axis == position else 1 for axis in range(len(shape))])
    return loudness


def split_up(number_of, total, most, lean):
    portions = [(1 << 20) // math.isqrt(rank ** lean) + 1 for rank in range(2, number_of + 1)]
    surplus, given = total - most - (number_of - 1), [1] * (number_of - 1)
    while surplus > 0:
        candidates = [i for i in range(number_of - 1) if given[i] < most]
        pool, remaining = sum([portions[i] for i in candidates]), surplus
        for i in candidates:
            addition = min(most - given[i], max(1, remaining * portions[i] // pool), surplus)
            given[i] = given[i] + addition
            surplus = surplus - addition
    return np.array([most] + given)


def ragged_sizes(stream_key, number_of, total, most, slope):
    if number_of == 2:
        one = jax.random.randint(stream_key, (), max(1, total - most), min(most, total - 1) + 1)
        return jnp.stack([one, total - one])
    sizes = jnp.asarray(split_up(number_of, total, most, slope), jnp.int32)
    twos = (number_of - 1) // 2
    source_of, taker = sizes[1:1 + 2 * twos:2], sizes[2:2 + 2 * twos:2]
    room = jnp.minimum(source_of - 1, most - taker)
    moved = jax.random.randint(jax.random.fold_in(stream_key, 1), (twos,), 0, 1 << 20) % (room + 1)
    sizes = sizes.at[1:1 + 2 * twos:2].set(source_of - moved).at[2:2 + 2 * twos:2].set(taker + moved)
    return sizes[jax.random.permutation(jax.random.fold_in(stream_key, 2), number_of)]


def bell_draw(key, shape, scale, most, pieces=(), kind=jnp.bfloat16):
    level = block_levels(key, shape, pieces, -0.22, 0.18) if pieces else 1.0
    array = jax.random.normal(key, shape, jnp.float32) * scale * level
    return jnp.minimum(jnp.maximum(array, -most), most).astype(kind)


def setup_inputs(seed: int = 0) -> dict:
    splits = jax.random.split(jax.random.key(seed), 14)
    return {
        "tokens": bell_draw(splits[0], (TOKENS, D), 1.0, 6.0, ((0, 32),)),
        "doc_ids": jnp.searchsorted(jnp.cumsum(ragged_sizes(splits[1], DOCS, TOKENS, SEQ, 2)), jnp.arange(TOKENS), side="right").astype(jnp.int32),
        "norm_gain": jnp.clip(1.0 + 0.1 * jax.random.normal(splits[2], (D,), jnp.float32), 0.5, 1.5).astype(jnp.bfloat16),
        "qkv_weight": bell_draw(splits[3], (D, 3 * D), D ** -0.5, 0.15625, ((1, 16),)),
        "group_gain": jnp.clip(1.0 + 0.1 * jax.random.normal(splits[4], (D,), jnp.float32), 0.5, 1.5).astype(jnp.bfloat16),
        "out_weight": bell_draw(splits[5], (D, D), D ** -0.5, 0.15625, ((1, 16),)),
        "ffn_gain": jnp.clip(1.0 + 0.1 * jax.random.normal(splits[6], (D,), jnp.float32), 0.5, 1.5).astype(jnp.bfloat16),
        "gate_weight": bell_draw(splits[7], (D, FF), D ** -0.5, 0.15625, ((1, 16),)),
        "up_weight": bell_draw(splits[8], (D, FF), D ** -0.5, 0.15625, ((1, 16),)),
        "down_weight": bell_draw(splits[9], (FF, D), FF ** -0.5, 0.09375, ((0, 16),)),
        "conv_kernel": bell_draw(splits[10], (H, CQ * CK), 0.25, 1.5, (), jnp.float32),
        "head_mix": jnp.clip(jax.random.uniform(splits[11], (H // 2, 2, 2), jnp.float32, 0.25, 1.0), 0.25, 1.0),
        "out_grad": bell_draw(splits[12], (TOKENS, D), 1.0, 6.0, ((0, 32),), jnp.float32),
    }


@jax.custom_vjp
def low(v):
    return lax.optimization_barrier(v.astype(jnp.bfloat16)).astype(jnp.float32)

@jax.custom_vjp
def low_back(v):
    return v

def low_keep(v):
    return (low(v), None)

def low_pass(kept, grad):
    return (grad,)

def back_keep(v):
    return (v, None)

def back_low(kept, grad):
    return (low(grad),)
low.defvjp(low_keep, low_pass)
low_back.defvjp(back_keep, back_low)

def rms_norm(values, gain):
    return values * lax.rsqrt(lax.optimization_barrier(jnp.mean(values * values, axis=-1, keepdims=True)) + 1e-05) * gain

def group_norm(values, gain):
    centre = values - lax.optimization_barrier(jnp.mean(values, axis=-1, keepdims=True))
    spread = lax.optimization_barrier(jnp.mean(centre * centre, axis=-1, keepdims=True))
    return centre * lax.rsqrt(spread + 1e-05) * gain

def mixed_probs(logits, row_doc, row_pos, key_doc, kernel, mixing):
    head_count, ext_count, key_count = logits.shape
    row_lag = CQ - 1
    row_count = ext_count - row_lag
    key_left = CK // 2
    key_place = jnp.arange(key_count, dtype=jnp.int32)
    allowed = (key_place[None, :] <= row_pos[:, None]) & (key_doc[None, :] == row_doc[:, None])
    masked = jnp.where(allowed[None], logits, 0.0)
    padded = jnp.pad(masked, ((0, 0), (0, 0), (key_left, CK - 1 - key_left)))
    out_doc = row_doc[row_lag:]
    summed = jnp.zeros((head_count, row_count, key_count), logits.dtype)
    for shift in range(CQ):
        same_doc = (row_doc[row_lag - shift:row_lag - shift + row_count] == out_doc).astype(logits.dtype)
        partial_sum = jnp.zeros((head_count, row_count, key_count), logits.dtype)
        for column in range(CK):
            offset = 2 * key_left - column
            partial_sum = partial_sum + kernel[:, shift * CK + column][:, None, None] * padded[:, row_lag - shift:row_lag - shift + row_count, offset:offset + key_count]
        summed = summed + same_doc[None, :, None] * partial_sum
    scores = jnp.where(allowed[None, row_lag:], summed, -1e+30)
    row_max = lax.optimization_barrier(jnp.max(scores, axis=-1, keepdims=True))
    weights = jnp.exp(scores - row_max)
    attend = weights / lax.optimization_barrier(jnp.sum(weights, axis=-1, keepdims=True))
    grouped = attend.reshape(head_count // 2, 2, row_count, key_count)
    mixed = jnp.einsum('gcd,gdrk->gcrk', mixing, grouped, precision=lax.Precision.HIGHEST)
    return mixed.reshape(head_count, row_count, key_count)

def reference(tokens, doc_ids, norm_gain, qkv_weight, group_gain, out_weight, ffn_gain, gate_weight, up_weight, down_weight, conv_kernel, head_mix, out_grad):
    row_total = N_REP * N_FSDP
    docs = doc_ids.reshape(row_total, SEQ).astype(jnp.int32)
    scale = HD ** (-0.5)
    highest = lax.Precision.HIGHEST

    def forward(inputs, gain_one, w_qkv, gain_group, w_out, gain_two, w_gate, w_up, w_down, kernel, mixing):

        def attend_row(item):
            packed_row, row_docs = item
            queries = packed_row[:, :D].reshape(SEQ, H, HD)
            key_vecs = packed_row[:, D:2 * D].reshape(SEQ, H, HD)
            values = packed_row[:, 2 * D:].reshape(SEQ, H, HD)
            logits = low_back(jnp.einsum('qhd,khd->hqk', queries, key_vecs, precision=highest) * scale)
            extended = jnp.pad(logits, ((0, 0), (CQ - 1, 0), (0, 0)))
            row_doc = jnp.concatenate([jnp.full((CQ - 1,), -1, jnp.int32), row_docs])
            row_pos = jnp.arange(1 - CQ, SEQ, dtype=jnp.int32)
            mixed = mixed_probs(extended, row_doc, row_pos, row_docs, kernel, mixing)
            output = jnp.einsum('hqk,khd->qhd', low(mixed), values, precision=highest)
            return low_back(output.reshape(SEQ, D))
        normed = low(rms_norm(inputs, gain_one))
        packed = low(low_back(jnp.einsum('rsd,de->rse', normed, w_qkv, precision=highest)))
        attended = lax.map(jax.checkpoint(attend_row), (packed, docs))
        grouped = group_norm(attended.reshape(row_total, SEQ, H, HD), gain_group.reshape(H, HD))
        grouped = low(grouped.reshape(row_total, SEQ, D))
        branch = low_back(jnp.einsum('rsd,de->rse', grouped, w_out, precision=highest))
        middle = inputs + branch
        second = low(rms_norm(middle, gain_two))
        gate = low_back(jnp.einsum('rsd,df->rsf', second, w_gate, precision=highest))
        upper = low_back(jnp.einsum('rsd,df->rsf', second, w_up, precision=highest))
        hidden = low(jax.nn.silu(gate) * upper)
        ffn_out = low_back(jnp.einsum('rsf,fd->rsd', hidden, w_down, precision=highest))
        return middle + ffn_out
    floats = (tokens.reshape(row_total, SEQ, D).astype(jnp.float32), norm_gain.astype(jnp.float32), qkv_weight.astype(jnp.float32), group_gain.astype(jnp.float32), out_weight.astype(jnp.float32), ffn_gain.astype(jnp.float32), gate_weight.astype(jnp.float32), up_weight.astype(jnp.float32), down_weight.astype(jnp.float32), conv_kernel.astype(jnp.float32), head_mix.astype(jnp.float32))
    result, pullback = jax.vjp(forward, *floats)
    grads = pullback(out_grad.reshape(row_total, SEQ, D).astype(jnp.float32))
    return (result.reshape(TOKENS, D).astype(jnp.bfloat16), grads[0].reshape(TOKENS, D), grads[1], grads[2], grads[3], grads[4], grads[5], grads[6], grads[7], grads[8], grads[9], grads[10])
```

```python
import functools
import jax
import jax.numpy as jnp
from jax import lax
from jax.experimental import pallas as pl
from jax.experimental.pallas import tpu as pltpu
from jax.sharding import PartitionSpec as P

D = 1536
H = 16
HD = 96
CQ = 6
CK = 11
NEG = -1e30
PAIRS = H // 2
PW = 2 * HD
BF = jnp.bfloat16
F32 = jnp.float32


def dot(a, b, ca, cb):
    return lax.dot_general(a, b, (((ca,), (cb,)), ((), ())), preferred_element_type=F32)


def split(v):
    hi = v.astype(BF)
    return hi, (v - hi.astype(F32)).astype(BF)


def taps_kernel(fwd_ref, bwd_ref, th_ref, tl_ref, tt_ref):
    n = th_ref.shape[-1]
    row = lax.broadcasted_iota(jnp.int32, (n, n), 0)
    col = lax.broadcasted_iota(jnp.int32, (n, n), 1)
    near = jnp.abs(row - col) <= CK // 2
    for a in range(CQ):
        wide = jnp.broadcast_to(fwd_ref[0, a : a + 1, :], (n, n))
        band = jnp.where(near, pltpu.roll(wide, 0, 1, stride=1, stride_axis=0), 0.0)
        hi, lo = split(band)
        th_ref[0, a * n : (a + 1) * n, :] = hi
        tl_ref[0, a * n : (a + 1) * n, :] = lo
        wide = jnp.broadcast_to(bwd_ref[0, a : a + 1, :], (n, n))
        band = jnp.where(near, pltpu.roll(wide, 0, 1, stride=1, stride_axis=0), 0.0)
        tt_ref[0, a * n : (a + 1) * n, :] = band.astype(BF)


def band_taps(kernel, n):
    taps = kernel.reshape(H, CQ, CK)
    half = CK // 2
    fwd = jnp.zeros((H, 8, n), F32)
    fwd = fwd.at[:, :CQ, : half + 1].set(taps[:, :, half:]).at[:, :CQ, n - half :].set(taps[:, :, :half])
    flip = taps[:, :, ::-1]
    bwd = jnp.zeros((H, 8, n), F32)
    bwd = bwd.at[:, :CQ, : half + 1].set(flip[:, :, half:]).at[:, :CQ, n - half :].set(flip[:, :, :half])
    row = pl.BlockSpec((1, 8, n), lambda h: (h, 0, 0))
    out = pl.BlockSpec((1, CQ * n, n), lambda h: (h, 0, 0))
    shape = jax.ShapeDtypeStruct((H, CQ * n, n), BF)
    return pl.pallas_call(
        taps_kernel,
        grid=(H,),
        in_specs=[row, row],
        out_specs=[out, out, out],
        out_shape=[shape, shape, shape],
        cost_estimate=pl.CostEstimate(flops=H * 12 * n * n, bytes_accessed=6 * H * CQ * n * n, transcendentals=0),
    )(fwd, bwd)


def doc_masks(drow_ref, dcol_ref, allow_ref, same_ref):
    n = allow_ref.shape[0]
    row = lax.broadcasted_iota(jnp.int32, (n, n), 0)
    col = lax.broadcasted_iota(jnp.int32, (n, n), 1)
    same = dcol_ref[...] == drow_ref[...]
    same_ref[...] = jnp.where(same, 1.0, 0.0)
    allow_ref[...] = jnp.where(same & (col <= row), 1.0, 0.0)


def attend_kernel(
    mix_ref, q_ref, k_ref, v_ref, th_ref, tl_ref, drow_ref, dcol_ref, gain_ref,
    prob_ref, att_ref, grp_ref, allow_ref, same_ref, pad_ref, xh_ref, xl_ref,
):
    g = pl.program_id(0)
    n = q_ref.shape[1]

    @pl.when(g == 0)
    def _():
        doc_masks(drow_ref, dcol_ref, allow_ref, same_ref)
        pad_ref[0:8, :] = jnp.zeros((8, n), F32)

    for e in range(2):
        q = q_ref[e * HD : (e + 1) * HD, :]
        k = k_ref[e * HD : (e + 1) * HD, :]
        logits = dot(q, k, 0, 0) * (HD ** (-0.5))
        pad_ref[8 : 8 + n, :] = jnp.where(allow_ref[...] > 0, logits, 0.0)
        for a in range(CQ):
            part = jnp.where(same_ref[...] > 0, pad_ref[8 - a : 8 - a + n, :], 0.0)
            hi, lo = split(part)
            xh_ref[:, a * n : (a + 1) * n] = hi
            xl_ref[:, a * n : (a + 1) * n] = lo
        conv = (
            dot(xh_ref[...], th_ref[e], 1, 0)
            + dot(xh_ref[...], tl_ref[e], 1, 0)
            + dot(xl_ref[...], th_ref[e], 1, 0)
        )
        scores = jnp.where(allow_ref[...] > 0, conv, NEG)
        weights = jnp.exp(scores - jnp.max(scores, axis=1, keepdims=True))
        prob_ref[e] = weights * (1.0 / jnp.sum(weights, axis=1, keepdims=True))
    for c in range(2):
        mixed = (mix_ref[g, 2 * c] * prob_ref[0] + mix_ref[g, 2 * c + 1] * prob_ref[1]).astype(BF)
        att = dot(v_ref[c * HD : (c + 1) * HD, :], mixed, 1, 1)
        att_ref[c * HD : (c + 1) * HD, :] = att
        centre = att - jnp.mean(att, axis=0, keepdims=True)
        spread = jnp.mean(centre * centre, axis=0, keepdims=True)
        grp_ref[c * HD : (c + 1) * HD, :] = (
            centre * lax.rsqrt(spread + 1e-05) * gain_ref[c * HD : (c + 1) * HD, :]
        ).astype(BF)


def attend(packed_t, docs, th, tl, mix, gain):
    n = packed_t.shape[1]
    blk = lambda off: pl.BlockSpec((PW, n), lambda g: (g + off, 0))
    tap = pl.BlockSpec((2, CQ * n, n), lambda g: (g, 0, 0))
    whole = lambda s: pl.BlockSpec(s, lambda g: (0, 0))
    return pl.pallas_call(
        attend_kernel,
        grid=(PAIRS,),
        in_specs=[
            pl.BlockSpec(memory_space=pltpu.SMEM),
            blk(0), blk(PAIRS), blk(2 * PAIRS), tap, tap,
            whole((1, n)), whole((n, 1)),
            pl.BlockSpec((PW, 1), lambda g: (g, 0)),
        ],
        out_specs=[pl.BlockSpec((2, n, n), lambda g: (g, 0, 0)), blk(0), blk(0)],
        out_shape=[
            jax.ShapeDtypeStruct((H, n, n), F32),
            jax.ShapeDtypeStruct((D, n), F32),
            jax.ShapeDtypeStruct((D, n), BF),
        ],
        scratch_shapes=[
            pltpu.VMEM((n, n), F32), pltpu.VMEM((n, n), F32), pltpu.VMEM((n + 8, n), F32),
            pltpu.VMEM((n, CQ * n), BF), pltpu.VMEM((n, CQ * n), BF),
        ],
        compiler_params=pltpu.CompilerParams(vmem_limit_bytes=40 * 2**20),
        cost_estimate=pl.CostEstimate(flops=42 * H * n * n * n, bytes_accessed=34 * 2**20, transcendentals=H * n * n),
    )(mix.reshape(PAIRS, 4), packed_t, packed_t, packed_t, th, tl, docs.reshape(1, n), docs.reshape(n, 1), gain)


def attend_back_kernel(
    mix_ref, q_ref, k_ref, v_ref, tt_ref, drow_ref, dcol_ref, gain_ref, prob_ref, att_ref, dgrp_ref,
    dq_ref, dk_ref, dv_ref, dgain_ref, dtap_ref, dmix_ref,
    allow_ref, same_ref, pad_ref, y_ref, dm_ref,
):
    g = pl.program_id(0)
    n = q_ref.shape[1]
    scale = HD ** (-0.5)

    @pl.when(g == 0)
    def _():
        doc_masks(drow_ref, dcol_ref, allow_ref, same_ref)
        pad_ref[n : n + 8, :] = jnp.zeros((8, n), F32)

    for c in range(2):
        rows = slice(c * HD, (c + 1) * HD)
        att = att_ref[rows, :]
        centre = att - jnp.mean(att, axis=0, keepdims=True)
        rstd = lax.rsqrt(jnp.mean(centre * centre, axis=0, keepdims=True) + 1e-05)
        hat = centre * rstd
        dgrp = dgrp_ref[rows, :]
        dgain_ref[rows, :] = jnp.sum(dgrp * hat, axis=1, keepdims=True)
        dhat = dgrp * gain_ref[rows, :]
        datt = rstd * (
            dhat
            - jnp.mean(dhat, axis=0, keepdims=True)
            - hat * jnp.mean(dhat * hat, axis=0, keepdims=True)
        )
        datt = datt.astype(BF)
        mixed = (mix_ref[g, 2 * c] * prob_ref[0] + mix_ref[g, 2 * c + 1] * prob_ref[1]).astype(BF)
        dv_ref[rows, :] = dot(datt, mixed, 1, 0).astype(BF)
        dmixed = dot(datt, v_ref[rows, :], 0, 0)
        dm_ref[c] = dmixed
        for e in range(2):
            dmix_ref[0, 2 * c + e : 2 * c + e + 1, :] = jnp.sum(dmixed * prob_ref[e], axis=0, keepdims=True)
    dmix_ref[0, 4:8, :] = jnp.zeros((4, n), F32)
    row = lax.broadcasted_iota(jnp.int32, (128, 128), 0)
    col = lax.broadcasted_iota(jnp.int32, (128, 128), 1)
    off = col - row
    half = CK // 2
    for e in range(2):
        rows = slice(e * HD, (e + 1) * HD)
        q = q_ref[rows, :]
        k = k_ref[rows, :]
        allowed = allow_ref[...] > 0
        masked_t = dot(k, q, 0, 0) * scale
        prob = prob_ref[e]
        dprob = mix_ref[g, e] * dm_ref[0] + mix_ref[g, 2 + e] * dm_ref[1]
        pad_ref[0:n, :] = prob * (dprob - jnp.sum(prob * dprob, axis=1, keepdims=True))
        for a in range(CQ):
            y_ref[:, a * n : (a + 1) * n] = jnp.where(same_ref[...] > 0, pad_ref[a : a + n, :], 0.0).astype(BF)
        dlog = jnp.where(allowed, dot(y_ref[...], tt_ref[e], 1, 0), 0.0).astype(BF)
        dq_ref[rows, :] = (dot(k, dlog, 1, 1) * scale).astype(BF)
        dk_ref[rows, :] = (dot(q, dlog, 1, 0) * scale).astype(BF)
        krow = lax.broadcasted_iota(jnp.int32, (n, n), 0)
        qcol = lax.broadcasted_iota(jnp.int32, (n, n), 1)
        masked_t = jnp.where((same_ref[...] > 0) & (krow <= qcol), masked_t, 0.0).astype(BF)
        for a in range(CQ):
            full = dot(masked_t, y_ref[:, a * n : (a + 1) * n], 1, 0)
            fold = jnp.zeros((128, 128), F32)
            blocks = n // 128
            for r in range(blocks):
                fold = fold + full[r * 128 : (r + 1) * 128, r * 128 : (r + 1) * 128]
            fold = jnp.where(jnp.abs(off) <= half, fold, 0.0)
            for r in range(blocks - 1):
                up = full[r * 128 : (r + 1) * 128, (r + 1) * 128 : (r + 2) * 128]
                down = full[(r + 1) * 128 : (r + 2) * 128, r * 128 : (r + 1) * 128]
                fold = fold + jnp.where(off <= half - 128, up, 0.0) + jnp.where(off >= 128 - half, down, 0.0)
            lined = fold[0:8, :]
            for t in range(1, 16):
                lined = lined + pltpu.roll(fold[8 * t : 8 * t + 8, :], 128 - 8 * t, 1)
            dtap_ref[e, 8 * a : 8 * a + 8, :] = lined


def attend_back(packed_t, docs, tt, mix, gain, prob, att, dgrp):
    n = packed_t.shape[1]
    blk = lambda off: pl.BlockSpec((PW, n), lambda g: (g + off, 0))
    whole = lambda s: pl.BlockSpec(s, lambda g: (0, 0))
    thin = pl.BlockSpec((PW, 1), lambda g: (g, 0))
    dq, dk, dv, dgain, dtap, dmix = pl.pallas_call(
        attend_back_kernel,
        grid=(PAIRS,),
        in_specs=[
            pl.BlockSpec(memory_space=pltpu.SMEM),
            blk(0), blk(PAIRS), blk(2 * PAIRS),
            pl.BlockSpec((2, CQ * n, n), lambda g: (g, 0, 0)),
            whole((1, n)), whole((n, 1)), thin,
            pl.BlockSpec((2, n, n), lambda g: (g, 0, 0)),
            blk(0), blk(0),
        ],
        out_specs=[
            blk(0), blk(0), blk(0), thin,
            pl.BlockSpec((2, 8 * CQ, 128), lambda g: (g, 0, 0)),
            pl.BlockSpec((1, 8, n), lambda g: (g, 0, 0)),
        ],
        out_shape=[
            jax.ShapeDtypeStruct((D, n), BF),
            jax.ShapeDtypeStruct((D, n), BF),
            jax.ShapeDtypeStruct((D, n), BF),
            jax.ShapeDtypeStruct((D, 1), F32),
            jax.ShapeDtypeStruct((H, 8 * CQ, 128), F32),
            jax.ShapeDtypeStruct((PAIRS, 8, n), F32),
        ],
        scratch_shapes=[
            pltpu.VMEM((n, n), F32), pltpu.VMEM((n, n), F32), pltpu.VMEM((n + 8, n), F32),
            pltpu.VMEM((n, CQ * n), BF), pltpu.VMEM((2, n, n), F32),
        ],
        compiler_params=pltpu.CompilerParams(vmem_limit_bytes=40 * 2**20),
        cost_estimate=pl.CostEstimate(flops=40 * H * n * n * n, bytes_accessed=24 * 2**20, transcendentals=0),
    )(mix.reshape(PAIRS, 4), packed_t, packed_t, packed_t, tt, docs.reshape(1, n), docs.reshape(n, 1), gain, prob, att, dgrp)
    lane = jnp.arange(128)[None, None, :] - jnp.arange(8)[None, :, None]
    tap = jnp.arange(CK)[:, None, None] - CK // 2
    pick = (jnp.remainder(lane - tap, 128) == 0).astype(F32)
    dtap = jnp.sum(dtap.reshape(H, CQ, 1, 8, 128) * pick, axis=(3, 4))
    dmix = jnp.sum(dmix[:, :4, :], axis=2)
    return dq, dk, dv, dgain[:, 0], dtap.reshape(H, CQ * CK), dmix.reshape(PAIRS, 2, 2)


def rms_norm(values, gain):
    return values * lax.rsqrt(jnp.mean(values * values, axis=-1, keepdims=True) + 1e-05) * gain


def rms_back(values, gain, grad):
    rstd = lax.rsqrt(jnp.mean(values * values, axis=-1, keepdims=True) + 1e-05)
    hat = values * rstd
    dhat = grad * gain
    dvalues = rstd * (dhat - hat * jnp.mean(dhat * hat, axis=-1, keepdims=True))
    return dvalues, jnp.sum(grad * hat, axis=0)


class Slice:
    def __init__(self, reps, shards):
        self.axes = ("rep", "fsdp")
        self.shards = shards
        self.lines = [[4 * o + i for o in range(shards // 4)] for i in range(4)]
        places = [(y, f) for y in range(reps) for f in range(shards)]

        def perm(move):
            out = []
            for y, f in places:
                to = move(y, f)
                out.append((y * shards + f, to[0] * shards + to[1]))
            return out

        self.hops = {
            (dy, di): perm(lambda y, f, dy=dy, di=di: (y ^ dy, f ^ di))
            for dy in range(2)
            for di in range(4)
        }
        self.corner = perm(lambda y, f: (y, f ^ 2) if f & 1 else (1 - y, f))
        self.doubling = []
        bit = 1
        while bit < shards:
            self.doubling.append((bit, perm(lambda y, f, bit=bit: (y, f ^ bit))))
            bit *= 2
        self.rep = lax.axis_index("rep")
        self.fsdp = lax.axis_index("fsdp")
        self.odd = (self.fsdp & 1) == 1

    def hop(self, value, dy, di):
        return lax.ppermute(value, self.axes, self.hops[dy, di])

    def gather_line(self, value):
        return lax.all_gather(value, "fsdp", axis=0, tiled=True, axis_index_groups=self.lines)

    def scatter_line(self, value):
        return lax.psum_scatter(
            value.astype(BF), "fsdp", scatter_dimension=0, tiled=True, axis_index_groups=self.lines
        )

    def gather_small(self, value):
        for bit, perm in self.doubling:
            other = lax.ppermute(value, self.axes, perm)
            high = (self.fsdp & bit) != 0
            value = jnp.concatenate(
                [jnp.where(high, other, value), jnp.where(high, value, other)], axis=0
            )
        return value

    def gather_plane(self, value):
        along_x = self.hop(value, 0, 2)
        along_y = self.hop(value, 1, 0)
        corner = lax.ppermute(jnp.where(self.odd, along_y, along_x), self.axes, self.corner)
        near = jnp.concatenate([value, along_x, along_y, corner], axis=0)
        return near, self.hop(near, 0, 1)

    def scatter_plane(self, near, far):
        rows = near.shape[0] // 4
        total = near + self.hop(far.astype(BF), 0, 1)
        blocks = [total[b * rows : (b + 1) * rows] for b in range(4)]
        corner = lax.ppermute(blocks[3].astype(BF), self.axes, self.corner).astype(F32)
        along_x = blocks[1] + jnp.where(self.odd, 0.0, corner)
        along_y = blocks[2] + jnp.where(self.odd, corner, 0.0)
        return (
            blocks[0]
            + self.hop(along_x.astype(BF), 0, 2).astype(F32)
            + self.hop(along_y.astype(BF), 1, 0).astype(F32)
        )

    def both_halves(self, half):
        other = self.hop(half, 1, 0)
        first = self.rep == 0
        return jnp.concatenate(
            [jnp.where(first, half, other), jnp.where(first, other, half)], axis=0
        ).astype(F32)

    def own_half(self, shard):
        rows = shard.shape[0] // 2
        return lax.dynamic_slice_in_dim(shard, self.rep * rows, rows, axis=0)


def on_device(
    reps,
    shards,
    tokens,
    doc_ids,
    norm_gain,
    qkv_weight,
    group_gain,
    out_weight,
    ffn_gain,
    gate_weight,
    up_weight,
    down_weight,
    conv_kernel,
    head_mix,
    out_grad,
):
    net = Slice(reps, shards)
    lines = shards // 4
    n = tokens.shape[0]
    cols = 3 * D // shards // 2
    wide = gate_weight.shape[1] // 2

    w_qkv = net.gather_line(net.own_half(qkv_weight.T))
    x_near, x_far = net.gather_plane(tokens)
    gains = net.gather_small(jnp.stack([norm_gain, group_gain, ffn_gain])[None])
    gains = gains.transpose(1, 0, 2).reshape(3, D).astype(F32)
    w_down = net.gather_line(net.own_half(down_weight))
    w_gu = net.gather_line(
        jnp.concatenate([net.own_half(gate_weight.T), net.own_half(up_weight.T)], axis=0)
    )
    w_out = lax.all_gather(out_weight.T, "fsdp", axis=0, tiled=True)
    taps_hi, taps_lo, taps_back = band_taps(conv_kernel, n)
    inputs = tokens.astype(F32)

    normed = [rms_norm(b.astype(F32), gains[0]).astype(BF) for b in (x_near, x_far)]
    parts = [dot(w_qkv, b, 1, 1).astype(BF) for b in normed]
    place = net.rep * 4 + (net.fsdp & 3)
    packed_t = jnp.zeros((lines, 4, 2, cols, n), BF)
    for dy in range(2):
        for di in range(4):
            block = 2 * dy + di // 2
            piece = parts[di % 2][:, block * n : (block + 1) * n]
            if dy or di:
                piece = net.hop(piece, dy, di)
            source = place ^ (4 * dy + di)
            packed_t = lax.dynamic_update_slice(
                packed_t, piece.reshape(lines, 1, 1, cols, n), (0, source & 3, source >> 2, 0, 0)
            )
    packed_t = packed_t.reshape(3 * D, n)
    group_col = gains[1].reshape(D, 1)
    probs, attended, grouped = attend(packed_t, doc_ids, taps_hi, taps_lo, head_mix, group_col)

    middle = inputs + dot(grouped, w_out, 0, 1)
    second_low = rms_norm(middle, gains[2]).astype(BF)
    second = net.gather_plane(second_low)
    d_ffn = net.gather_plane(out_grad.astype(BF))

    hidden, d_gu, d_hid = [], [], [dot(b, w_down, 1, 1) for b in d_ffn]
    for s in range(2):
        gu = dot(second[s], w_gu, 1, 1).reshape(-1, lines, 2, wide)
        gate, upper = gu[:, :, 0], gu[:, :, 1]
        dh = d_hid[s].reshape(-1, lines, wide)
        sig = jax.nn.sigmoid(gate)
        act = gate * sig
        hidden.append((act * upper).astype(BF).reshape(-1, lines * wide))
        d_gate = (dh * upper * (sig * (1.0 + gate * (1.0 - sig)))).astype(BF)
        d_up = (dh * act).astype(BF)
        d_gu.append(jnp.stack([d_gate, d_up], axis=2).reshape(-1, lines * 2 * wide))
    d_second = net.scatter_plane(*[dot(b, w_gu, 1, 0) for b in d_gu])
    ffn_out = net.scatter_plane(*[dot(b, w_down, 1, 0) for b in hidden])
    layer_out = (middle + ffn_out).astype(BF)
    g_down = dot(hidden[0], d_ffn[0], 0, 0) + dot(hidden[1], d_ffn[1], 0, 0)
    g_gu = dot(d_gu[0], second[0], 0, 0) + dot(d_gu[1], second[1], 0, 0)
    g_down = net.both_halves(net.scatter_line(g_down))
    g_gu = net.scatter_line(g_gu)
    g_gate = net.both_halves(g_gu[:wide]).T
    g_up = net.both_halves(g_gu[wide:]).T

    d_norm, g_ffn_gain = rms_back(middle, gains[2], d_second)
    d_middle = out_grad + d_norm
    branch = d_middle.astype(BF)
    d_grouped = dot(w_out, branch, 0, 1)
    g_out = dot(branch, grouped, 0, 1).astype(BF)
    g_out = lax.psum_scatter(g_out, "fsdp", scatter_dimension=0, tiled=True)
    g_out = (g_out.astype(F32) + net.hop(g_out, 1, 0).astype(F32)).T
    d_q, d_k, d_v, g_group, g_taps, g_mix = attend_back(
        packed_t, doc_ids, taps_back, head_mix, group_col, probs, attended, d_grouped
    )

    d_packed = jnp.concatenate([d_q, d_k, d_v], axis=0).reshape(lines, 4, 2, cols, n)
    pieces = [[], []]
    for dy in range(2):
        for di in range(4):
            target = place ^ (4 * dy + di)
            piece = lax.dynamic_slice(
                d_packed, (0, target & 3, target >> 2, 0, 0), (lines, 1, 1, cols, n)
            ).reshape(lines * cols, n)
            if dy or di:
                piece = net.hop(piece, dy, di)
            pieces[di % 2].append(piece)
    d_packed = [jnp.concatenate(p, axis=1) for p in pieces]
    d_normed = net.scatter_plane(*[dot(b, w_qkv, 0, 0) for b in d_packed])
    g_qkv = dot(d_packed[0], normed[0], 1, 0) + dot(d_packed[1], normed[1], 1, 0)
    g_qkv = net.both_halves(net.scatter_line(g_qkv)).T
    d_in, g_norm = rms_back(inputs, gains[0], d_normed)
    input_grad = d_middle + d_in

    small = lax.psum(
        jnp.concatenate([g_norm, g_group, g_ffn_gain, g_taps.reshape(-1), g_mix.reshape(-1)]),
        ("rep", "fsdp"),
    )
    part = D // shards
    gain_grads = [
        lax.dynamic_slice_in_dim(small, b * D + net.fsdp * part, part) for b in range(3)
    ]
    g_taps = small[3 * D : 3 * D + H * CQ * CK].reshape(H, CQ * CK)
    g_mix = small[3 * D + H * CQ * CK :].reshape(PAIRS, 2, 2)
    return (
        layer_out,
        input_grad,
        gain_grads[0],
        g_qkv,
        gain_grads[1],
        g_out,
        gain_grads[2],
        g_gate,
        g_up,
        g_down,
        g_taps,
        g_mix,
    )


def solution(mesh):
    placed = (
        P(("rep", "fsdp"), None),
        P(("rep", "fsdp")),
        P("fsdp"),
        P(None, "fsdp"),
        P("fsdp"),
        P(None, "fsdp"),
        P("fsdp"),
        P(None, "fsdp"),
        P(None, "fsdp"),
        P("fsdp", None),
        P(),
        P(),
        P(("rep", "fsdp"), None),
    )
    return jax.shard_map(
        functools.partial(on_device, mesh.shape["rep"], mesh.shape["fsdp"]),
        mesh=mesh,
        in_specs=placed,
        out_specs=(
            P(("rep", "fsdp"), None),
            P(("rep", "fsdp"), None),
            P("fsdp"),
            P(None, "fsdp"),
            P("fsdp"),
            P(None, "fsdp"),
            P("fsdp"),
            P(None, "fsdp"),
            P(None, "fsdp"),
            P("fsdp", None),
            P(),
            P(),
        ),
        check_vma=False,
    )
```

```python
import functools
import jax
import jax.numpy as jnp
from jax import lax
from jax.experimental import pallas as pl
from jax.experimental.pallas import tpu as pltpu
from jax.sharding import PartitionSpec as P

D = 1536
H = 16
HD = 96
CQ = 6
CK = 11
NEG = -1e30
PAIRS = H // 2
PW = 2 * HD
BF = jnp.bfloat16
F32 = jnp.float32


def cost(time):
    return pl.CostEstimate(flops=int(time * 5e8), bytes_accessed=0, transcendentals=0)


def dot(a, b, ca, cb):
    return lax.dot_general(a, b, (((ca,), (cb,)), ((), ())), preferred_element_type=F32)


def split(v):
    hi = v.astype(BF)
    return hi, (v - hi.astype(F32)).astype(BF)


def taps_kernel(fwd_ref, bwd_ref, th_ref, tl_ref, tt_ref):
    n = th_ref.shape[-1]
    row = lax.broadcasted_iota(jnp.int32, (n, n), 0)
    col = lax.broadcasted_iota(jnp.int32, (n, n), 1)
    near = jnp.abs(row - col) <= CK // 2
    for a in range(CQ):
        wide = jnp.broadcast_to(fwd_ref[0, a : a + 1, :], (n, n))
        band = jnp.where(near, pltpu.roll(wide, 0, 1, stride=1, stride_axis=0), 0.0)
        hi, lo = split(band)
        th_ref[0, a * n : (a + 1) * n, :] = hi
        tl_ref[0, a * n : (a + 1) * n, :] = lo
        wide = jnp.broadcast_to(bwd_ref[0, a : a + 1, :], (n, n))
        band = jnp.where(near, pltpu.roll(wide, 0, 1, stride=1, stride_axis=0), 0.0)
        tt_ref[0, a * n : (a + 1) * n, :] = band.astype(BF)


def band_taps(kernel, n):
    half = CK // 2

    def around(taps):
        gap = jnp.zeros((H, CQ, n - CK), F32)
        rows = jnp.concatenate([taps[:, :, half:], gap, taps[:, :, :half]], axis=2)
        return jnp.pad(rows, ((0, 0), (0, 8 - CQ), (0, 0)))

    taps = kernel.reshape(H, CQ, CK)
    fwd, bwd = around(taps), around(taps[:, :, ::-1])
    row = pl.BlockSpec((1, 8, n), lambda h: (h, 0, 0))
    out = pl.BlockSpec((1, CQ * n, n), lambda h: (h, 0, 0))
    shape = jax.ShapeDtypeStruct((H, CQ * n, n), BF)
    return pl.pallas_call(
        taps_kernel,
        cost_estimate=cost(16),
        grid=(H,),
        in_specs=[row, row],
        out_specs=[out, out, out],
        out_shape=[shape, shape, shape],
    )(fwd, bwd)


def fence_kernel(*refs):
    del refs


def fence(*values, time=0.1):
    return pl.pallas_call(
        fence_kernel,
        cost_estimate=cost(time),
        in_specs=[pl.BlockSpec(memory_space=pl.ANY)] * len(values),
        out_specs=[pl.BlockSpec(memory_space=pl.ANY)] * len(values),
        out_shape=[jax.ShapeDtypeStruct(v.shape, v.dtype) for v in values],
        input_output_aliases={i: i for i in range(len(values))},
    )(*values)


def project_kernel(x_ref, gain_ref, w_ref, normed_ref, *part_refs):
    cols = part_refs[0].shape[0] // w_ref.shape[0]
    x = x_ref[...].astype(F32)
    normed = rms_norm(x, gain_ref[...]).astype(BF)
    normed_ref[...] = normed
    w = w_ref[:, :cols, :].reshape(-1, D)
    part = dot(w, normed, 1, 1).astype(BF)
    for b, ref in enumerate(part_refs):

        @pl.when(pl.program_id(0) == b)
        def _():
            ref[...] = part


def project(blocks, gain, w_attn, cols, n):
    lines, count = w_attn.shape[0], blocks.shape[0] // n
    rows = lines * cols
    if cols % 16:
        normed = rms_norm(blocks.astype(F32), gain).astype(BF)
        part = dot(w_attn[:, :cols].reshape(rows, D), normed, 1, 1).astype(BF)
        return normed, [part[:, b * n : (b + 1) * n] for b in range(count)]
    out = pl.pallas_call(
        project_kernel,
        cost_estimate=cost(1.2 * count),
        grid=(count,),
        in_specs=[
            pl.BlockSpec((n, D), lambda b: (b, 0)),
            pl.BlockSpec((1, D), lambda b: (0, 0)),
            pl.BlockSpec(w_attn.shape, lambda b: (0, 0, 0)),
        ],
        out_specs=[pl.BlockSpec((n, D), lambda b: (b, 0))]
        + [pl.BlockSpec((rows, n), lambda b: (0, 0))] * count,
        out_shape=[jax.ShapeDtypeStruct(blocks.shape, BF)]
        + [jax.ShapeDtypeStruct((rows, n), BF)] * count,
        compiler_params=pltpu.CompilerParams(vmem_limit_bytes=60 * 2**20),
    )(blocks, gain.reshape(1, D), w_attn)
    return out[0], out[1:]


def move_kernel(joins, count, cols, place_ref, *refs):
    *arrays, sems = refs
    if joins:
        *blocks, held = arrays
    else:
        whole, *blocks, held, sem = arrays
        first = pltpu.make_async_copy(whole, held, sem)
        first.start()
        first.wait()
    lines = held.shape[0]
    rows = lines * cols
    copies = []
    for b in range(8):
        other = place_ref[0] ^ order(b)
        for z in range(lines):
            part = blocks[b // count].at[pl.ds(b % count * rows + z * cols, cols)]
            spot = held.at[z, other & 3, other >> 2]
            pair = (part, spot) if joins else (spot, part)
            copies.append(pltpu.make_async_copy(*pair, sems.at[len(copies)]))
            copies[-1].start()
    for copy in copies:
        copy.wait()


def move(joins, values, place, lines, cols, n, count):
    anywhere = pl.BlockSpec(memory_space=pl.ANY)
    whole = (lines, 4, 2, cols, n)
    held = [pltpu.VMEM(whole, BF), pltpu.SemaphoreType.DMA(())]
    if joins:
        out_specs = pl.BlockSpec(memory_space=pltpu.VMEM)
        shape = jax.ShapeDtypeStruct(whole, BF)
    else:
        out_specs = [anywhere] * (8 // count)
        shape = [jax.ShapeDtypeStruct((lines * cols * count, n), BF)] * (8 // count)
    return pl.pallas_call(
        functools.partial(move_kernel, joins, count, cols),
        cost_estimate=cost(2),
        in_specs=[pl.BlockSpec(memory_space=pltpu.SMEM)] + [anywhere] * len(values),
        out_specs=out_specs,
        out_shape=shape,
        scratch_shapes=([] if joins else held) + [pltpu.SemaphoreType.DMA((8 * lines,))],
        compiler_params=pltpu.CompilerParams(vmem_limit_bytes=60 * 2**20),
    )(place.reshape(1), *values)


def out_grad_kernel(place_ref, branch_ref, grouped_ref, *refs):
    outs, held = refs[:-1], refs[-1]
    lines = outs[0].shape[0] // (held.shape[0] // 8)
    wide, half = held.shape[0], held.shape[0] // 8
    for z in range(lines):
        held[...] = dot(branch_ref[:, z * wide : (z + 1) * wide], grouped_ref[...], 0, 1)
        for b, ref in enumerate(outs):
            other = place_ref[0] ^ order(b)
            start = pl.multiple_of((other & 3) * 2 * half + (other >> 2) * half, half)
            ref[z * half : (z + 1) * half, :] = held[pl.ds(start, half), :].astype(ref.dtype)


def out_weight_grad(branch, grouped, place, lines, half):
    n = branch.shape[0]
    if half % 16:
        full = dot(branch, grouped, 0, 1).reshape(lines, 4, 2, half, D)
        blocks = []
        for b in range(8):
            other = place ^ order(b)
            block = lax.dynamic_slice(full, (0, other & 3, other >> 2, 0, 0), (lines, 1, 1, half, D))
            blocks.append(block.reshape(lines * half, D).astype(F32 if b < 4 else BF))
        return blocks
    vmem = pl.BlockSpec(memory_space=pltpu.VMEM)
    return pl.pallas_call(
        out_grad_kernel,
        cost_estimate=cost(0),
        grid=(1,),
        in_specs=[
            pl.BlockSpec(memory_space=pltpu.SMEM),
            pl.BlockSpec((n, D), lambda t: (0, 0)),
            pl.BlockSpec((D, n), lambda t: (0, 0)),
        ],
        out_specs=[pl.BlockSpec((lines * half, D), lambda t: (0, 0))] * 8,
        out_shape=[
            jax.ShapeDtypeStruct((lines * half, D), F32 if b < 4 else BF) for b in range(8)
        ],
        scratch_shapes=[pltpu.VMEM((8 * half, D), F32)],
        compiler_params=pltpu.CompilerParams(vmem_limit_bytes=60 * 2**20),
    )(place.reshape(1), branch, grouped)


def join(values, place, lines, cols):
    count, n = 8 // len(values), values[0].shape[1]
    if cols % 16 == 0:
        return move(True, values, place, lines, cols, n, count).reshape(-1, n)
    out = jnp.zeros((lines, 4, 2, cols, n), BF)
    for b in range(8):
        source = place ^ order(b)
        block = values[b // count].reshape(count, lines, 1, 1, cols, n)[b % count]
        out = lax.dynamic_update_slice(out, block, (0, source & 3, source >> 2, 0, 0))
    return out.reshape(-1, n)


def cut(value, place, lines, cols):
    n = value.shape[1]
    value = value.reshape(lines, 4, 2, cols, n)
    if cols % 16 == 0:
        return move(False, [value], place, lines, cols, n, 1)
    pieces = []
    for b in range(8):
        target = place ^ order(b)
        piece = lax.dynamic_slice(value, (0, target & 3, target >> 2, 0, 0), (lines, 1, 1, cols, n))
        pieces.append(piece.reshape(lines * cols, n))
    return pieces


def order(b):
    return (b // 2 % 2) * 4 + (b % 2) * 2 + b // 4


def gated(gate, upper, d_hidden):
    sig = 1.0 / (1.0 + jnp.exp(-gate))
    act = gate * sig
    hidden = (act * upper).astype(BF)
    d_gate = (d_hidden * upper * (sig * (1.0 + gate * (1.0 - sig)))).astype(BF)
    return hidden, d_gate, (d_hidden * act).astype(BF)


def ffn_kernel(s_ref, o_ref, w_ref, hid_ref, dgu_ref, ds_ref, yo_ref):
    lines, wide = w_ref.shape[0], w_ref.shape[1] // 3
    w_gu = w_ref[:, : 2 * wide, :].reshape(-1, D)
    w_down = w_ref[:, 2 * wide :, :].reshape(-1, D)
    gu = dot(s_ref[...], w_gu, 1, 1)
    dh = dot(o_ref[...], w_down, 1, 1)
    for z in range(lines):
        lo, mid, hi = 2 * z * wide, (2 * z + 1) * wide, (2 * z + 2) * wide
        cut_h = slice(z * wide, (z + 1) * wide)
        hidden, d_gate, d_up = gated(gu[:, lo:mid], gu[:, mid:hi], dh[:, cut_h])
        hid_ref[:, cut_h] = hidden
        dgu_ref[:, lo:mid] = d_gate
        dgu_ref[:, mid:hi] = d_up
    ds_ref[...] = dot(dgu_ref[...], w_gu, 1, 0).astype(ds_ref.dtype)
    yo_ref[...] = dot(hid_ref[...], w_down, 1, 0).astype(yo_ref.dtype)


def ffn(second, d_ffn, w_ffn, n, dtype, start, count):
    rows, lines, wide = count * n, w_ffn.shape[0], w_ffn.shape[1] // 3
    if wide % 128:
        second, d_ffn = (v[start * n : start * n + rows] for v in (second, d_ffn))
        w_gu = w_ffn[:, : 2 * wide].reshape(-1, D)
        w_down = w_ffn[:, 2 * wide :].reshape(-1, D)
        gu = dot(second, w_gu, 1, 1).reshape(rows, lines, 2, wide)
        dh = dot(d_ffn, w_down, 1, 1).reshape(rows, lines, wide)
        hidden, d_gate, d_up = gated(gu[:, :, 0], gu[:, :, 1], dh)
        hidden = hidden.reshape(rows, lines * wide)
        d_gu = jnp.stack([d_gate, d_up], axis=2).reshape(rows, 2 * lines * wide)
        return hidden, d_gu, dot(d_gu, w_gu, 1, 0).astype(dtype), dot(hidden, w_down, 1, 0).astype(dtype)
    out = lambda width: pl.BlockSpec((n, width), lambda b: (b, 0))
    block = pl.BlockSpec((n, D), lambda b: (b + start, 0))
    return pl.pallas_call(
        ffn_kernel,
        cost_estimate=cost(3.8 * count),
        grid=(count,),
        in_specs=[block, block, pl.BlockSpec(w_ffn.shape, lambda b: (0, 0, 0))],
        out_specs=[out(lines * wide), out(2 * lines * wide), out(D), out(D)],
        out_shape=[
            jax.ShapeDtypeStruct((rows, lines * wide), BF),
            jax.ShapeDtypeStruct((rows, 2 * lines * wide), BF),
            jax.ShapeDtypeStruct((rows, D), dtype),
            jax.ShapeDtypeStruct((rows, D), dtype),
        ],
        compiler_params=pltpu.CompilerParams(vmem_limit_bytes=60 * 2**20),
    )(second, d_ffn, w_ffn)


def ffn_grad_kernel(counts, *refs):
    runs = len(counts)
    hid, dgu, sec, dff = (refs[i * runs : (i + 1) * runs] for i in range(4))
    out_ref, gu_ref, down_ref = refs[4 * runs :]
    t = pl.program_id(0)
    start = 0
    for r in range(runs):

        @pl.when((t >= start) & (t < start + counts[r]))
        def _():
            gu = dot(dgu[r][...], sec[r][...], 0, 0)
            down = dot(hid[r][...], dff[r][...], 0, 0)
            if r == 0:
                gu_ref[...] = jnp.where(t == 0, gu, gu_ref[...] + gu)
                down_ref[...] = jnp.where(t == 0, down, down_ref[...] + down)
            else:
                gu_ref[...] += gu
                down_ref[...] += down

        start += counts[r]

    @pl.when(t == start - 1)
    def _():
        lines, wide = out_ref.shape[0], out_ref.shape[1] // 3
        for z in range(lines):
            out_ref[z, : 2 * wide, :] = gu_ref[2 * z * wide : 2 * (z + 1) * wide, :].astype(BF)
            out_ref[z, 2 * wide :, :] = down_ref[z * wide : (z + 1) * wide, :].astype(BF)


def ffn_grad(hidden, d_gu, second, d_ffn, lines, wide, n):
    counts = [h.shape[0] // n for h in hidden]
    if wide % 128:
        rows = lambda group: [v[f * n : (f + c) * n] for (v, f), c in zip(group, counts)]
        gu = sum(dot(a, b, 0, 0) for a, b in zip(d_gu, rows(second))).reshape(lines, 2 * wide, D)
        down = sum(dot(a, b, 0, 0) for a, b in zip(hidden, rows(d_ffn))).reshape(lines, wide, D)
        return jnp.concatenate([gu, down], axis=1).astype(BF)
    hidden, d_gu = ([(v, 0) for v in group] for group in (hidden, d_gu))
    specs, starts = [], [sum(counts[:r]) for r in range(len(counts))]
    for group in (hidden, d_gu, second, d_ffn):
        for (value, first), start, count in zip(group, starts, counts):
            specs.append(
                pl.BlockSpec(
                    (n, value.shape[1]),
                    lambda t, s=start, c=count, f=first: (jnp.clip(t - s, 0, c - 1) + f, 0),
                )
            )
    out = (lines, 3 * wide, D)
    return pl.pallas_call(
        functools.partial(ffn_grad_kernel, counts),
        cost_estimate=cost(18),
        grid=(sum(counts),),
        in_specs=specs,
        out_specs=pl.BlockSpec(out, lambda t: (0, 0, 0)),
        out_shape=jax.ShapeDtypeStruct(out, BF),
        scratch_shapes=[pltpu.VMEM((2 * lines * wide, D), F32), pltpu.VMEM((lines * wide, D), F32)],
        compiler_params=pltpu.CompilerParams(vmem_limit_bytes=60 * 2**20),
    )(*(v for group in (hidden, d_gu, second, d_ffn) for v, _ in group))


def back_project_kernel(count, *refs):
    parts, (x_ref, normed_ref, w_ref) = refs[:count], refs[count : count + 3]
    before, (dn_ref, out_ref, gain_ref, g_ref) = refs[count + 3 : -4], refs[-4:]
    rows = g_ref.shape[0]
    w = w_ref[:, : rows // w_ref.shape[0], :].reshape(rows, D)
    t = pl.program_id(0)

    @pl.when(t == 0)
    def _():
        if before:
            g_ref[...] = before[0][...]
            gain_ref[...] = before[1][...]
        else:
            g_ref[...] = jnp.zeros_like(g_ref)
            gain_ref[...] = jnp.zeros_like(gain_ref)

    for b in range(count):

        @pl.when(t == b)
        def _():
            grad = parts[b][...]
            g_ref[...] += dot(grad, normed_ref[...], 1, 0)
            dn = dot(grad, w, 0, 0)
            dn_ref[...] = dn.astype(dn_ref.dtype)
            x = x_ref[...].astype(F32)
            hat = x * lax.rsqrt(jnp.mean(x * x, axis=1, keepdims=True) + 1e-05)
            gain_ref[...] += jnp.sum(dn * hat, axis=0, keepdims=True)

    @pl.when(t == count - 1)
    def _():
        out_ref[...] = g_ref[...].astype(out_ref.dtype)


def back_project(parts, x, normed, w_attn, cols, n, dtype, before=()):
    lines, count = w_attn.shape[0], len(parts)
    rows = lines * cols
    if cols % 16:
        grad = jnp.concatenate(parts, axis=1)
        dn = dot(grad, w_attn[:, :cols].reshape(rows, D), 0, 0)
        values = x.astype(F32)
        hat = values * lax.rsqrt(jnp.mean(values * values, axis=1, keepdims=True) + 1e-05)
        sums = (dot(grad, normed, 1, 0), jnp.sum(dn * hat, axis=0, keepdims=True))
        if before:
            sums = (sums[0] + before[0], sums[1] + before[1])
        return (dn.astype(dtype),) + sums
    block = pl.BlockSpec((n, D), lambda b: (b, 0))
    whole = lambda shape: pl.BlockSpec(shape, lambda b: (0,) * len(shape))
    return pl.pallas_call(
        functools.partial(back_project_kernel, count),
        cost_estimate=cost(2.5 * count),
        grid=(count,),
        in_specs=[whole((rows, n))] * count
        + [block, block, whole(w_attn.shape)]
        + [whole(v.shape) for v in before],
        out_specs=[block, whole((rows, D)), whole((1, D))],
        out_shape=[
            jax.ShapeDtypeStruct((count * n, D), dtype),
            jax.ShapeDtypeStruct((rows, D), BF if before else F32),
            jax.ShapeDtypeStruct((1, D), F32),
        ],
        scratch_shapes=[pltpu.VMEM((rows, D), F32)],
        compiler_params=pltpu.CompilerParams(vmem_limit_bytes=60 * 2**20),
    )(*parts, x, normed, w_attn, *before)


def doc_masks(drow_ref, dcol_ref, allow_ref, same_ref):
    n = allow_ref.shape[0]
    row = lax.broadcasted_iota(jnp.int32, (n, n), 0)
    col = lax.broadcasted_iota(jnp.int32, (n, n), 1)
    same = dcol_ref[...] == drow_ref[...]
    same_ref[...] = jnp.where(same, 1.0, 0.0)
    allow_ref[...] = jnp.where(same & (col <= row), 1.0, 0.0)


def attend_kernel(
    mix_ref, q_ref, k_ref, v_ref, th_ref, tl_ref, drow_ref, dcol_ref, gain_ref, *refs
):
    prob_ref, att_ref, grp_ref, allow_ref, same_ref, pad_ref, xh_ref, xl_ref = refs[-8:]
    g = pl.program_id(0)
    n = q_ref.shape[1]

    @pl.when(g == 0)
    def _():
        doc_masks(drow_ref, dcol_ref, allow_ref, same_ref)
        pad_ref[0:8, :] = jnp.zeros((8, n), F32)

    for e in range(2):
        q = q_ref[e * HD : (e + 1) * HD, :]
        k = k_ref[e * HD : (e + 1) * HD, :]
        logits = dot(q, k, 0, 0) * (HD ** (-0.5))
        pad_ref[8 : 8 + n, :] = jnp.where(allow_ref[...] > 0, logits, 0.0)
        for a in range(CQ):
            part = jnp.where(same_ref[...] > 0, pad_ref[8 - a : 8 - a + n, :], 0.0)
            hi, lo = split(part)
            xh_ref[:, a * n : (a + 1) * n] = hi
            xl_ref[:, a * n : (a + 1) * n] = lo
        conv = (
            dot(xh_ref[...], th_ref[e], 1, 0)
            + dot(xh_ref[...], tl_ref[e], 1, 0)
            + dot(xl_ref[...], th_ref[e], 1, 0)
        )
        scores = jnp.where(allow_ref[...] > 0, conv, NEG)
        weights = jnp.exp(scores - jnp.max(scores, axis=1, keepdims=True))
        prob_ref[e] = weights * (1.0 / jnp.sum(weights, axis=1, keepdims=True))
    for c in range(2):
        mixed = (mix_ref[g, 2 * c] * prob_ref[0] + mix_ref[g, 2 * c + 1] * prob_ref[1]).astype(BF)
        att = dot(v_ref[c * HD : (c + 1) * HD, :], mixed, 1, 1)
        att_ref[c * HD : (c + 1) * HD, :] = att
        centre = att - jnp.mean(att, axis=0, keepdims=True)
        spread = jnp.mean(centre * centre, axis=0, keepdims=True)
        grp_ref[c * HD : (c + 1) * HD, :] = (
            centre * lax.rsqrt(spread + 1e-05) * gain_ref[c * HD : (c + 1) * HD, :]
        ).astype(BF)


def attend(packed_t, docs, th, tl, mix, gain, start, count, before=()):
    n = packed_t.shape[1]
    blk = lambda off: pl.BlockSpec((PW, n), lambda g: (g + off, 0))
    tap = pl.BlockSpec((2, CQ * n, n), lambda g: (g + start, 0, 0))
    whole = lambda s: pl.BlockSpec(s, lambda g: (0, 0))
    return pl.pallas_call(
        attend_kernel,
        cost_estimate=cost(2.7 * count),
        grid=(count,),
        in_specs=[
            pl.BlockSpec(memory_space=pltpu.SMEM),
            blk(start), blk(PAIRS + start), blk(2 * PAIRS + start), tap, tap,
            whole((1, n)), whole((n, 1)),
            pl.BlockSpec((PW, 1), lambda g: (g + start, 0)),
        ]
        + [pl.BlockSpec(memory_space=pl.ANY)] * len(before),
        out_specs=[pl.BlockSpec((2, n, n), lambda g: (g, 0, 0)), blk(0), blk(start)],
        out_shape=[
            jax.ShapeDtypeStruct((2 * count, n, n), F32),
            jax.ShapeDtypeStruct((count * PW, n), F32),
            jax.ShapeDtypeStruct((D, n), BF),
        ],
        input_output_aliases={9: 2} if before else {},
        scratch_shapes=[
            pltpu.VMEM((n, n), F32), pltpu.VMEM((n, n), F32), pltpu.VMEM((n + 8, n), F32),
            pltpu.VMEM((n, CQ * n), BF), pltpu.VMEM((n, CQ * n), BF),
        ],
        compiler_params=pltpu.CompilerParams(vmem_limit_bytes=60 * 2**20),
    )(
        mix[start : start + count].reshape(count, 4), packed_t, packed_t, packed_t, th, tl,
        docs.reshape(1, n), docs.reshape(n, 1), gain, *before,
    )


def attend_back_kernel(
    mix_ref, q_ref, k_ref, v_ref, tt_ref, drow_ref, dcol_ref, gain_ref, prob_ref, att_ref, dgrp_ref, *refs
):
    d_ref, dgain_ref, dtap_ref, dmix_ref, allow_ref, same_ref, pad_ref, y_ref, dm_ref = refs[-9:]
    g = pl.program_id(0)
    n = q_ref.shape[1]
    scale = HD ** (-0.5)

    @pl.when(g == 0)
    def _():
        doc_masks(drow_ref, dcol_ref, allow_ref, same_ref)
        pad_ref[n : n + 8, :] = jnp.zeros((8, n), F32)

    for c in range(2):
        rows = slice(c * HD, (c + 1) * HD)
        att = att_ref[rows, :]
        centre = att - jnp.mean(att, axis=0, keepdims=True)
        rstd = lax.rsqrt(jnp.mean(centre * centre, axis=0, keepdims=True) + 1e-05)
        hat = centre * rstd
        dgrp = dgrp_ref[rows, :]
        dgain_ref[rows, :] = jnp.sum(dgrp * hat, axis=1, keepdims=True)
        dhat = dgrp * gain_ref[rows, :]
        datt = rstd * (
            dhat
            - jnp.mean(dhat, axis=0, keepdims=True)
            - hat * jnp.mean(dhat * hat, axis=0, keepdims=True)
        )
        datt = datt.astype(BF)
        mixed = (mix_ref[g, 2 * c] * prob_ref[0] + mix_ref[g, 2 * c + 1] * prob_ref[1]).astype(BF)
        d_ref[2, rows, :] = dot(datt, mixed, 1, 0).astype(BF)
        dmixed = dot(datt, v_ref[rows, :], 0, 0)
        dm_ref[c] = dmixed
        for e in range(2):
            dmix_ref[0, 2 * c + e : 2 * c + e + 1, :] = jnp.sum(dmixed * prob_ref[e], axis=0, keepdims=True)
    dmix_ref[0, 4:8, :] = jnp.zeros((4, n), F32)
    row = lax.broadcasted_iota(jnp.int32, (128, 128), 0)
    col = lax.broadcasted_iota(jnp.int32, (128, 128), 1)
    off = col - row
    half = CK // 2
    for e in range(2):
        rows = slice(e * HD, (e + 1) * HD)
        q = q_ref[rows, :]
        k = k_ref[rows, :]
        allowed = allow_ref[...] > 0
        masked_t = dot(k, q, 0, 0) * scale
        prob = prob_ref[e]
        dprob = mix_ref[g, e] * dm_ref[0] + mix_ref[g, 2 + e] * dm_ref[1]
        pad_ref[0:n, :] = prob * (dprob - jnp.sum(prob * dprob, axis=1, keepdims=True))
        for a in range(CQ):
            y_ref[:, a * n : (a + 1) * n] = jnp.where(same_ref[...] > 0, pad_ref[a : a + n, :], 0.0).astype(BF)
        dlog = jnp.where(allowed, dot(y_ref[...], tt_ref[e], 1, 0), 0.0).astype(BF)
        d_ref[0, rows, :] = (dot(k, dlog, 1, 1) * scale).astype(BF)
        d_ref[1, rows, :] = (dot(q, dlog, 1, 0) * scale).astype(BF)
        krow = lax.broadcasted_iota(jnp.int32, (n, n), 0)
        qcol = lax.broadcasted_iota(jnp.int32, (n, n), 1)
        masked_t = jnp.where((same_ref[...] > 0) & (krow <= qcol), masked_t, 0.0).astype(BF)
        for a in range(CQ):
            full = dot(masked_t, y_ref[:, a * n : (a + 1) * n], 1, 0)
            fold = jnp.zeros((128, 128), F32)
            blocks = n // 128
            for r in range(blocks):
                fold = fold + full[r * 128 : (r + 1) * 128, r * 128 : (r + 1) * 128]
            fold = jnp.where(jnp.abs(off) <= half, fold, 0.0)
            for r in range(blocks - 1):
                up = full[r * 128 : (r + 1) * 128, (r + 1) * 128 : (r + 2) * 128]
                down = full[(r + 1) * 128 : (r + 2) * 128, r * 128 : (r + 1) * 128]
                fold = fold + jnp.where(off <= half - 128, up, 0.0) + jnp.where(off >= 128 - half, down, 0.0)
            lined = fold[0:8, :]
            for t in range(1, 16):
                lined = lined + pltpu.roll(fold[8 * t : 8 * t + 8, :], 128 - 8 * t, 1)
            dtap_ref[e, 8 * a : 8 * a + 8, :] = lined


def attend_back(packed_t, docs, tt, mix, gain, prob, att, dgrp, start, count, before=()):
    n = packed_t.shape[1]
    blk = lambda off: pl.BlockSpec((PW, n), lambda g: (g + off, 0))
    whole = lambda s: pl.BlockSpec(s, lambda g: (0, 0))
    thin = lambda off: pl.BlockSpec((PW, 1), lambda g: (g + off, 0))
    rows = count * PW
    d_packed, dgain, dtap, dmix = pl.pallas_call(
        attend_back_kernel,
        cost_estimate=cost(2.7 * count),
        grid=(count,),
        in_specs=[
            pl.BlockSpec(memory_space=pltpu.SMEM),
            blk(start), blk(PAIRS + start), blk(2 * PAIRS + start),
            pl.BlockSpec((2, CQ * n, n), lambda g: (g + start, 0, 0)),
            whole((1, n)), whole((n, 1)), thin(start),
            pl.BlockSpec((2, n, n), lambda g: (g, 0, 0)),
            blk(0), blk(start),
        ]
        + [pl.BlockSpec(memory_space=pl.ANY)] * len(before),
        out_specs=[
            pl.BlockSpec((3, PW, n), lambda g: (0, g + start, 0)), thin(0),
            pl.BlockSpec((2, 8 * CQ, 128), lambda g: (g, 0, 0)),
            pl.BlockSpec((1, 8, n), lambda g: (g, 0, 0)),
        ],
        out_shape=[
            jax.ShapeDtypeStruct((3, D, n), BF),
            jax.ShapeDtypeStruct((rows, 1), F32),
            jax.ShapeDtypeStruct((2 * count, 8 * CQ, 128), F32),
            jax.ShapeDtypeStruct((count, 8, n), F32),
        ],
        scratch_shapes=[
            pltpu.VMEM((n, n), F32), pltpu.VMEM((n, n), F32), pltpu.VMEM((n + 8, n), F32),
            pltpu.VMEM((n, CQ * n), BF), pltpu.VMEM((2, n, n), F32),
        ],
        input_output_aliases={11: 0} if before else {},
        compiler_params=pltpu.CompilerParams(vmem_limit_bytes=60 * 2**20),
    )(
        mix[start : start + count].reshape(count, 4), packed_t, packed_t, packed_t, tt,
        docs.reshape(1, n), docs.reshape(n, 1), gain, prob, att, dgrp, *before,
    )
    lane = jnp.arange(128)[None, None, :] - jnp.arange(8)[None, :, None]
    tap = jnp.arange(CK)[:, None, None] - CK // 2
    pick = (jnp.remainder(lane - tap, 128) == 0).astype(F32)
    dtap = jnp.sum(dtap.reshape(2 * count, CQ, 1, 8, 128) * pick, axis=(3, 4))
    dmix = jnp.sum(dmix[:, :4, :], axis=2)
    return d_packed, dgain, dtap.reshape(2 * count, CQ * CK), dmix.reshape(count, 2, 2)


def rms_norm(values, gain):
    return values * lax.rsqrt(jnp.mean(values * values, axis=-1, keepdims=True) + 1e-05) * gain


def rms_back(values, gain, grad):
    rstd = lax.rsqrt(jnp.mean(values * values, axis=-1, keepdims=True) + 1e-05)
    hat = values * rstd
    dhat = grad * gain
    dvalues = rstd * (dhat - hat * jnp.mean(dhat * hat, axis=-1, keepdims=True))
    return dvalues, jnp.sum(grad * hat, axis=0)


class Slice:
    def __init__(self, reps, shards):
        self.axes = ("rep", "fsdp")
        self.shards = shards
        self.lines = [[4 * o + i for o in range(shards // 4)] for i in range(4)]
        places = [(y, f) for y in range(reps) for f in range(shards)]

        def perm(move):
            out = []
            for y, f in places:
                to = move(y, f)
                out.append((y * shards + f, to[0] * shards + to[1]))
            return out

        self.hops = {
            (dy, di): perm(lambda y, f, dy=dy, di=di: (y ^ dy, f ^ di))
            for dy in range(2)
            for di in (range(16) if shards == 16 else range(4))
        }
        self.corner = perm(lambda y, f: (y, f ^ 2) if f & 1 else (1 - y, f))
        self.doubling = []
        bit = 1
        while bit < shards:
            self.doubling.append((bit, perm(lambda y, f, bit=bit: (y, f ^ bit))))
            bit *= 2
        self.rep = lax.axis_index("rep")
        self.fsdp = lax.axis_index("fsdp")
        self.odd = (self.fsdp & 1) == 1
        self.place = self.rep * 4 + (self.fsdp & 3)

    def hop(self, value, dy, di):
        return lax.ppermute(value, self.axes, self.hops[dy, di])

    def hop_block(self, value, b):
        return self.hop(value, order(b) >> 2, order(b) & 3) if b else value

    def gather_line(self, value):
        return lax.all_gather(value, "fsdp", axis=0, tiled=True, axis_index_groups=self.lines)

    def scatter_line(self, value):
        return lax.psum_scatter(
            value.astype(BF), "fsdp", scatter_dimension=0, tiled=True, axis_index_groups=self.lines
        )

    def gather_small(self, value):
        for bit, perm in self.doubling:
            other = lax.ppermute(value, self.axes, perm)
            high = (self.fsdp & bit) != 0
            value = jnp.concatenate(
                [jnp.where(high, other, value), jnp.where(high, value, other)], axis=0
            )
        return value

    def sides(self, value):
        return self.hop(value, 0, 2), self.hop(value, 1, 0)

    def far_corner(self, along_x, along_y):
        return lax.ppermute(jnp.where(self.odd, along_y, along_x), self.axes, self.corner)

    def near_blocks(self, value, along_x, along_y, corner):
        near = jnp.concatenate([value, along_x, along_y, jnp.zeros_like(value)], axis=0)
        return lax.dynamic_update_slice(near, corner, (3 * value.shape[0], 0))

    def scatter_corner(self, near, far):
        own, to_x, to_y, last = (a + b.astype(F32) for a, b in zip(near, far))
        corner = lax.ppermute(last.astype(BF), self.axes, self.corner).astype(F32)
        to_x = (to_x + jnp.where(self.odd, 0.0, corner)).astype(BF)
        to_y = (to_y + jnp.where(self.odd, corner, 0.0)).astype(BF)
        return own, to_x, to_y

    def scatter_last(self, own, to_x, to_y):
        return own + self.hop(to_x, 0, 2).astype(F32) + self.hop(to_y, 1, 0).astype(F32)

    def scatter_line_small(self, value):
        lines = self.shards // 4
        if lines != 4:
            return self.scatter_line(value).astype(F32)
        rows = value.shape[0] // lines
        value = value.astype(BF)
        line = self.fsdp // 4
        part = lambda d: lax.dynamic_slice_in_dim(value, (line ^ d) * rows, rows, axis=0)
        return sum([self.hop(part(d), 0, 4 * d).astype(F32) for d in range(1, 4)], part(0).astype(F32))

    def sum_small(self, value):
        value = value + self.hop(value, 1, 0)
        for _, perm in self.doubling:
            value = value + lax.ppermute(value, self.axes, perm)
        return value

    def both_halves(self, half, axis=0, other=None):
        if other is None:
            other = self.hop(half, 1, 0)
        first = self.rep == 0
        return jnp.concatenate(
            [jnp.where(first, half, other), jnp.where(first, other, half)], axis=axis
        ).astype(F32)

    def own_half(self, shard):
        rows = shard.shape[0] // 2
        return lax.dynamic_slice_in_dim(shard, self.rep * rows, rows, axis=0)


def on_device(
    reps,
    shards,
    tokens,
    doc_ids,
    norm_gain,
    qkv_weight,
    group_gain,
    out_weight,
    ffn_gain,
    gate_weight,
    up_weight,
    down_weight,
    conv_kernel,
    head_mix,
    out_grad,
):
    net = Slice(reps, shards)
    lines = shards // 4
    n = tokens.shape[0]
    cols = 3 * D // shards // 2
    wide = gate_weight.shape[1] // 2

    half_out = D // shards // 2
    rows_of = lambda v: [v[b * n : (b + 1) * n] for b in range(v.shape[0] // n)]

    attn_half = jnp.concatenate([net.own_half(qkv_weight.T), net.own_half(out_weight.T)], axis=0)
    attn_half, tokens = fence(attn_half, tokens)
    w_attn = net.gather_line(attn_half).reshape(lines, -1, D)
    x_side = net.sides(tokens)
    ffn_half = jnp.concatenate(
        [net.own_half(gate_weight.T), net.own_half(up_weight.T), net.own_half(down_weight)], axis=0
    )
    taps = band_taps(conv_kernel, n)
    gains = net.gather_small(jnp.stack([norm_gain, group_gain, ffn_gain])[None])
    *x_side, ffn_half, gains, d_low, taps_hi, taps_lo, taps_back = fence(
        *x_side, ffn_half, gains, out_grad.astype(BF), *taps
    )
    w_ffn = net.gather_line(ffn_half).reshape(lines, -1, D)
    gains = gains.transpose(1, 0, 2).reshape(3, D).astype(F32)
    corner = net.far_corner(*x_side)
    d_side = net.sides(d_low)
    w_attn = fence(w_attn, time=100)[0]
    corner, *d_side, w_attn = fence(corner, *d_side, w_attn)
    x_near = net.near_blocks(tokens, *x_side, corner)
    x_far = net.hop(x_near, 0, 1)
    d_near = net.near_blocks(d_low, *d_side, net.far_corner(*d_side))
    inputs = tokens.astype(F32)

    norm_near, parts = project(x_near, gains[0], w_attn, cols, n)
    norm_far, more = project(x_far, gains[0], w_attn, cols, n)
    pieces = [net.hop_block(p, b) for b, p in enumerate((*parts, *more))]
    *pieces, w_cls, d_near = fence(*pieces, w_attn[:, cols:].reshape(-1, D), d_near)
    d_far = net.hop(d_near, 0, 1)
    w_side = (*net.sides(w_cls), net.hop(w_cls, 1, 2))
    packed_t = join(pieces, net.place, lines, cols)
    group_col = gains[1].reshape(D, 1)
    heads = PAIRS // 2
    front = functools.partial(attend, packed_t, doc_ids, taps_hi, taps_lo, head_mix, group_col)
    *w_side, prob_a, att_a, grouped = fence(*w_side, *front(0, heads))
    w_near = (w_cls, *w_side)
    w_far = [net.hop(w, 0, 1) for w in w_near]
    *w_far, prob_b, att_b, grouped = fence(*w_far, *front(heads, PAIRS - heads, (grouped,)))
    w_out = join([*w_near, *w_far], net.place, lines, half_out)

    middle = inputs + dot(grouped, w_out, 0, 1)
    second = rms_norm(middle, gains[2]).astype(BF)
    s_side = net.sides(second)
    s_near = net.near_blocks(second, *s_side, net.far_corner(*s_side))
    s_far = net.hop(s_near, 0, 1)

    w_ffn = fence(w_ffn, time=100)[0]
    run_a = ffn(s_near, d_near, w_ffn, n, F32, 0, 2)
    *run_a, s_far = fence(*run_a, s_far)
    run_f = ffn(s_far, d_far, w_ffn, n, BF, 0, 4)
    run_b = ffn(s_near, d_near, w_ffn, n, F32, 2, 2)
    ds_far, yo_far = net.hop(run_f[2], 0, 1), net.hop(run_f[3], 0, 1)
    own, to_x, to_y = net.scatter_corner(rows_of(run_a[2]) + rows_of(run_b[2]), rows_of(ds_far))
    acts = [r[i] for i in range(2) for r in (run_a, run_f, run_b)]
    to_x, to_y, *acts = fence(to_x, to_y, *acts)
    d_second = net.scatter_last(own, to_x, to_y)
    g_ffn = ffn_grad(
        acts[:3], acts[3:], [(s_near, 0), (s_far, 0), (s_near, 2)], [(d_near, 0), (d_far, 0), (d_near, 2)],
        lines, wide, n,
    )
    d_second, yo_far, g_ffn = fence(d_second, yo_far, g_ffn)
    g_ffn = fence(net.scatter_line(g_ffn.reshape(-1, D)), time=60)[0]

    d_norm, g_ffn_gain = rms_back(middle, gains[2], d_second)
    d_middle = out_grad + d_norm
    branch = d_middle.astype(BF)
    d_grouped = dot(w_out, branch, 0, 1)
    back = functools.partial(attend_back, packed_t, doc_ids, taps_back, head_mix, group_col)
    own, to_x, to_y = net.scatter_corner(rows_of(run_a[3]) + rows_of(run_b[3]), rows_of(yo_far))
    first = back(prob_a, att_a, d_grouped, 0, heads)
    to_x, to_y, *first = fence(to_x, to_y, *first)
    layer_out = (middle + net.scatter_last(own, to_x, to_y)).astype(BF)
    d_packed, *last = back(prob_b, att_b, d_grouped, heads, PAIRS - heads, first[:1])
    g_group, g_taps, g_mix = (jnp.concatenate([a, b], axis=0) for a, b in zip(first[1:], last))
    pieces = cut(d_packed.reshape(3 * D, n), net.place, lines, cols)
    pieces = [net.hop_block(p, b) for b, p in enumerate(pieces)]
    g_blocks = out_weight_grad(branch, grouped, net.place, lines, half_out)
    g_far = [net.hop(g, 0, 1) for g in g_blocks[4:]]
    *pieces, g_ffn = fence(*pieces, g_ffn)
    own, to_x, to_y = net.scatter_corner(g_blocks[:4], g_far)
    g_other = net.hop(g_ffn, 1, 0)
    far = back_project(pieces[4:], x_far, norm_far, w_attn, cols, n, BF)
    to_x, to_y, *far = fence(to_x, to_y, *far)
    g_out = net.scatter_last(own, to_x, to_y)
    dn_far = net.hop(far[0], 0, 1)
    near = back_project(pieces[:4], x_near, norm_near, w_attn, cols, n, F32, far[1:])
    g_other, *near = fence(g_other, *near)
    g_qkv = fence(net.scatter_line(near[1]), time=30)[0]
    g_qkv = net.both_halves(g_qkv).T
    g_out = net.both_halves(net.scatter_line_small(g_out).astype(BF)).T
    shape = (3, wide, D)
    g_ffn = net.both_halves(g_ffn.reshape(shape), 1, g_other.reshape(shape))
    g_gate, g_up, g_down = g_ffn[0].T, g_ffn[1].T, g_ffn[2]
    own, to_x, to_y = net.scatter_corner(rows_of(near[0]), rows_of(dn_far))
    d_normed = net.scatter_last(own, to_x, to_y)
    d_in = rms_back(inputs, gains[0], d_normed)[0]
    input_grad = d_middle + d_in

    small = net.sum_small(
        jnp.concatenate([near[2][0], g_group[:, 0], g_ffn_gain, g_taps.reshape(-1), g_mix.reshape(-1)])
    )
    part = D // shards
    gain_grads = [
        lax.dynamic_slice_in_dim(small, b * D + net.fsdp * part, part) for b in range(3)
    ]
    g_taps = small[3 * D : 3 * D + H * CQ * CK].reshape(H, CQ * CK)
    g_mix = small[3 * D + H * CQ * CK :].reshape(PAIRS, 2, 2)
    return (
        layer_out,
        input_grad,
        gain_grads[0],
        g_qkv,
        gain_grads[1],
        g_out,
        gain_grads[2],
        g_gate,
        g_up,
        g_down,
        g_taps,
        g_mix,
    )


def solution(mesh):
    placed = (
        P(("rep", "fsdp"), None),
        P(("rep", "fsdp")),
        P("fsdp"),
        P(None, "fsdp"),
        P("fsdp"),
        P(None, "fsdp"),
        P("fsdp"),
        P(None, "fsdp"),
        P(None, "fsdp"),
        P("fsdp", None),
        P(),
        P(),
        P(("rep", "fsdp"), None),
    )
    return jax.shard_map(
        functools.partial(on_device, mesh.shape["rep"], mesh.shape["fsdp"]),
        mesh=mesh,
        in_specs=placed,
        out_specs=(
            P(("rep", "fsdp"), None),
            P(("rep", "fsdp"), None),
            P("fsdp"),
            P(None, "fsdp"),
            P("fsdp"),
            P(None, "fsdp"),
            P("fsdp"),
            P(None, "fsdp"),
            P(None, "fsdp"),
            P("fsdp", None),
            P(),
            P(),
        ),
        check_vma=False,
    )
```

```python
import functools
import jax
import jax.numpy as jnp
from jax import lax
from jax.experimental import pallas as pl
from jax.experimental.pallas import tpu as pltpu
from jax.sharding import PartitionSpec as P

D = 1536
H = 16
HD = 96
CQ = 6
CK = 11
NEG = -1e30
PAIRS = H // 2
PW = 2 * HD
BF = jnp.bfloat16
F32 = jnp.float32


def cost(time):
    return pl.CostEstimate(flops=int(time * 5e8), bytes_accessed=0, transcendentals=0)


def dot(a, b, ca, cb):
    return lax.dot_general(a, b, (((ca,), (cb,)), ((), ())), preferred_element_type=F32)


def split(v):
    hi = v.astype(BF)
    return hi, (v - hi.astype(F32)).astype(BF)


def taps_kernel(fwd_ref, bwd_ref, th_ref, tl_ref, tt_ref):
    n = th_ref.shape[-1]
    row = lax.broadcasted_iota(jnp.int32, (n, n), 0)
    col = lax.broadcasted_iota(jnp.int32, (n, n), 1)
    near = jnp.abs(row - col) <= CK // 2
    for a in range(CQ):
        wide = jnp.broadcast_to(fwd_ref[0, a : a + 1, :], (n, n))
        band = jnp.where(near, pltpu.roll(wide, 0, 1, stride=1, stride_axis=0), 0.0)
        hi, lo = split(band)
        th_ref[0, a * n : (a + 1) * n, :] = hi
        tl_ref[0, a * n : (a + 1) * n, :] = lo
        wide = jnp.broadcast_to(bwd_ref[0, a : a + 1, :], (n, n))
        band = jnp.where(near, pltpu.roll(wide, 0, 1, stride=1, stride_axis=0), 0.0)
        tt_ref[0, a * n : (a + 1) * n, :] = band.astype(BF)


def band_taps(kernel, n):
    half = CK // 2

    def around(taps):
        gap = jnp.zeros((H, CQ, n - CK), F32)
        rows = jnp.concatenate([taps[:, :, half:], gap, taps[:, :, :half]], axis=2)
        return jnp.pad(rows, ((0, 0), (0, 8 - CQ), (0, 0)))

    taps = kernel.reshape(H, CQ, CK)
    fwd, bwd = around(taps), around(taps[:, :, ::-1])
    row = pl.BlockSpec((1, 8, n), lambda h: (h, 0, 0))
    out = pl.BlockSpec((1, CQ * n, n), lambda h: (h, 0, 0))
    shape = jax.ShapeDtypeStruct((H, CQ * n, n), BF)
    return pl.pallas_call(
        taps_kernel,
        cost_estimate=cost(16),
        grid=(H,),
        in_specs=[row, row],
        out_specs=[out, out, out],
        out_shape=[shape, shape, shape],
    )(fwd, bwd)


def fence_kernel(*refs):
    del refs


def fence(*values, time=0.1):
    return pl.pallas_call(
        fence_kernel,
        cost_estimate=cost(time),
        in_specs=[pl.BlockSpec(memory_space=pl.ANY)] * len(values),
        out_specs=[pl.BlockSpec(memory_space=pl.ANY)] * len(values),
        out_shape=[jax.ShapeDtypeStruct(v.shape, v.dtype) for v in values],
        input_output_aliases={i: i for i in range(len(values))},
    )(*values)


def project_kernel(x_ref, gain_ref, w_ref, normed_ref, *part_refs):
    cols = part_refs[0].shape[0] // w_ref.shape[0]
    x = x_ref[...].astype(F32)
    normed = rms_norm(x, gain_ref[...]).astype(BF)
    normed_ref[...] = normed
    w = w_ref[:, :cols, :].reshape(-1, D)
    part = dot(w, normed, 1, 1).astype(BF)
    for b, ref in enumerate(part_refs):

        @pl.when(pl.program_id(0) == b)
        def _():
            ref[...] = part


def project(blocks, gain, w_attn, cols, n):
    lines, count = w_attn.shape[0], blocks.shape[0] // n
    rows = lines * cols
    if cols % 16:
        normed = rms_norm(blocks.astype(F32), gain).astype(BF)
        part = dot(w_attn[:, :cols].reshape(rows, D), normed, 1, 1).astype(BF)
        return normed, [part[:, b * n : (b + 1) * n] for b in range(count)]
    out = pl.pallas_call(
        project_kernel,
        cost_estimate=cost(1.2 * count),
        grid=(count,),
        in_specs=[
            pl.BlockSpec((n, D), lambda b: (b, 0)),
            pl.BlockSpec((1, D), lambda b: (0, 0)),
            pl.BlockSpec(w_attn.shape, lambda b: (0, 0, 0)),
        ],
        out_specs=[pl.BlockSpec((n, D), lambda b: (b, 0))]
        + [pl.BlockSpec((rows, n), lambda b: (0, 0))] * count,
        out_shape=[jax.ShapeDtypeStruct(blocks.shape, BF)]
        + [jax.ShapeDtypeStruct((rows, n), BF)] * count,
        compiler_params=pltpu.CompilerParams(vmem_limit_bytes=60 * 2**20),
    )(blocks, gain.reshape(1, D), w_attn)
    return out[0], out[1:]


def move_kernel(joins, count, cols, place_ref, *refs):
    *arrays, sems = refs
    if joins:
        *blocks, held = arrays
    else:
        whole, *blocks, held, sem = arrays
        first = pltpu.make_async_copy(whole, held, sem)
        first.start()
        first.wait()
    lines = held.shape[0]
    rows = lines * cols
    copies = []
    for b in range(8):
        other = place_ref[0] ^ order(b)
        for z in range(lines):
            part = blocks[b // count].at[pl.ds(b % count * rows + z * cols, cols)]
            spot = held.at[z, other & 3, other >> 2]
            pair = (part, spot) if joins else (spot, part)
            copies.append(pltpu.make_async_copy(*pair, sems.at[len(copies)]))
            copies[-1].start()
    for copy in copies:
        copy.wait()


def move(joins, values, place, lines, cols, n, count):
    anywhere = pl.BlockSpec(memory_space=pl.ANY)
    whole = (lines, 4, 2, cols, n)
    held = [pltpu.VMEM(whole, BF), pltpu.SemaphoreType.DMA(())]
    if joins:
        out_specs = pl.BlockSpec(memory_space=pltpu.VMEM)
        shape = jax.ShapeDtypeStruct(whole, BF)
    else:
        out_specs = [anywhere] * (8 // count)
        shape = [jax.ShapeDtypeStruct((lines * cols * count, n), BF)] * (8 // count)
    return pl.pallas_call(
        functools.partial(move_kernel, joins, count, cols),
        cost_estimate=cost(2),
        in_specs=[pl.BlockSpec(memory_space=pltpu.SMEM)] + [anywhere] * len(values),
        out_specs=out_specs,
        out_shape=shape,
        scratch_shapes=([] if joins else held) + [pltpu.SemaphoreType.DMA((8 * lines,))],
        compiler_params=pltpu.CompilerParams(vmem_limit_bytes=60 * 2**20),
    )(place.reshape(1), *values)


def out_project_kernel(half, place_ref, grp_ref, near_ref, far_ref, x_ref, gain_ref, mid_ref, sec_ref, held):
    size = near_ref.shape[0] // 4
    for b in range(8):
        other = place_ref[0] ^ order(b)
        w = (near_ref, far_ref)[b // 4][b % 4 * size : (b % 4 + 1) * size, :]
        part = dot(w, grp_ref[...], 1, 0)
        for z in range(size // half):
            start = pl.multiple_of((z * 8 + (other & 3) * 2 + (other >> 2)) * half, half)
            held[pl.ds(start, half), :] = part[z * half : (z + 1) * half, :]
    middle = x_ref[...] + held[...].T
    mid_ref[...] = middle
    sec_ref[...] = rms_norm(middle, gain_ref[...]).astype(BF)


def out_project(grouped, near, far, x, gain, place, lines, half):
    n = grouped.shape[1]
    if half % 16:
        w_out = join([near, far], place, lines, half)
        middle = x + dot(grouped, w_out, 0, 1)
        return middle, rms_norm(middle, gain).astype(BF)
    whole = lambda shape: pl.BlockSpec(shape, lambda t: (0, 0))
    return pl.pallas_call(
        functools.partial(out_project_kernel, half),
        cost_estimate=cost(6),
        grid=(1,),
        in_specs=[
            pl.BlockSpec(memory_space=pltpu.SMEM),
            whole((D, n)), whole(near.shape), whole(far.shape), whole((n, D)), whole((1, D)),
        ],
        out_specs=[whole((n, D)), whole((n, D))],
        out_shape=[jax.ShapeDtypeStruct((n, D), F32), jax.ShapeDtypeStruct((n, D), BF)],
        scratch_shapes=[pltpu.VMEM((D, n), F32)],
        compiler_params=pltpu.CompilerParams(vmem_limit_bytes=60 * 2**20),
    )(place.reshape(1), grouped, near, far, x, gain.reshape(1, D))


def out_grad_kernel(place_ref, branch_ref, grouped_ref, *refs):
    *outs, far_ref, held = refs
    wide, half = held.shape[0], held.shape[0] // 8
    size = outs[0].shape[0]
    lines = size // half
    for z in range(lines):
        held[...] = dot(branch_ref[:, z * wide : (z + 1) * wide], grouped_ref[...], 0, 1)
        for b in range(8):
            other = place_ref[0] ^ order(b)
            start = pl.multiple_of((other & 3) * 2 * half + (other >> 2) * half, half)
            ref, first = (outs[b], 0) if b < 4 else (far_ref, (b - 4) * size)
            ref[first + z * half : first + (z + 1) * half, :] = held[pl.ds(start, half), :].astype(BF)


def out_weight_grad(branch, grouped, place, lines, half):
    n = branch.shape[0]
    if half % 16:
        full = dot(branch, grouped, 0, 1).reshape(lines, 4, 2, half, D)
        blocks = []
        for b in range(8):
            other = place ^ order(b)
            block = lax.dynamic_slice(full, (0, other & 3, other >> 2, 0, 0), (lines, 1, 1, half, D))
            blocks.append(block.reshape(lines * half, D).astype(BF))
        return blocks[:4] + [jnp.concatenate(blocks[4:], axis=0)]
    return pl.pallas_call(
        out_grad_kernel,
        cost_estimate=cost(0),
        grid=(1,),
        in_specs=[
            pl.BlockSpec(memory_space=pltpu.SMEM),
            pl.BlockSpec((n, D), lambda t: (0, 0)),
            pl.BlockSpec((D, n), lambda t: (0, 0)),
        ],
        out_specs=[pl.BlockSpec((c * lines * half, D), lambda t: (0, 0)) for c in (1, 1, 1, 1, 4)],
        out_shape=[
            jax.ShapeDtypeStruct((c * lines * half, D), BF) for c in (1, 1, 1, 1, 4)
        ],
        scratch_shapes=[pltpu.VMEM((8 * half, D), F32)],
        compiler_params=pltpu.CompilerParams(vmem_limit_bytes=60 * 2**20),
    )(place.reshape(1), branch, grouped)


def join(values, place, lines, cols):
    count, n = 8 // len(values), values[0].shape[1]
    if cols % 16 == 0:
        return move(True, values, place, lines, cols, n, count).reshape(-1, n)
    out = jnp.zeros((lines, 4, 2, cols, n), BF)
    for b in range(8):
        source = place ^ order(b)
        block = values[b // count].reshape(count, lines, 1, 1, cols, n)[b % count]
        out = lax.dynamic_update_slice(out, block, (0, source & 3, source >> 2, 0, 0))
    return out.reshape(-1, n)


def cut(value, place, lines, cols):
    n = value.shape[1]
    value = value.reshape(lines, 4, 2, cols, n)
    if cols % 16 == 0:
        return move(False, [value], place, lines, cols, n, 1)
    pieces = []
    for b in range(8):
        target = place ^ order(b)
        piece = lax.dynamic_slice(value, (0, target & 3, target >> 2, 0, 0), (lines, 1, 1, cols, n))
        pieces.append(piece.reshape(lines * cols, n))
    return pieces


def order(b):
    return (b // 2 % 2) * 4 + (b % 2) * 2 + b // 4


def gated(gate, upper, d_hidden):
    sig = 1.0 / (1.0 + jnp.exp(-gate))
    act = gate * sig
    hidden = (act * upper).astype(BF)
    d_gate = (d_hidden * upper * (sig * (1.0 + gate * (1.0 - sig)))).astype(BF)
    return hidden, d_gate, (d_hidden * act).astype(BF)


def ffn_kernel(counts, *refs):
    runs = len(counts)
    w_ref, hid_ref, dgu_ref, *sums = refs[2 * runs : -2]
    t, ends = pl.program_id(0), [sum(counts[: r + 1]) for r in range(runs)]

    for r in range(runs if runs > 1 else 0):

        @pl.when((t >= ends[r] - counts[r]) & (t < ends[r]))
        def _():
            refs[-2][...] = refs[r][...]
            refs[-1][...] = refs[runs + r][...]

    lines, wide = w_ref.shape[0], w_ref.shape[1] // 3
    w_gu = w_ref[:, : 2 * wide, :].reshape(-1, D)
    w_down = w_ref[:, 2 * wide :, :].reshape(-1, D)
    s, o = (refs[-2][...], refs[-1][...]) if runs > 1 else (refs[0][...], refs[1][...])
    gu = dot(s, w_gu, 1, 1)
    dh = dot(o, w_down, 1, 1)
    for z in range(lines):
        lo, mid, hi = 2 * z * wide, (2 * z + 1) * wide, (2 * z + 2) * wide
        cut_h = slice(z * wide, (z + 1) * wide)
        hidden, d_gate, d_up = gated(gu[:, lo:mid], gu[:, mid:hi], dh[:, cut_h])
        hid_ref[:, cut_h] = hidden
        dgu_ref[:, lo:mid] = d_gate
        dgu_ref[:, mid:hi] = d_up
    ds = dot(dgu_ref[...], w_gu, 1, 0).astype(BF)
    yo = dot(hid_ref[...], w_down, 1, 0).astype(BF)
    for r in range(runs):

        @pl.when((t >= ends[r] - counts[r]) & (t < ends[r]))
        def _():
            sums[2 * r][...] = ds
            sums[2 * r + 1][...] = yo


def ffn(sources, w_ffn, n, time):
    counts = [count for _, _, _, _, count in sources]
    rows, lines, wide = sum(counts) * n, w_ffn.shape[0], w_ffn.shape[1] // 3
    if wide % 128:
        second, d_ffn = (
            jnp.concatenate([src[i][src[2 + i] * n : (src[2 + i] + src[4]) * n] for src in sources], axis=0)
            for i in range(2)
        )
        w_gu = w_ffn[:, : 2 * wide].reshape(-1, D)
        w_down = w_ffn[:, 2 * wide :].reshape(-1, D)
        gu = dot(second, w_gu, 1, 1).reshape(rows, lines, 2, wide)
        dh = dot(d_ffn, w_down, 1, 1).reshape(rows, lines, wide)
        hidden, d_gate, d_up = gated(gu[:, :, 0], gu[:, :, 1], dh)
        hidden = hidden.reshape(rows, lines * wide)
        d_gu = jnp.stack([d_gate, d_up], axis=2).reshape(rows, 2 * lines * wide)
        ds, yo = dot(d_gu, w_gu, 1, 0).astype(BF), dot(hidden, w_down, 1, 0).astype(BF)
        at, sums = 0, []
        for count in counts:
            sums += [v[at : at + count * n] for v in (ds, yo)]
            at += count * n
        return [hidden, d_gu] + sums

    def spec(part, first):
        start, count = sum(counts[:part]), counts[part]
        return pl.BlockSpec((n, D), lambda t: (jnp.clip(t - start, 0, count - 1) + first, 0))

    out = lambda width: pl.BlockSpec((n, width), lambda t: (t, 0))
    return pl.pallas_call(
        functools.partial(ffn_kernel, counts),
        cost_estimate=cost(time),
        grid=(rows // n,),
        in_specs=[spec(p, src[2 + i]) for i in range(2) for p, src in enumerate(sources)]
        + [pl.BlockSpec(memory_space=pltpu.VMEM)],
        out_specs=[out(lines * wide), out(2 * lines * wide)]
        + [spec(p, 0) for p in range(len(sources)) for _ in range(2)],
        out_shape=[
            jax.ShapeDtypeStruct((rows, lines * wide), BF),
            jax.ShapeDtypeStruct((rows, 2 * lines * wide), BF),
        ]
        + [jax.ShapeDtypeStruct((src[4] * n, D), BF) for src in sources for _ in range(2)],
        scratch_shapes=[pltpu.VMEM((n, D), BF)] * 2,
        compiler_params=pltpu.CompilerParams(vmem_limit_bytes=58 * 2**20),
    )(*(src[i] for i in range(2) for src in sources), w_ffn)


def ffn_grad_kernel(runs, *refs):
    hid, dgu, sec, dff = (refs[i * runs : (i + 1) * runs] for i in range(4))
    out_ref, gu_ref, down_ref = refs[4 * runs :]

    @pl.when(pl.program_id(0) == 0)
    def _():
        start = 0
        for h, d in zip(hid, dgu):
            rows = h.shape[0]
            gu_ref[:, start : start + rows] = d[...].T
            down_ref[:, start : start + rows] = h[...].T
            start += rows

    lines, wide = out_ref.shape[0], out_ref.shape[1] // 3
    gu, down, start = 0.0, 0.0, 0
    for a, b in zip(sec, dff):
        rows = slice(start, start + a.shape[0])
        gu = gu + dot(gu_ref[:, rows], a[...], 1, 0)
        down = down + dot(down_ref[:, rows], b[...], 1, 0)
        start += a.shape[0]
    for z in range(lines):
        out_ref[z, : 2 * wide, :] = gu[2 * z * wide : 2 * (z + 1) * wide, :].astype(BF)
        out_ref[z, 2 * wide :, :] = down[z * wide : (z + 1) * wide, :].astype(BF)


def ffn_grad(hidden, d_gu, second, d_ffn, lines, wide):
    if wide % 128:
        rows = lambda group: [v[f * c : (f + 1) * c] for v, c, f in group]
        gu = sum(dot(a, b, 0, 0) for a, b in zip(rows(d_gu), rows(second))).reshape(lines, 2 * wide, D)
        down = sum(dot(a, b, 0, 0) for a, b in zip(rows(hidden), rows(d_ffn))).reshape(lines, wide, D)
        return jnp.concatenate([gu, down], axis=1).astype(BF)
    step = 256
    whole = [
        pl.BlockSpec((c, v.shape[1]), lambda t, f=f: (f, 0)) for v, c, f in (*hidden, *d_gu)
    ]
    slab = [pl.BlockSpec((c, step), lambda t, f=f: (f, t)) for _, c, f in (*second, *d_ffn)]
    out, tall = (lines, 3 * wide), sum(c for _, c, _ in hidden)
    return pl.pallas_call(
        functools.partial(ffn_grad_kernel, len(hidden)),
        cost_estimate=cost(14),
        grid=(D // step,),
        in_specs=whole + slab,
        out_specs=pl.BlockSpec(out + (step,), lambda t: (0, 0, t)),
        out_shape=jax.ShapeDtypeStruct(out + (D,), BF),
        scratch_shapes=[
            pltpu.VMEM((2 * lines * wide, tall), BF),
            pltpu.VMEM((lines * wide, tall), BF),
        ],
        compiler_params=pltpu.CompilerParams(vmem_limit_bytes=60 * 2**20),
    )(*(v for group in (hidden, d_gu, second, d_ffn) for v, _, _ in group))


def qkv_grad_kernel(count, *refs):
    parts, (near_ref, far_ref, out_ref, held) = refs[:count], refs[count:]
    n = parts[0].shape[1]

    @pl.when(pl.program_id(0) == 0)
    def _():
        for b, part in enumerate(parts):
            held[:, b * n : (b + 1) * n] = part[...]

    rows = near_ref.shape[0]
    out_ref[...] = (
        dot(held[:, :rows], near_ref[...], 1, 0) + dot(held[:, rows:], far_ref[...], 1, 0)
    ).astype(BF)


def qkv_grad(parts, near, far, cols):
    rows, n = parts[0].shape
    if cols % 16:
        half = len(parts) // 2
        grads = (jnp.concatenate(p, axis=1) for p in (parts[:half], parts[half:]))
        return sum(dot(g, v, 1, 0) for g, v in zip(grads, (near, far))).astype(BF)
    step = 256
    slab = pl.BlockSpec((near.shape[0], step), lambda t: (0, t))
    return pl.pallas_call(
        functools.partial(qkv_grad_kernel, len(parts)),
        cost_estimate=cost(6),
        grid=(D // step,),
        in_specs=[pl.BlockSpec((rows, n), lambda t: (0, 0))] * len(parts) + [slab, slab],
        out_specs=pl.BlockSpec((rows, step), lambda t: (0, t)),
        out_shape=jax.ShapeDtypeStruct((rows, D), BF),
        scratch_shapes=[pltpu.VMEM((rows, len(parts) * n), BF)],
        compiler_params=pltpu.CompilerParams(vmem_limit_bytes=60 * 2**20),
    )(*parts, near, far)


def back_project_kernel(count, *refs):
    parts, (x_ref, w_ref, dn_ref, gain_ref) = refs[:count], refs[count:]
    rows = parts[0].shape[0]
    w = w_ref[:, : rows // w_ref.shape[0], :].reshape(rows, D)
    t = pl.program_id(0)

    @pl.when(t == 0)
    def _():
        gain_ref[...] = jnp.zeros_like(gain_ref)

    for b in range(count):

        @pl.when(t == b)
        def _():
            dn = dot(parts[b][...], w, 0, 0)
            dn_ref[...] = dn.astype(BF)
            x = x_ref[...].astype(F32)
            hat = x * lax.rsqrt(jnp.mean(x * x, axis=1, keepdims=True) + 1e-05)
            gain_ref[...] += jnp.sum(dn * hat, axis=0, keepdims=True)


def back_project(parts, x, first, w_attn, cols, n, time):
    lines, count = w_attn.shape[0], len(parts)
    rows = lines * cols
    if cols % 16:
        dn = dot(jnp.concatenate(parts, axis=1), w_attn[:, :cols].reshape(rows, D), 0, 0)
        values = x[first * n : (first + count) * n].astype(F32)
        hat = values * lax.rsqrt(jnp.mean(values * values, axis=1, keepdims=True) + 1e-05)
        return dn.astype(BF), jnp.sum(dn * hat, axis=0, keepdims=True)
    whole = lambda shape: pl.BlockSpec(shape, lambda b: (0,) * len(shape))
    return pl.pallas_call(
        functools.partial(back_project_kernel, count),
        cost_estimate=cost(time),
        grid=(count,),
        in_specs=[whole((rows, n))] * count
        + [pl.BlockSpec((n, D), lambda b: (b + first, 0)), whole(w_attn.shape)],
        out_specs=[pl.BlockSpec((n, D), lambda b: (b, 0)), whole((1, D))],
        out_shape=[
            jax.ShapeDtypeStruct((count * n, D), BF),
            jax.ShapeDtypeStruct((1, D), F32),
        ],
        compiler_params=pltpu.CompilerParams(vmem_limit_bytes=60 * 2**20),
    )(*parts, x, w_attn)


def doc_masks(drow_ref, dcol_ref, allow_ref, same_ref):
    n = allow_ref.shape[0]
    row = lax.broadcasted_iota(jnp.int32, (n, n), 0)
    col = lax.broadcasted_iota(jnp.int32, (n, n), 1)
    same = dcol_ref[...] == drow_ref[...]
    same_ref[...] = jnp.where(same, 1.0, 0.0)
    allow_ref[...] = jnp.where(same & (col <= row), 1.0, 0.0)


def attend_kernel(
    mix_ref, q_ref, k_ref, v_ref, th_ref, tl_ref, drow_ref, dcol_ref, gain_ref, *refs
):
    prob_ref, att_ref, grp_ref, allow_ref, same_ref, pad_ref, xh_ref, xl_ref = refs[-8:]
    g = pl.program_id(0)
    n = q_ref.shape[1]

    @pl.when(g == 0)
    def _():
        doc_masks(drow_ref, dcol_ref, allow_ref, same_ref)
        pad_ref[:, 0:8, :] = jnp.zeros((2, 8, n), F32)

    for e in range(2):
        q = q_ref[e * HD : (e + 1) * HD, :]
        k = k_ref[e * HD : (e + 1) * HD, :]
        logits = dot(q, k, 0, 0) * (HD ** (-0.5))
        pad_ref[e, 8 : 8 + n, :] = jnp.where(allow_ref[...] > 0, logits, 0.0)
        for a in range(CQ):
            part = jnp.where(same_ref[...] > 0, pad_ref[e, 8 - a : 8 - a + n, :], 0.0)
            hi, lo = split(part)
            xh_ref[e, :, a * n : (a + 1) * n] = hi
            xl_ref[e, :, a * n : (a + 1) * n] = lo
        conv = (
            dot(xh_ref[e], th_ref[e], 1, 0)
            + dot(xh_ref[e], tl_ref[e], 1, 0)
            + dot(xl_ref[e], th_ref[e], 1, 0)
        )
        scores = jnp.where(allow_ref[...] > 0, conv, NEG)
        weights = jnp.exp(scores - jnp.max(scores, axis=1, keepdims=True))
        prob_ref[e] = weights * (1.0 / jnp.sum(weights, axis=1, keepdims=True))
    for c in range(2):
        mixed = (mix_ref[g, 2 * c] * prob_ref[0] + mix_ref[g, 2 * c + 1] * prob_ref[1]).astype(BF)
        att = dot(v_ref[c * HD : (c + 1) * HD, :], mixed, 1, 1)
        att_ref[c * HD : (c + 1) * HD, :] = att
        centre = att - jnp.mean(att, axis=0, keepdims=True)
        spread = jnp.mean(centre * centre, axis=0, keepdims=True)
        grp_ref[c * HD : (c + 1) * HD, :] = (
            centre * lax.rsqrt(spread + 1e-05) * gain_ref[c * HD : (c + 1) * HD, :]
        ).astype(BF)


def attend(packed_t, docs, th, tl, mix, gain, start, count, before=()):
    n = packed_t.shape[1]
    blk = lambda off: pl.BlockSpec((PW, n), lambda g: (g + off, 0))
    tap = pl.BlockSpec((2, CQ * n, n), lambda g: (g + start, 0, 0))
    whole = lambda s: pl.BlockSpec(s, lambda g: (0, 0))
    return pl.pallas_call(
        attend_kernel,
        cost_estimate=cost(2.7 * count),
        grid=(count,),
        in_specs=[
            pl.BlockSpec(memory_space=pltpu.SMEM),
            blk(start), blk(PAIRS + start), blk(2 * PAIRS + start), tap, tap,
            whole((1, n)), whole((n, 1)),
            pl.BlockSpec((PW, 1), lambda g: (g + start, 0)),
        ]
        + [pl.BlockSpec(memory_space=pl.ANY)] * len(before),
        out_specs=[pl.BlockSpec((2, n, n), lambda g: (g, 0, 0)), blk(0), blk(start)],
        out_shape=[
            jax.ShapeDtypeStruct((2 * count, n, n), F32),
            jax.ShapeDtypeStruct((count * PW, n), F32),
            jax.ShapeDtypeStruct((D, n), BF),
        ],
        input_output_aliases={9: 2} if before else {},
        scratch_shapes=[
            pltpu.VMEM((n, n), F32), pltpu.VMEM((n, n), F32), pltpu.VMEM((2, n + 8, n), F32),
            pltpu.VMEM((2, n, CQ * n), BF), pltpu.VMEM((2, n, CQ * n), BF),
        ],
        compiler_params=pltpu.CompilerParams(vmem_limit_bytes=60 * 2**20),
    )(
        mix[start : start + count].reshape(count, 4), packed_t, packed_t, packed_t, th, tl,
        docs.reshape(1, n), docs.reshape(n, 1), gain, *before,
    )


def attend_back_kernel(
    first, mix_ref, q_ref, k_ref, v_ref, tt_ref, drow_ref, dcol_ref, gain_ref,
    prob_a_ref, prob_b_ref, att_a_ref, att_b_ref, dgrp_ref,
    d_ref, dgain_ref, dtap_ref, dmix_ref,
    allow_ref, same_ref, pad_ref, y_ref, dm_ref, prob_ref, att_ref,
):
    g = pl.program_id(0)
    n = q_ref.shape[1]
    scale = HD ** (-0.5)

    @pl.when(g == 0)
    def _():
        doc_masks(drow_ref, dcol_ref, allow_ref, same_ref)
        pad_ref[:, n : n + 8, :] = jnp.zeros((2, 8, n), F32)

    @pl.when(g < first)
    def _():
        prob_ref[...] = prob_a_ref[...]
        att_ref[...] = att_a_ref[...]

    @pl.when(g >= first)
    def _():
        prob_ref[...] = prob_b_ref[...]
        att_ref[...] = att_b_ref[...]

    for c in range(2):
        rows = slice(c * HD, (c + 1) * HD)
        att = att_ref[rows, :]
        centre = att - jnp.mean(att, axis=0, keepdims=True)
        rstd = lax.rsqrt(jnp.mean(centre * centre, axis=0, keepdims=True) + 1e-05)
        hat = centre * rstd
        dgrp = dgrp_ref[rows, :]
        dgain_ref[rows, :] = jnp.sum(dgrp * hat, axis=1, keepdims=True)
        dhat = dgrp * gain_ref[rows, :]
        datt = rstd * (
            dhat
            - jnp.mean(dhat, axis=0, keepdims=True)
            - hat * jnp.mean(dhat * hat, axis=0, keepdims=True)
        )
        datt = datt.astype(BF)
        mixed = (mix_ref[g, 2 * c] * prob_ref[0] + mix_ref[g, 2 * c + 1] * prob_ref[1]).astype(BF)
        d_ref[2, rows, :] = dot(datt, mixed, 1, 0).astype(BF)
        dmixed = dot(datt, v_ref[rows, :], 0, 0)
        dm_ref[c] = dmixed
        for e in range(2):
            dmix_ref[0, 2 * c + e : 2 * c + e + 1, :] = jnp.sum(dmixed * prob_ref[e], axis=0, keepdims=True)
    dmix_ref[0, 4:8, :] = jnp.zeros((4, n), F32)
    row = lax.broadcasted_iota(jnp.int32, (128, 128), 0)
    col = lax.broadcasted_iota(jnp.int32, (128, 128), 1)
    off = col - row
    half = CK // 2
    for e in range(2):
        rows = slice(e * HD, (e + 1) * HD)
        q = q_ref[rows, :]
        k = k_ref[rows, :]
        allowed = allow_ref[...] > 0
        masked_t = dot(k, q, 0, 0) * scale
        prob = prob_ref[e]
        dprob = mix_ref[g, e] * dm_ref[0] + mix_ref[g, 2 + e] * dm_ref[1]
        pad_ref[e, 0:n, :] = prob * (dprob - jnp.sum(prob * dprob, axis=1, keepdims=True))
        for a in range(CQ):
            y_ref[e, :, a * n : (a + 1) * n] = jnp.where(same_ref[...] > 0, pad_ref[e, a : a + n, :], 0.0).astype(BF)
        dlog = jnp.where(allowed, dot(y_ref[e], tt_ref[e], 1, 0), 0.0).astype(BF)
        d_ref[0, rows, :] = (dot(k, dlog, 1, 1) * scale).astype(BF)
        d_ref[1, rows, :] = (dot(q, dlog, 1, 0) * scale).astype(BF)
        krow = lax.broadcasted_iota(jnp.int32, (n, n), 0)
        qcol = lax.broadcasted_iota(jnp.int32, (n, n), 1)
        masked_t = jnp.where((same_ref[...] > 0) & (krow <= qcol), masked_t, 0.0).astype(BF)
        for a in range(CQ):
            full = dot(masked_t, y_ref[e, :, a * n : (a + 1) * n], 1, 0)
            fold = jnp.zeros((128, 128), F32)
            blocks = n // 128
            for r in range(blocks):
                fold = fold + full[r * 128 : (r + 1) * 128, r * 128 : (r + 1) * 128]
            fold = jnp.where(jnp.abs(off) <= half, fold, 0.0)
            for r in range(blocks - 1):
                up = full[r * 128 : (r + 1) * 128, (r + 1) * 128 : (r + 2) * 128]
                down = full[(r + 1) * 128 : (r + 2) * 128, r * 128 : (r + 1) * 128]
                fold = fold + jnp.where(off <= half - 128, up, 0.0) + jnp.where(off >= 128 - half, down, 0.0)
            lined = fold[0:8, :]
            for t in range(1, 16):
                lined = lined + pltpu.roll(fold[8 * t : 8 * t + 8, :], 128 - 8 * t, 1)
            dtap_ref[e, 8 * a : 8 * a + 8, :] = lined


def attend_back(packed_t, docs, tt, mix, gain, probs, atts, dgrp):
    n = packed_t.shape[1]
    first = probs[0].shape[0] // 2
    blk = lambda off: pl.BlockSpec((PW, n), lambda g: (g + off, 0))
    whole = lambda s: pl.BlockSpec(s, lambda g: (0, 0))
    thin = pl.BlockSpec((PW, 1), lambda g: (g, 0))
    low = lambda g: jnp.minimum(g, first - 1)
    high = lambda g: jnp.maximum(g - first, 0)
    return pl.pallas_call(
        functools.partial(attend_back_kernel, first),
        cost_estimate=cost(2.7 * PAIRS),
        grid=(PAIRS,),
        in_specs=[
            pl.BlockSpec(memory_space=pltpu.SMEM),
            blk(0), blk(PAIRS), blk(2 * PAIRS),
            pl.BlockSpec((2, CQ * n, n), lambda g: (g, 0, 0)),
            whole((1, n)), whole((n, 1)), thin,
            pl.BlockSpec((2, n, n), lambda g: (low(g), 0, 0)),
            pl.BlockSpec((2, n, n), lambda g: (high(g), 0, 0)),
            pl.BlockSpec((PW, n), lambda g: (low(g), 0)),
            pl.BlockSpec((PW, n), lambda g: (high(g), 0)),
            blk(0),
        ],
        out_specs=[
            pl.BlockSpec((3, PW, n), lambda g: (0, g, 0)), thin,
            pl.BlockSpec((2, 8 * CQ, 128), lambda g: (g, 0, 0)),
            pl.BlockSpec((1, 8, n), lambda g: (g, 0, 0)),
        ],
        out_shape=[
            jax.ShapeDtypeStruct((3, D, n), BF),
            jax.ShapeDtypeStruct((D, 1), F32),
            jax.ShapeDtypeStruct((H, 8 * CQ, 128), F32),
            jax.ShapeDtypeStruct((PAIRS, 8, n), F32),
        ],
        scratch_shapes=[
            pltpu.VMEM((n, n), F32), pltpu.VMEM((n, n), F32), pltpu.VMEM((2, n + 8, n), F32),
            pltpu.VMEM((2, n, CQ * n), BF), pltpu.VMEM((2, n, n), F32),
            pltpu.VMEM((2, n, n), F32), pltpu.VMEM((PW, n), F32),
        ],
        compiler_params=pltpu.CompilerParams(vmem_limit_bytes=60 * 2**20),
    )(
        mix.reshape(PAIRS, 4), packed_t, packed_t, packed_t, tt,
        docs.reshape(1, n), docs.reshape(n, 1), gain, *probs, *atts, dgrp,
    )


def fold_sums(dgain, dtap, dmix):
    lane = jnp.arange(128)[None, None, :] - jnp.arange(8)[None, :, None]
    tap = jnp.arange(CK)[:, None, None] - CK // 2
    pick = (jnp.remainder(lane - tap, 128) == 0).astype(F32)
    dtap = jnp.sum(dtap.reshape(H, CQ, 1, 8, 128) * pick, axis=(3, 4))
    dmix = jnp.sum(dmix[:, :4, :], axis=2)
    return jnp.concatenate([dgain[:, 0], dtap.reshape(-1), dmix.reshape(-1)])


def rms_norm(values, gain):
    return values * lax.rsqrt(jnp.mean(values * values, axis=-1, keepdims=True) + 1e-05) * gain


def rms_back(values, gain, grad):
    rstd = lax.rsqrt(jnp.mean(values * values, axis=-1, keepdims=True) + 1e-05)
    hat = values * rstd
    dhat = grad * gain
    dvalues = rstd * (dhat - hat * jnp.mean(dhat * hat, axis=-1, keepdims=True))
    return dvalues, jnp.sum(grad * hat, axis=0)


class Slice:
    def __init__(self, reps, shards):
        self.axes = ("rep", "fsdp")
        self.shards = shards
        self.lines = [[4 * o + i for o in range(shards // 4)] for i in range(4)]
        places = [(y, f) for y in range(reps) for f in range(shards)]

        def perm(move):
            out = []
            for y, f in places:
                to = move(y, f)
                out.append((y * shards + f, to[0] * shards + to[1]))
            return out

        self.hops = {
            (dy, di): perm(lambda y, f, dy=dy, di=di: (y ^ dy, f ^ di))
            for dy in range(2)
            for di in (range(16) if shards == 16 else range(4))
        }
        self.corner = perm(lambda y, f: (y, f ^ 2) if f & 1 else (1 - y, f))
        self.doubling = []
        bit = 1
        while bit < shards:
            self.doubling.append((bit, perm(lambda y, f, bit=bit: (y, f ^ bit))))
            bit *= 2
        self.rep = lax.axis_index("rep")
        self.fsdp = lax.axis_index("fsdp")
        self.odd = (self.fsdp & 1) == 1
        self.place = self.rep * 4 + (self.fsdp & 3)

    def hop(self, value, dy, di):
        return lax.ppermute(value, self.axes, self.hops[dy, di])

    def hop_block(self, value, b):
        return self.hop(value, order(b) >> 2, order(b) & 3) if b else value

    def gather_line(self, value):
        return lax.all_gather(value, "fsdp", axis=0, tiled=True, axis_index_groups=self.lines)

    def scatter_line(self, value):
        return lax.psum_scatter(
            value.astype(BF), "fsdp", scatter_dimension=0, tiled=True, axis_index_groups=self.lines
        )

    def gather_small(self, value):
        for bit, perm in self.doubling:
            other = lax.ppermute(value, self.axes, perm)
            high = (self.fsdp & bit) != 0
            value = jnp.concatenate(
                [jnp.where(high, other, value), jnp.where(high, value, other)], axis=0
            )
        return value

    def sides(self, value):
        return self.hop(value, 0, 2), self.hop(value, 1, 0)

    def far_corner(self, along_x, along_y):
        return lax.ppermute(jnp.where(self.odd, along_y, along_x), self.axes, self.corner)

    def near_blocks(self, value, along_x, along_y, corner):
        near = jnp.concatenate([value, along_x, along_y, jnp.zeros_like(value)], axis=0)
        return lax.dynamic_update_slice(near, corner, (3 * value.shape[0], 0))

    def scatter_corner(self, near, far):
        own, to_x, to_y, last = (a.astype(F32) + b.astype(F32) for a, b in zip(near, far))
        corner = lax.ppermute(last.astype(BF), self.axes, self.corner).astype(F32)
        to_x = (to_x + jnp.where(self.odd, 0.0, corner)).astype(BF)
        to_y = (to_y + jnp.where(self.odd, corner, 0.0)).astype(BF)
        return own, to_x, to_y

    def send_corner(self, near, far):
        return lax.ppermute((near.astype(F32) + far.astype(F32)).astype(BF), self.axes, self.corner)

    def with_corner(self, near, far, corner):
        corner = corner.astype(F32)
        to_x, to_y = (a.astype(F32) + b.astype(F32) for a, b in zip(near, far))
        to_x = (to_x + jnp.where(self.odd, 0.0, corner)).astype(BF)
        return to_x, (to_y + jnp.where(self.odd, corner, 0.0)).astype(BF)

    def scatter_last(self, own, to_x, to_y):
        return own + self.hop(to_x, 0, 2).astype(F32) + self.hop(to_y, 1, 0).astype(F32)

    def scatter_line_small(self, value):
        lines = self.shards // 4
        if lines != 4:
            return self.scatter_line(value).astype(F32)
        rows = value.shape[0] // lines
        value = value.astype(BF)
        line = self.fsdp // 4
        part = lambda d: lax.dynamic_slice_in_dim(value, (line ^ d) * rows, rows, axis=0)
        return sum([self.hop(part(d), 0, 4 * d).astype(F32) for d in range(1, 4)], part(0).astype(F32))

    def sum_small(self, value, bits):
        for bit, perm in self.doubling:
            if bit in bits:
                value = value + lax.ppermute(value, self.axes, perm)
        return value

    def both_halves(self, half, axis=0, other=None):
        if other is None:
            other = self.hop(half, 1, 0)
        first = self.rep == 0
        return jnp.concatenate(
            [jnp.where(first, half, other), jnp.where(first, other, half)], axis=axis
        ).astype(F32)

    def own_half(self, shard, rep=None):
        rows = shard.shape[0] // 2
        return lax.dynamic_slice_in_dim(shard, (self.rep if rep is None else rep) * rows, rows, axis=0)


def on_device(
    reps,
    shards,
    tokens,
    doc_ids,
    norm_gain,
    qkv_weight,
    group_gain,
    out_weight,
    ffn_gain,
    gate_weight,
    up_weight,
    down_weight,
    conv_kernel,
    head_mix,
    out_grad,
):
    net = Slice(reps, shards)
    lines = shards // 4
    n = tokens.shape[0]
    cols = 3 * D // shards // 2
    wide = gate_weight.shape[1] // 2

    half_out = D // shards // 2
    rows_of = lambda v: [v[b * n : (b + 1) * n] for b in range(v.shape[0] // n)]

    attn_half = jnp.concatenate([net.own_half(qkv_weight.T), net.own_half(out_weight.T)], axis=0)
    w_attn = net.gather_line(attn_half).reshape(lines, -1, D)
    x_side = net.sides(tokens)
    d_low = out_grad.astype(BF)
    d_side = net.sides(d_low)
    taps = band_taps(conv_kernel, n)
    gains, *sides = fence(
        jnp.stack([norm_gain, group_gain, ffn_gain])[None], *x_side, *d_side, *taps
    )
    x_side, d_side, (taps_hi, taps_lo, taps_back) = sides[:2], sides[2:4], sides[4:]
    rep = jnp.broadcast_to(net.rep, (8, 128))
    x_near, rep = fence(net.near_blocks(tokens, *x_side, net.far_corner(*x_side)), rep)
    x_far = net.hop(x_near, 0, 1)
    d_near = net.near_blocks(d_low, *d_side, net.far_corner(*d_side))
    gains = net.gather_small(gains)
    w_attn = fence(w_attn, time=100)[0]
    x_far = fence(x_far, time=40)[0]
    d_near = fence(d_near, time=60)[0]
    ffn_half = jnp.concatenate(
        [net.own_half(v, rep[0, 0]) for v in (gate_weight.T, up_weight.T, down_weight)], axis=0
    )
    w_attn, d_near, x_far, gains, ffn_half = fence(w_attn, d_near, x_far, gains, ffn_half)
    gains = gains.transpose(1, 0, 2).reshape(3, D).astype(F32)
    w_ffn = net.gather_line(ffn_half).reshape(lines, -1, D)
    w_cls = w_attn[:, cols:].reshape(-1, D)
    inputs = tokens.astype(F32)

    norm_near, parts = project(x_near, gains[0], w_attn, cols, n)
    norm_near, x_far, *parts = fence(norm_near, x_far, *parts)
    norm_far, more = project(x_far, gains[0], w_attn, cols, n)
    pieces = [net.hop_block(p, b) for b, p in enumerate((*parts, *more))]
    d_far = net.hop(d_near, 0, 1)
    pieces = fence(*pieces, time=45)
    *pieces, w_cls, d_far = fence(*pieces, w_cls, d_far)
    w_side = (*net.sides(w_cls), net.hop(w_cls, 1, 2))
    packed_t = join(pieces, net.place, lines, cols)
    group_col = gains[1].reshape(D, 1)
    heads = 5
    front = functools.partial(attend, packed_t, doc_ids, taps_hi, taps_lo, head_mix, group_col)
    *w_side, prob_a, att_a, grouped = fence(*w_side, *front(0, heads))
    w_near = jnp.concatenate([w_cls, *w_side], axis=0)
    w_far, prob_b, att_b, grouped = fence(
        net.hop(w_near, 0, 1), *front(heads, PAIRS - heads, (grouped,))
    )
    middle, second = out_project(grouped, w_near, w_far, inputs, gains[2], net.place, lines, half_out)
    w_near, w_far, second = fence(w_near, w_far, second)
    w_out = join([w_near, w_far], net.place, lines, half_out)
    s_side = net.sides(second)
    s_corner = net.far_corner(*s_side)
    s_a = jnp.concatenate([second, s_side[0]], axis=0)
    far_a = net.hop(s_a, 0, 1)
    w_ffn = fence(w_ffn, time=100)[0]
    run_a = ffn([(s_a, d_near, 0, 0, 2)], w_ffn, n, 7)
    s_corner, far_a, w_out, *run_a = fence(s_corner, far_a, w_out, *run_a)
    s_b = jnp.concatenate([s_side[1], s_corner], axis=0)
    far_b = net.hop(s_b, 0, 1)
    run_f = ffn([(far_a, d_far, 0, 0, 2), (far_b, d_far, 0, 2, 2)], w_ffn, n, 14)
    ds_f, ds_g = net.hop(run_f[2], 0, 1), net.hop(run_f[4], 0, 1)
    run_b = ffn([(s_b, d_near, 0, 2, 2)], w_ffn, n, 7)
    ds_f, ds_g, *run_b = fence(ds_f, ds_g, *run_b)
    corner = net.send_corner(run_b[2][n:], ds_g[n:])
    to_x, to_y = net.with_corner((run_a[2][n:], run_b[2][:n]), (ds_f[n:], ds_g[:n]), corner)
    own = run_a[2][:n].astype(F32) + ds_f[:n].astype(F32)
    to_x, to_y, *acts = fence(to_x, to_y, *[r[i] for i in range(2) for r in (run_a, run_f, run_b)])
    yo_f, yo_g = net.hop(run_f[3], 0, 1), net.hop(run_f[5], 0, 1)
    d_second = net.scatter_last(own, to_x, to_y)
    blocks = lambda a, f, b: [(a, 2 * n, 0), (f, 2 * n, 0), (f, 2 * n, 1), (b, 2 * n, 0)]
    g_ffn = ffn_grad(
        blocks(*acts[:3]),
        blocks(*acts[3:]),
        [(s_a, 2 * n, 0), (far_a, 2 * n, 0), (far_b, 2 * n, 0), (s_b, 2 * n, 0)],
        [(d_near, 2 * n, 0), (d_far, 2 * n, 0), (d_far, 2 * n, 1), (d_near, 2 * n, 1)],
        lines, wide,
    )
    d_second, yo_f, yo_g, g_ffn = fence(d_second, yo_f, yo_g, g_ffn)
    g_ffn = fence(net.scatter_line(g_ffn.reshape(-1, D)), time=80)[0]

    d_norm, g_ffn_gain = rms_back(middle, gains[2], d_second)
    d_middle = out_grad + d_norm
    branch = d_middle.astype(BF)
    d_grouped = dot(w_out, branch, 0, 1)
    corner = net.send_corner(run_b[3][n:], yo_g[n:])
    to_x, to_y = net.with_corner((run_a[3][n:], run_b[3][:n]), (yo_f[n:], yo_g[:n]), corner)
    own = run_a[3][:n].astype(F32) + yo_f[:n].astype(F32)
    to_x, to_y, d_grouped = fence(to_x, to_y, d_grouped)
    along_x, along_y = net.hop(to_x, 0, 2), net.hop(to_y, 1, 0)
    d_packed, g_group, g_taps, g_mix = attend_back(
        packed_t, doc_ids, taps_back, head_mix, group_col, (prob_a, prob_b), (att_a, att_b), d_grouped
    )
    along_x, along_y, d_packed = fence(along_x, along_y, d_packed)
    layer_out = (middle + (own + along_x.astype(F32) + along_y.astype(F32))).astype(BF)
    pieces = cut(d_packed.reshape(3 * D, n), net.place, lines, cols)
    *pieces, branch = fence(*pieces, branch)
    pieces = [net.hop_block(p, b) for b, p in enumerate(pieces)]
    g_blocks = out_weight_grad(branch, grouped, net.place, lines, half_out)
    pieces = fence(*pieces, time=52)
    *pieces, g_far, sums = fence(
        *pieces, net.hop(g_blocks[4], 0, 1), fold_sums(g_group, g_taps, g_mix)
    )
    size = lines * half_out
    g_far = [g_far[b * size : (b + 1) * size] for b in range(4)]
    own, to_x, to_y = net.scatter_corner(g_blocks[:4], g_far)
    g_qkv, g_ffn, *pieces = fence(qkv_grad(pieces, norm_near, norm_far, cols), g_ffn, *pieces)
    g_qkv = fence(net.scatter_line(g_qkv), time=20)[0]
    g_other = net.hop(g_ffn, 1, 0)
    near_c = back_project(pieces[3:4], x_near, 3, w_attn, cols, n, 1)
    far = back_project(pieces[4:], x_far, 0, w_attn, cols, n, 8)
    to_x, to_y, *rest = fence(to_x, to_y, *near_c, *far)
    near_c, far = rest[:2], rest[2:]
    dn_far = net.hop(far[0], 0, 1)
    along_x, along_y = net.hop(to_x, 0, 2), net.hop(to_y, 1, 0)
    corner = (near_c[0].astype(F32) + dn_far[3 * n :].astype(F32)).astype(BF)
    corner, *pieces = fence(corner, *pieces[:3])
    corner = net.hop(corner, 0, 2)
    *near, g_other, corner = fence(
        *back_project(pieces, x_near, 0, w_attn, cols, n, 1), g_other, corner
    )
    small = jnp.concatenate([near_c[1][0] + near[1][0] + far[1][0], g_ffn_gain, sums])
    small = net.sum_small(small, [bit for bit, _ in net.doubling if bit > 2])
    to_x, to_y = (near[0][b * n : (b + 1) * n].astype(F32) + dn_far[b * n : (b + 1) * n].astype(F32) for b in (1, 2))
    to_x, to_y = to_x.astype(BF), (to_y + corner.astype(F32)).astype(BF)
    to_x, to_y, small, g_other, along_x, along_y = fence(to_x, to_y, small, g_other, along_x, along_y)
    sent = fence(net.hop(to_x, 0, 2), net.hop(to_y, 1, 0), time=30)
    g_out = net.scatter_line_small(own + along_x.astype(F32) + along_y.astype(F32)).astype(BF)
    *sent, small, g_out, g_qkv = fence(*sent, small, g_out, g_qkv)
    small = net.sum_small(small, [1, 2])
    small = small + net.hop(small, 1, 0)
    d_normed = near[0][:n].astype(F32) + dn_far[:n].astype(F32) + sent[0].astype(F32) + sent[1].astype(F32)
    g_out = net.both_halves(g_out).T
    shape = (3, wide, D)
    g_ffn = net.both_halves(g_ffn.reshape(shape), 1, g_other.reshape(shape))
    g_gate, g_up, g_down = g_ffn[0].T, g_ffn[1].T, g_ffn[2]
    g_qkv = net.both_halves(g_qkv).T
    d_in = rms_back(inputs, gains[0], d_normed)[0]
    input_grad = d_middle + d_in

    part = D // shards
    gain_grads = [
        lax.dynamic_slice_in_dim(small, b * D + net.fsdp * part, part) for b in (0, 2, 1)
    ]
    g_taps = small[3 * D : 3 * D + H * CQ * CK].reshape(H, CQ * CK)
    g_mix = small[3 * D + H * CQ * CK :].reshape(PAIRS, 2, 2)
    return (
        layer_out,
        input_grad,
        gain_grads[0],
        g_qkv,
        gain_grads[1],
        g_out,
        gain_grads[2],
        g_gate,
        g_up,
        g_down,
        g_taps,
        g_mix,
    )


def solution(mesh):
    placed = (
        P(("rep", "fsdp"), None),
        P(("rep", "fsdp")),
        P("fsdp"),
        P(None, "fsdp"),
        P("fsdp"),
        P(None, "fsdp"),
        P("fsdp"),
        P(None, "fsdp"),
        P(None, "fsdp"),
        P("fsdp", None),
        P(),
        P(),
        P(("rep", "fsdp"), None),
    )
    return jax.shard_map(
        functools.partial(on_device, mesh.shape["rep"], mesh.shape["fsdp"]),
        mesh=mesh,
        in_specs=placed,
        out_specs=(
            P(("rep", "fsdp"), None),
            P(("rep", "fsdp"), None),
            P("fsdp"),
            P(None, "fsdp"),
            P("fsdp"),
            P(None, "fsdp"),
            P("fsdp"),
            P(None, "fsdp"),
            P(None, "fsdp"),
            P("fsdp", None),
            P(),
            P(),
        ),
        check_vma=False,
    )
```

```python
import functools
import jax
import jax.numpy as jnp
from jax import lax
from jax.experimental import pallas as pl
from jax.experimental.pallas import tpu as pltpu
from jax.sharding import PartitionSpec as P

D = 1536
H = 16
HD = 96
CQ = 6
CK = 11
NEG = -1e30
PAIRS = H // 2
PW = 2 * HD
BF = jnp.bfloat16
F32 = jnp.float32


def cost(time):
    return pl.CostEstimate(flops=int(time * 5e8), bytes_accessed=0, transcendentals=0)


def dot(a, b, ca, cb):
    return lax.dot_general(a, b, (((ca,), (cb,)), ((), ())), preferred_element_type=F32)


def split(v):
    hi = v.astype(BF)
    return hi, (v - hi.astype(F32)).astype(BF)


def taps_kernel(fwd_ref, bwd_ref, th_ref, tl_ref, tt_ref):
    n = th_ref.shape[-1]
    row = lax.broadcasted_iota(jnp.int32, (n, n), 0)
    col = lax.broadcasted_iota(jnp.int32, (n, n), 1)
    near = jnp.abs(row - col) <= CK // 2
    for a in range(CQ):
        wide = jnp.broadcast_to(fwd_ref[0, a : a + 1, :], (n, n))
        band = jnp.where(near, pltpu.roll(wide, 0, 1, stride=1, stride_axis=0), 0.0)
        hi, lo = split(band)
        th_ref[0, a * n : (a + 1) * n, :] = hi
        tl_ref[0, a * n : (a + 1) * n, :] = lo
        wide = jnp.broadcast_to(bwd_ref[0, a : a + 1, :], (n, n))
        band = jnp.where(near, pltpu.roll(wide, 0, 1, stride=1, stride_axis=0), 0.0)
        tt_ref[0, a * n : (a + 1) * n, :] = band.astype(BF)


def band_taps(kernel, n):
    half = CK // 2

    def around(taps):
        gap = jnp.zeros((H, CQ, n - CK), F32)
        rows = jnp.concatenate([taps[:, :, half:], gap, taps[:, :, :half]], axis=2)
        return jnp.pad(rows, ((0, 0), (0, 8 - CQ), (0, 0)))

    taps = kernel.reshape(H, CQ, CK)
    fwd, bwd = around(taps), around(taps[:, :, ::-1])
    row = pl.BlockSpec((1, 8, n), lambda h: (h, 0, 0))
    out = pl.BlockSpec((1, CQ * n, n), lambda h: (h, 0, 0))
    shape = jax.ShapeDtypeStruct((H, CQ * n, n), BF)
    return pl.pallas_call(
        taps_kernel,
        cost_estimate=cost(16),
        grid=(H,),
        in_specs=[row, row],
        out_specs=[out, out, out],
        out_shape=[shape, shape, shape],
    )(fwd, bwd)


def fence_kernel(*refs):
    del refs


def fence(*values, time=0.1):
    return pl.pallas_call(
        fence_kernel,
        cost_estimate=cost(time),
        in_specs=[pl.BlockSpec(memory_space=pl.ANY)] * len(values),
        out_specs=[pl.BlockSpec(memory_space=pl.ANY)] * len(values),
        out_shape=[jax.ShapeDtypeStruct(v.shape, v.dtype) for v in values],
        input_output_aliases={i: i for i in range(len(values))},
    )(*values)


def project_kernel(x_ref, gain_ref, w_ref, normed_ref, *part_refs):
    cols = part_refs[0].shape[0] // w_ref.shape[0]
    x = x_ref[...].astype(F32)
    normed = rms_norm(x, gain_ref[...]).astype(BF)
    normed_ref[...] = normed
    w = w_ref[:, :cols, :].reshape(-1, D)
    part = dot(w, normed, 1, 1).astype(BF)
    for b, ref in enumerate(part_refs):

        @pl.when(pl.program_id(0) == b)
        def _():
            ref[...] = part


def project(blocks, gain, w_attn, cols, n):
    lines, count = w_attn.shape[0], blocks.shape[0] // n
    rows = lines * cols
    if cols % 16:
        normed = rms_norm(blocks.astype(F32), gain).astype(BF)
        part = dot(w_attn[:, :cols].reshape(rows, D), normed, 1, 1).astype(BF)
        return normed, [part[:, b * n : (b + 1) * n] for b in range(count)]
    out = pl.pallas_call(
        project_kernel,
        cost_estimate=cost(0),
        grid=(count,),
        in_specs=[
            pl.BlockSpec((n, D), lambda b: (b, 0)),
            pl.BlockSpec((1, D), lambda b: (0, 0)),
            pl.BlockSpec(w_attn.shape, lambda b: (0, 0, 0)),
        ],
        out_specs=[pl.BlockSpec((n, D), lambda b: (b, 0))]
        + [pl.BlockSpec((rows, n), lambda b: (0, 0))] * count,
        out_shape=[jax.ShapeDtypeStruct(blocks.shape, BF)]
        + [jax.ShapeDtypeStruct((rows, n), BF)] * count,
        compiler_params=pltpu.CompilerParams(vmem_limit_bytes=60 * 2**20),
    )(blocks, gain.reshape(1, D), w_attn)
    return out[0], out[1:]


def move_kernel(joins, count, cols, place_ref, *refs):
    *arrays, sems = refs
    if joins:
        *blocks, held = arrays
    else:
        whole, *blocks, held, sem = arrays
        first = pltpu.make_async_copy(whole, held, sem)
        first.start()
        first.wait()
    lines = held.shape[0]
    rows = lines * cols
    copies = []
    for b in range(8):
        other = place_ref[0] ^ order(b)
        for z in range(lines):
            part = blocks[b // count].at[pl.ds(b % count * rows + z * cols, cols)]
            spot = held.at[z, other & 3, other >> 2]
            pair = (part, spot) if joins else (spot, part)
            copies.append(pltpu.make_async_copy(*pair, sems.at[len(copies)]))
            copies[-1].start()
    for copy in copies:
        copy.wait()


def move(joins, values, place, lines, cols, n, count):
    anywhere = pl.BlockSpec(memory_space=pl.ANY)
    whole = (lines, 4, 2, cols, n)
    held = [pltpu.VMEM(whole, BF), pltpu.SemaphoreType.DMA(())]
    if joins:
        out_specs = pl.BlockSpec(memory_space=pltpu.VMEM)
        shape = jax.ShapeDtypeStruct(whole, BF)
    else:
        out_specs = [anywhere] * (8 // count)
        shape = [jax.ShapeDtypeStruct((lines * cols * count, n), BF)] * (8 // count)
    return pl.pallas_call(
        functools.partial(move_kernel, joins, count, cols),
        cost_estimate=cost(2),
        in_specs=[pl.BlockSpec(memory_space=pltpu.SMEM)] + [anywhere] * len(values),
        out_specs=out_specs,
        out_shape=shape,
        scratch_shapes=([] if joins else held) + [pltpu.SemaphoreType.DMA((8 * lines,))],
        compiler_params=pltpu.CompilerParams(vmem_limit_bytes=60 * 2**20),
    )(place.reshape(1), *values)


def out_blocks_kernel(grp_ref, w_ref, out_ref):
    out_ref[...] = dot(w_ref[...], grp_ref[...], 1, 0)


def out_blocks(grouped, w):
    n = grouped.shape[1]
    return pl.pallas_call(
        out_blocks_kernel,
        cost_estimate=cost(0),
        out_shape=jax.ShapeDtypeStruct((w.shape[0], n), F32),
        compiler_params=pltpu.CompilerParams(vmem_limit_bytes=60 * 2**20),
    )(grouped, w)


def out_project_kernel(half, place_ref, grp_ref, far_ref, near_ref, x_ref, gain_ref, mid_ref, sec_ref, held):
    size = far_ref.shape[0] // 4
    for b in range(8):
        other = place_ref[0] ^ order(b)
        rows = slice(b % 4 * size, (b % 4 + 1) * size)
        part = near_ref[rows, :] if b < 4 else dot(far_ref[rows, :], grp_ref[...], 1, 0)
        for z in range(size // half):
            start = pl.multiple_of((z * 8 + (other & 3) * 2 + (other >> 2)) * half, half)
            held[pl.ds(start, half), :] = part[z * half : (z + 1) * half, :]
    middle = x_ref[...] + held[...].T
    mid_ref[...] = middle
    sec_ref[...] = rms_norm(middle, gain_ref[...]).astype(BF)


def out_project(grouped, near, far, out_near, x, gain, place, lines, half):
    n = grouped.shape[1]
    if half % 16:
        w_out = join([near, far], place, lines, half)
        middle = x + dot(grouped, w_out, 0, 1)
        return middle, rms_norm(middle, gain).astype(BF)
    whole = lambda shape: pl.BlockSpec(shape, lambda t: (0, 0))
    return pl.pallas_call(
        functools.partial(out_project_kernel, half),
        cost_estimate=cost(0),
        grid=(1,),
        in_specs=[
            pl.BlockSpec(memory_space=pltpu.SMEM),
            whole((D, n)), whole(far.shape), whole(out_near.shape), whole((n, D)), whole((1, D)),
        ],
        out_specs=[whole((n, D)), whole((n, D))],
        out_shape=[jax.ShapeDtypeStruct((n, D), F32), jax.ShapeDtypeStruct((n, D), BF)],
        scratch_shapes=[pltpu.VMEM((D, n), F32)],
        compiler_params=pltpu.CompilerParams(vmem_limit_bytes=60 * 2**20),
    )(place.reshape(1), grouped, far, out_near, x, gain.reshape(1, D))


def back_middle_kernel(
    a_ref, f_ref, sx_ref, sy_ref, mid_ref, dy_ref, gain_ref, w_ref, dm_ref, branch_ref, dgrp_ref, dgain_ref
):
    d_second = sum(r[...].astype(F32) for r in (a_ref, f_ref, sx_ref, sy_ref))
    d_norm, dgain = rms_back(mid_ref[...], gain_ref[...], d_second)
    d_middle = dy_ref[...] + d_norm
    dm_ref[...] = d_middle
    branch = d_middle.astype(BF)
    branch_ref[...] = branch
    dgain_ref[...] = dgain[None]
    dgrp_ref[...] = dot(branch, w_ref[...], 1, 0).T


def back_middle(own, far, along_x, along_y, middle, out_grad, gain, w_out):
    n = middle.shape[0]
    block = pl.BlockSpec((n, D), lambda t: (0, 0))
    whole = lambda shape: pl.BlockSpec(shape, lambda t: (0, 0))
    return pl.pallas_call(
        back_middle_kernel,
        cost_estimate=cost(6),
        grid=(1,),
        in_specs=[block] * 6 + [whole((1, D)), whole((D, D))],
        out_specs=[block, block, whole((D, n)), whole((1, D))],
        out_shape=[
            jax.ShapeDtypeStruct((n, D), F32), jax.ShapeDtypeStruct((n, D), BF),
            jax.ShapeDtypeStruct((D, n), F32), jax.ShapeDtypeStruct((1, D), F32),
        ],
        compiler_params=pltpu.CompilerParams(vmem_limit_bytes=60 * 2**20),
    )(own, far, along_x, along_y, middle, out_grad, gain.reshape(1, D), w_out)


def out_grad_kernel(place_ref, branch_ref, grouped_ref, *refs):
    *outs, far_ref, held = refs
    wide, half = held.shape[0], held.shape[0] // 8
    size = outs[0].shape[0]
    lines = size // half
    for z in range(lines):
        held[...] = dot(branch_ref[:, z * wide : (z + 1) * wide], grouped_ref[...], 0, 1)
        for b in range(8):
            other = place_ref[0] ^ order(b)
            start = pl.multiple_of((other & 3) * 2 * half + (other >> 2) * half, half)
            ref, first = (outs[b], 0) if b < 4 else (far_ref, (b - 4) * size)
            ref[first + z * half : first + (z + 1) * half, :] = held[pl.ds(start, half), :].astype(BF)


def out_weight_grad(branch, grouped, place, lines, half):
    n = branch.shape[0]
    if half % 16:
        full = dot(branch, grouped, 0, 1).reshape(lines, 4, 2, half, D)
        blocks = []
        for b in range(8):
            other = place ^ order(b)
            block = lax.dynamic_slice(full, (0, other & 3, other >> 2, 0, 0), (lines, 1, 1, half, D))
            blocks.append(block.reshape(lines * half, D).astype(BF))
        return blocks[:4] + [jnp.concatenate(blocks[4:], axis=0)]
    return pl.pallas_call(
        out_grad_kernel,
        cost_estimate=cost(0),
        grid=(1,),
        in_specs=[
            pl.BlockSpec(memory_space=pltpu.SMEM),
            pl.BlockSpec((n, D), lambda t: (0, 0)),
            pl.BlockSpec((D, n), lambda t: (0, 0)),
        ],
        out_specs=[pl.BlockSpec((c * lines * half, D), lambda t: (0, 0)) for c in (1, 1, 1, 1, 4)],
        out_shape=[
            jax.ShapeDtypeStruct((c * lines * half, D), BF) for c in (1, 1, 1, 1, 4)
        ],
        scratch_shapes=[pltpu.VMEM((8 * half, D), F32)],
        compiler_params=pltpu.CompilerParams(vmem_limit_bytes=60 * 2**20),
    )(place.reshape(1), branch, grouped)


def join(values, place, lines, cols):
    count, n = 8 // len(values), values[0].shape[1]
    if cols % 16 == 0:
        return move(True, values, place, lines, cols, n, count).reshape(-1, n)
    out = jnp.zeros((lines, 4, 2, cols, n), BF)
    for b in range(8):
        source = place ^ order(b)
        block = values[b // count].reshape(count, lines, 1, 1, cols, n)[b % count]
        out = lax.dynamic_update_slice(out, block, (0, source & 3, source >> 2, 0, 0))
    return out.reshape(-1, n)


def cut(value, place, lines, cols):
    n = value.shape[1]
    value = value.reshape(lines, 4, 2, cols, n)
    if cols % 16 == 0:
        return move(False, [value], place, lines, cols, n, 1)
    pieces = []
    for b in range(8):
        target = place ^ order(b)
        piece = lax.dynamic_slice(value, (0, target & 3, target >> 2, 0, 0), (lines, 1, 1, cols, n))
        pieces.append(piece.reshape(lines * cols, n))
    return pieces


def order(b):
    return (b // 2 % 2) * 4 + (b % 2) * 2 + b // 4


def gated(gate, upper, d_hidden):
    sig = 1.0 / (1.0 + jnp.exp(-gate))
    act = gate * sig
    hidden = (act * upper).astype(BF)
    d_gate = (d_hidden * upper * (sig * (1.0 + gate * (1.0 - sig)))).astype(BF)
    return hidden, d_gate, (d_hidden * act).astype(BF)


def ffn_kernel(counts, *refs):
    runs = len(counts)
    w_ref, hid_ref, dgu_ref, *sums = refs[2 * runs : -2]
    t, ends = pl.program_id(0), [sum(counts[: r + 1]) for r in range(runs)]

    for r in range(runs if runs > 1 else 0):

        @pl.when((t >= ends[r] - counts[r]) & (t < ends[r]))
        def _():
            refs[-2][...] = refs[r][...]
            refs[-1][...] = refs[runs + r][...]

    lines, wide = w_ref.shape[0], w_ref.shape[1] // 3
    w_gu = w_ref[:, : 2 * wide, :].reshape(-1, D)
    w_down = w_ref[:, 2 * wide :, :].reshape(-1, D)
    s, o = (refs[-2][...], refs[-1][...]) if runs > 1 else (refs[0][...], refs[1][...])
    gu = dot(s, w_gu, 1, 1)
    dh = dot(o, w_down, 1, 1)
    for z in range(lines):
        lo, mid, hi = 2 * z * wide, (2 * z + 1) * wide, (2 * z + 2) * wide
        cut_h = slice(z * wide, (z + 1) * wide)
        hidden, d_gate, d_up = gated(gu[:, lo:mid], gu[:, mid:hi], dh[:, cut_h])
        hid_ref[:, cut_h] = hidden
        dgu_ref[:, lo:mid] = d_gate
        dgu_ref[:, mid:hi] = d_up
    ds = dot(dgu_ref[...], w_gu, 1, 0).astype(BF)
    yo = dot(hid_ref[...], w_down, 1, 0).astype(BF)
    for r in range(runs):

        @pl.when((t >= ends[r] - counts[r]) & (t < ends[r]))
        def _():
            sums[2 * r][...] = ds
            sums[2 * r + 1][...] = yo


def ffn(sources, w_ffn, n, time):
    counts = [count for _, _, _, _, count in sources]
    rows, lines, wide = sum(counts) * n, w_ffn.shape[0], w_ffn.shape[1] // 3
    if wide % 128:
        second, d_ffn = (
            jnp.concatenate([src[i][src[2 + i] * n : (src[2 + i] + src[4]) * n] for src in sources], axis=0)
            for i in range(2)
        )
        w_gu = w_ffn[:, : 2 * wide].reshape(-1, D)
        w_down = w_ffn[:, 2 * wide :].reshape(-1, D)
        gu = dot(second, w_gu, 1, 1).reshape(rows, lines, 2, wide)
        dh = dot(d_ffn, w_down, 1, 1).reshape(rows, lines, wide)
        hidden, d_gate, d_up = gated(gu[:, :, 0], gu[:, :, 1], dh)
        hidden = hidden.reshape(rows, lines * wide)
        d_gu = jnp.stack([d_gate, d_up], axis=2).reshape(rows, 2 * lines * wide)
        ds, yo = dot(d_gu, w_gu, 1, 0).astype(BF), dot(hidden, w_down, 1, 0).astype(BF)
        at, sums = 0, []
        for count in counts:
            sums += [v[at : at + count * n] for v in (ds, yo)]
            at += count * n
        return [hidden, d_gu] + sums

    def spec(part, first):
        start, count = sum(counts[:part]), counts[part]
        return pl.BlockSpec((n, D), lambda t: (jnp.clip(t - start, 0, count - 1) + first, 0))

    out = lambda width: pl.BlockSpec((n, width), lambda t: (t, 0))
    return pl.pallas_call(
        functools.partial(ffn_kernel, counts),
        cost_estimate=cost(time),
        grid=(rows // n,),
        in_specs=[spec(p, src[2 + i]) for i in range(2) for p, src in enumerate(sources)]
        + [pl.BlockSpec(memory_space=pltpu.VMEM)],
        out_specs=[out(lines * wide), out(2 * lines * wide)]
        + [spec(p, 0) for p in range(len(sources)) for _ in range(2)],
        out_shape=[
            jax.ShapeDtypeStruct((rows, lines * wide), BF),
            jax.ShapeDtypeStruct((rows, 2 * lines * wide), BF),
        ]
        + [jax.ShapeDtypeStruct((src[4] * n, D), BF) for src in sources for _ in range(2)],
        scratch_shapes=[pltpu.VMEM((n, D), BF)] * 2,
        compiler_params=pltpu.CompilerParams(vmem_limit_bytes=58 * 2**20),
    )(*(src[i] for i in range(2) for src in sources), w_ffn)


def ffn_grad_kernel(runs, *refs):
    hid, dgu, sec, dff = (refs[i * runs : (i + 1) * runs] for i in range(4))
    out_ref, gu_ref, down_ref = refs[4 * runs :]

    @pl.when(pl.program_id(0) == 0)
    def _():
        start = 0
        for h, d in zip(hid, dgu):
            rows = h.shape[0]
            gu_ref[:, start : start + rows] = d[...].T
            down_ref[:, start : start + rows] = h[...].T
            start += rows

    lines, wide = out_ref.shape[0], out_ref.shape[1] // 3
    gu, down, start = 0.0, 0.0, 0
    for a, b in zip(sec, dff):
        rows = slice(start, start + a.shape[0])
        gu = gu + dot(gu_ref[:, rows], a[...], 1, 0)
        down = down + dot(down_ref[:, rows], b[...], 1, 0)
        start += a.shape[0]
    for z in range(lines):
        out_ref[z, : 2 * wide, :] = gu[2 * z * wide : 2 * (z + 1) * wide, :].astype(BF)
        out_ref[z, 2 * wide :, :] = down[z * wide : (z + 1) * wide, :].astype(BF)


def ffn_grad(hidden, d_gu, second, d_ffn, lines, wide):
    if wide % 128:
        rows = lambda group: [v[f * c : (f + 1) * c] for v, c, f in group]
        gu = sum(dot(a, b, 0, 0) for a, b in zip(rows(d_gu), rows(second))).reshape(lines, 2 * wide, D)
        down = sum(dot(a, b, 0, 0) for a, b in zip(rows(hidden), rows(d_ffn))).reshape(lines, wide, D)
        return jnp.concatenate([gu, down], axis=1).astype(BF)
    step = 256
    whole = [
        pl.BlockSpec((c, v.shape[1]), lambda t, f=f: (f, 0)) for v, c, f in (*hidden, *d_gu)
    ]
    slab = [pl.BlockSpec((c, step), lambda t, f=f: (f, t)) for _, c, f in (*second, *d_ffn)]
    out, tall = (lines, 3 * wide), sum(c for _, c, _ in hidden)
    return pl.pallas_call(
        functools.partial(ffn_grad_kernel, len(hidden)),
        cost_estimate=cost(14),
        grid=(D // step,),
        in_specs=whole + slab,
        out_specs=pl.BlockSpec(out + (step,), lambda t: (0, 0, t)),
        out_shape=jax.ShapeDtypeStruct(out + (D,), BF),
        scratch_shapes=[
            pltpu.VMEM((2 * lines * wide, tall), BF),
            pltpu.VMEM((lines * wide, tall), BF),
        ],
        compiler_params=pltpu.CompilerParams(vmem_limit_bytes=60 * 2**20),
    )(*(v for group in (hidden, d_gu, second, d_ffn) for v, _, _ in group))


def qkv_grad_kernel(count, *refs):
    parts, (near_ref, far_ref, out_ref, held) = refs[:count], refs[count:]
    n = parts[0].shape[1]

    @pl.when(pl.program_id(0) == 0)
    def _():
        for b, part in enumerate(parts):
            held[:, b * n : (b + 1) * n] = part[...]

    rows = near_ref.shape[0]
    out_ref[...] = (
        dot(held[:, :rows], near_ref[...], 1, 0) + dot(held[:, rows:], far_ref[...], 1, 0)
    ).astype(BF)


def qkv_grad(parts, near, far, cols):
    rows, n = parts[0].shape
    if cols % 16:
        half = len(parts) // 2
        grads = (jnp.concatenate(p, axis=1) for p in (parts[:half], parts[half:]))
        return sum(dot(g, v, 1, 0) for g, v in zip(grads, (near, far))).astype(BF)
    step = 256
    slab = pl.BlockSpec((near.shape[0], step), lambda t: (0, t))
    return pl.pallas_call(
        functools.partial(qkv_grad_kernel, len(parts)),
        cost_estimate=cost(6),
        grid=(D // step,),
        in_specs=[pl.BlockSpec((rows, n), lambda t: (0, 0))] * len(parts) + [slab, slab],
        out_specs=pl.BlockSpec((rows, step), lambda t: (0, t)),
        out_shape=jax.ShapeDtypeStruct((rows, D), BF),
        scratch_shapes=[pltpu.VMEM((rows, len(parts) * n), BF)],
        compiler_params=pltpu.CompilerParams(vmem_limit_bytes=60 * 2**20),
    )(*parts, near, far)


def normed_back_kernel(*refs):
    count = len(refs) // 2
    refs[-1][...] = sum(dot(p[...], w[...], 0, 0) for p, w in zip(refs[:count], refs[count:-1]))


def normed_back(parts, weights):
    vmem = pl.BlockSpec(memory_space=pltpu.VMEM)
    return pl.pallas_call(
        normed_back_kernel,
        cost_estimate=cost(1),
        in_specs=[vmem] * (2 * len(parts)),
        out_specs=vmem,
        out_shape=jax.ShapeDtypeStruct((parts[0].shape[1], D), F32),
        compiler_params=pltpu.CompilerParams(vmem_limit_bytes=60 * 2**20),
    )(*parts, *weights)


def input_back_kernel(*refs):
    p_ref, p2_ref, w_ref, w2_ref, before_ref, x_ref, dm_ref, gain_ref, out_ref, dgain_ref = refs
    d_normed = before_ref[...] + dot(p_ref[...], w_ref[...], 0, 0) + dot(p2_ref[...], w2_ref[...], 0, 0)
    d_in, dgain = rms_back(x_ref[...].astype(F32), gain_ref[...], d_normed)
    out_ref[...] = dm_ref[...] + d_in
    dgain_ref[...] = dgain[None]


def input_back(parts, weights, before, x, d_middle, gain):
    vmem = pl.BlockSpec(memory_space=pltpu.VMEM)
    return pl.pallas_call(
        input_back_kernel,
        cost_estimate=cost(5),
        in_specs=[vmem] * 8,
        out_specs=[vmem] * 2,
        out_shape=[jax.ShapeDtypeStruct(x.shape, F32), jax.ShapeDtypeStruct((1, D), F32)],
        compiler_params=pltpu.CompilerParams(vmem_limit_bytes=60 * 2**20),
    )(*parts, *weights, before, x, d_middle, gain.reshape(1, D))


def doc_masks(drow_ref, dcol_ref, allow_ref, same_ref):
    n = allow_ref.shape[0]
    row = lax.broadcasted_iota(jnp.int32, (n, n), 0)
    col = lax.broadcasted_iota(jnp.int32, (n, n), 1)
    same = dcol_ref[...] == drow_ref[...]
    same_ref[...] = jnp.where(same, 1.0, 0.0)
    allow_ref[...] = jnp.where(same & (col <= row), 1.0, 0.0)


def attend_kernel(
    mix_ref, q_ref, k_ref, v_ref, th_ref, tl_ref, drow_ref, dcol_ref, gain_ref, *refs
):
    prob_ref, att_ref, grp_ref, allow_ref, same_ref, pad_ref, xh_ref, xl_ref = refs[-8:]
    g = pl.program_id(0)
    n = q_ref.shape[1]

    @pl.when(g == 0)
    def _():
        doc_masks(drow_ref, dcol_ref, allow_ref, same_ref)
        pad_ref[:, 0:8, :] = jnp.zeros((2, 8, n), F32)

    for e in range(2):
        q = q_ref[e * HD : (e + 1) * HD, :]
        k = k_ref[e * HD : (e + 1) * HD, :]
        logits = dot(q, k, 0, 0) * (HD ** (-0.5))
        pad_ref[e, 8 : 8 + n, :] = jnp.where(allow_ref[...] > 0, logits, 0.0)
        for a in range(CQ):
            part = jnp.where(same_ref[...] > 0, pad_ref[e, 8 - a : 8 - a + n, :], 0.0)
            hi, lo = split(part)
            xh_ref[e, :, a * n : (a + 1) * n] = hi
            xl_ref[e, :, a * n : (a + 1) * n] = lo
        conv = (
            dot(xh_ref[e], th_ref[e], 1, 0)
            + dot(xh_ref[e], tl_ref[e], 1, 0)
            + dot(xl_ref[e], th_ref[e], 1, 0)
        )
        scores = jnp.where(allow_ref[...] > 0, conv, NEG)
        weights = jnp.exp(scores - jnp.max(scores, axis=1, keepdims=True))
        prob_ref[e] = weights * (1.0 / jnp.sum(weights, axis=1, keepdims=True))
    for c in range(2):
        mixed = (mix_ref[g, 2 * c] * prob_ref[0] + mix_ref[g, 2 * c + 1] * prob_ref[1]).astype(BF)
        att = dot(v_ref[c * HD : (c + 1) * HD, :], mixed, 1, 1)
        att_ref[c * HD : (c + 1) * HD, :] = att
        centre = att - jnp.mean(att, axis=0, keepdims=True)
        spread = jnp.mean(centre * centre, axis=0, keepdims=True)
        grp_ref[c * HD : (c + 1) * HD, :] = (
            centre * lax.rsqrt(spread + 1e-05) * gain_ref[c * HD : (c + 1) * HD, :]
        ).astype(BF)


def attend(packed_t, docs, th, tl, mix, gain, start, count, before=()):
    n = packed_t.shape[1]
    blk = lambda off: pl.BlockSpec((PW, n), lambda g: (g + off, 0))
    tap = pl.BlockSpec((2, CQ * n, n), lambda g: (g + start, 0, 0))
    whole = lambda s: pl.BlockSpec(s, lambda g: (0, 0))
    return pl.pallas_call(
        attend_kernel,
        cost_estimate=cost(0),
        grid=(count,),
        in_specs=[
            pl.BlockSpec(memory_space=pltpu.SMEM),
            blk(start), blk(PAIRS + start), blk(2 * PAIRS + start), tap, tap,
            whole((1, n)), whole((n, 1)),
            pl.BlockSpec((PW, 1), lambda g: (g + start, 0)),
        ]
        + [pl.BlockSpec(memory_space=pl.ANY)] * len(before),
        out_specs=[pl.BlockSpec((2, n, n), lambda g: (g, 0, 0)), blk(0), blk(start)],
        out_shape=[
            jax.ShapeDtypeStruct((2 * count, n, n), F32),
            jax.ShapeDtypeStruct((count * PW, n), F32),
            jax.ShapeDtypeStruct((D, n), BF),
        ],
        input_output_aliases={9: 2} if before else {},
        scratch_shapes=[
            pltpu.VMEM((n, n), F32), pltpu.VMEM((n, n), F32), pltpu.VMEM((2, n + 8, n), F32),
            pltpu.VMEM((2, n, CQ * n), BF), pltpu.VMEM((2, n, CQ * n), BF),
        ],
        compiler_params=pltpu.CompilerParams(vmem_limit_bytes=60 * 2**20),
    )(
        mix[start : start + count].reshape(count, 4), packed_t, packed_t, packed_t, th, tl,
        docs.reshape(1, n), docs.reshape(n, 1), gain, *before,
    )


def attend_back_kernel(
    mix_ref, q_ref, k_ref, v_ref, tt_ref, drow_ref, dcol_ref, gain_ref, prob_ref, att_ref, dgrp_ref,
    d_ref, dgain_ref, dtap_ref, dmix_ref,
    allow_ref, same_ref, pad_ref, y_ref, dm_ref,
):
    g = pl.program_id(0)
    n = q_ref.shape[1]
    scale = HD ** (-0.5)

    @pl.when(g == 0)
    def _():
        doc_masks(drow_ref, dcol_ref, allow_ref, same_ref)
        pad_ref[:, n : n + 8, :] = jnp.zeros((2, 8, n), F32)

    for c in range(2):
        rows = slice(c * HD, (c + 1) * HD)
        att = att_ref[rows, :]
        centre = att - jnp.mean(att, axis=0, keepdims=True)
        rstd = lax.rsqrt(jnp.mean(centre * centre, axis=0, keepdims=True) + 1e-05)
        hat = centre * rstd
        dgrp = dgrp_ref[rows, :]
        dgain_ref[rows, :] = jnp.sum(dgrp * hat, axis=1, keepdims=True)
        dhat = dgrp * gain_ref[rows, :]
        datt = rstd * (
            dhat
            - jnp.mean(dhat, axis=0, keepdims=True)
            - hat * jnp.mean(dhat * hat, axis=0, keepdims=True)
        )
        datt = datt.astype(BF)
        mixed = (mix_ref[g, 2 * c] * prob_ref[0] + mix_ref[g, 2 * c + 1] * prob_ref[1]).astype(BF)
        d_ref[2, rows, :] = dot(datt, mixed, 1, 0).astype(BF)
        dmixed = dot(datt, v_ref[rows, :], 0, 0)
        dm_ref[c] = dmixed
        for e in range(2):
            dmix_ref[0, 2 * c + e : 2 * c + e + 1, :] = jnp.sum(dmixed * prob_ref[e], axis=0, keepdims=True)
    dmix_ref[0, 4:8, :] = jnp.zeros((4, n), F32)
    row = lax.broadcasted_iota(jnp.int32, (128, 128), 0)
    col = lax.broadcasted_iota(jnp.int32, (128, 128), 1)
    off = col - row
    half = CK // 2
    for e in range(2):
        rows = slice(e * HD, (e + 1) * HD)
        q = q_ref[rows, :]
        k = k_ref[rows, :]
        allowed = allow_ref[...] > 0
        masked_t = dot(k, q, 0, 0) * scale
        prob = prob_ref[e]
        dprob = mix_ref[g, e] * dm_ref[0] + mix_ref[g, 2 + e] * dm_ref[1]
        pad_ref[e, 0:n, :] = prob * (dprob - jnp.sum(prob * dprob, axis=1, keepdims=True))
        for a in range(CQ):
            y_ref[e, :, a * n : (a + 1) * n] = jnp.where(same_ref[...] > 0, pad_ref[e, a : a + n, :], 0.0).astype(BF)
        dlog = jnp.where(allowed, dot(y_ref[e], tt_ref[e], 1, 0), 0.0).astype(BF)
        d_ref[0, rows, :] = (dot(k, dlog, 1, 1) * scale).astype(BF)
        d_ref[1, rows, :] = (dot(q, dlog, 1, 0) * scale).astype(BF)
        krow = lax.broadcasted_iota(jnp.int32, (n, n), 0)
        qcol = lax.broadcasted_iota(jnp.int32, (n, n), 1)
        masked_t = jnp.where((same_ref[...] > 0) & (krow <= qcol), masked_t, 0.0).astype(BF)
        for a in range(CQ):
            full = dot(masked_t, y_ref[e, :, a * n : (a + 1) * n], 1, 0)
            fold = jnp.zeros((128, 128), F32)
            blocks = n // 128
            for r in range(blocks):
                fold = fold + full[r * 128 : (r + 1) * 128, r * 128 : (r + 1) * 128]
            fold = jnp.where(jnp.abs(off) <= half, fold, 0.0)
            for r in range(blocks - 1):
                up = full[r * 128 : (r + 1) * 128, (r + 1) * 128 : (r + 2) * 128]
                down = full[(r + 1) * 128 : (r + 2) * 128, r * 128 : (r + 1) * 128]
                fold = fold + jnp.where(off <= half - 128, up, 0.0) + jnp.where(off >= 128 - half, down, 0.0)
            lined = fold[0:8, :]
            for t in range(1, 16):
                lined = lined + pltpu.roll(fold[8 * t : 8 * t + 8, :], 128 - 8 * t, 1)
            dtap_ref[e, 8 * a : 8 * a + 8, :] = lined


def attend_back(packed_t, docs, tt, mix, gain, prob, att, dgrp):
    n = packed_t.shape[1]
    blk = lambda off: pl.BlockSpec((PW, n), lambda g: (g + off, 0))
    whole = lambda s: pl.BlockSpec(s, lambda g: (0, 0))
    thin = pl.BlockSpec((PW, 1), lambda g: (g, 0))
    return pl.pallas_call(
        attend_back_kernel,
        cost_estimate=cost(24),
        grid=(PAIRS,),
        in_specs=[
            pl.BlockSpec(memory_space=pltpu.SMEM),
            blk(0), blk(PAIRS), blk(2 * PAIRS),
            pl.BlockSpec((2, CQ * n, n), lambda g: (g, 0, 0)),
            whole((1, n)), whole((n, 1)), thin,
            pl.BlockSpec((2, n, n), lambda g: (g, 0, 0)),
            blk(0), blk(0),
        ],
        out_specs=[
            pl.BlockSpec((3, PW, n), lambda g: (0, g, 0)), thin,
            pl.BlockSpec((2, 8 * CQ, 128), lambda g: (g, 0, 0)),
            pl.BlockSpec((1, 8, n), lambda g: (g, 0, 0)),
        ],
        out_shape=[
            jax.ShapeDtypeStruct((3, D, n), BF),
            jax.ShapeDtypeStruct((D, 1), F32),
            jax.ShapeDtypeStruct((H, 8 * CQ, 128), F32),
            jax.ShapeDtypeStruct((PAIRS, 8, n), F32),
        ],
        scratch_shapes=[
            pltpu.VMEM((n, n), F32), pltpu.VMEM((n, n), F32), pltpu.VMEM((2, n + 8, n), F32),
            pltpu.VMEM((2, n, CQ * n), BF), pltpu.VMEM((2, n, n), F32),
        ],
        compiler_params=pltpu.CompilerParams(vmem_limit_bytes=60 * 2**20),
    )(
        mix.reshape(PAIRS, 4), packed_t, packed_t, packed_t, tt,
        docs.reshape(1, n), docs.reshape(n, 1), gain, prob, att, dgrp,
    )


def fold_sums(dgain, dtap, dmix):
    lane = jnp.arange(128)[None, None, :] - jnp.arange(8)[None, :, None]
    tap = jnp.arange(CK)[:, None, None] - CK // 2
    pick = (jnp.remainder(lane - tap, 128) == 0).astype(F32)
    dtap = jnp.sum(dtap.reshape(H, CQ, 1, 8, 128) * pick, axis=(3, 4))
    dmix = jnp.sum(dmix[:, :4, :], axis=2)
    return jnp.concatenate([dgain[:, 0], dtap.reshape(-1), dmix.reshape(-1)])


def rms_norm(values, gain):
    return values * lax.rsqrt(jnp.mean(values * values, axis=-1, keepdims=True) + 1e-05) * gain


def rms_back(values, gain, grad):
    rstd = lax.rsqrt(jnp.mean(values * values, axis=-1, keepdims=True) + 1e-05)
    hat = values * rstd
    dhat = grad * gain
    dvalues = rstd * (dhat - hat * jnp.mean(dhat * hat, axis=-1, keepdims=True))
    return dvalues, jnp.sum(grad * hat, axis=0)


class Slice:
    def __init__(self, reps, shards):
        self.axes = ("rep", "fsdp")
        self.shards = shards
        self.lines = [[4 * o + i for o in range(shards // 4)] for i in range(4)]
        places = [(y, f) for y in range(reps) for f in range(shards)]

        def perm(move):
            out = []
            for y, f in places:
                to = move(y, f)
                out.append((y * shards + f, to[0] * shards + to[1]))
            return out

        self.hops = {
            (dy, di): perm(lambda y, f, dy=dy, di=di: (y ^ dy, f ^ di))
            for dy in range(2)
            for di in (range(16) if shards == 16 else range(4))
        }
        self.corner = perm(lambda y, f: (y, f ^ 2) if f & 1 else (1 - y, f))
        self.doubling = []
        bit = 1
        while bit < shards:
            self.doubling.append((bit, perm(lambda y, f, bit=bit: (y, f ^ bit))))
            bit *= 2
        self.rep = lax.axis_index("rep")
        self.fsdp = lax.axis_index("fsdp")
        self.odd = (self.fsdp & 1) == 1
        self.place = self.rep * 4 + (self.fsdp & 3)

    def hop(self, value, dy, di):
        return lax.ppermute(value, self.axes, self.hops[dy, di])

    def hop_block(self, value, b):
        return self.hop(value, order(b) >> 2, order(b) & 3) if b else value

    def gather_line(self, value):
        return lax.all_gather(value, "fsdp", axis=0, tiled=True, axis_index_groups=self.lines)

    def scatter_line(self, value):
        return lax.psum_scatter(
            value.astype(BF), "fsdp", scatter_dimension=0, tiled=True, axis_index_groups=self.lines
        )

    def gather_small(self, value):
        for bit, perm in self.doubling:
            other = lax.ppermute(value, self.axes, perm)
            high = (self.fsdp & bit) != 0
            value = jnp.concatenate(
                [jnp.where(high, other, value), jnp.where(high, value, other)], axis=0
            )
        return value

    def sides(self, value):
        return self.hop(value, 0, 2), self.hop(value, 1, 0)

    def far_corner(self, along_x, along_y):
        return lax.ppermute(jnp.where(self.odd, along_y, along_x), self.axes, self.corner)

    def near_blocks(self, value, along_x, along_y, corner):
        near = jnp.concatenate([value, along_x, along_y, jnp.zeros_like(value)], axis=0)
        return lax.dynamic_update_slice(near, corner, (3 * value.shape[0], 0))

    def scatter_corner(self, near, far):
        own, to_x, to_y, last = (a.astype(F32) + b.astype(F32) for a, b in zip(near, far))
        corner = lax.ppermute(last.astype(BF), self.axes, self.corner).astype(F32)
        to_x = (to_x + jnp.where(self.odd, 0.0, corner)).astype(BF)
        to_y = (to_y + jnp.where(self.odd, corner, 0.0)).astype(BF)
        return own, to_x, to_y

    def send_corner(self, near, far):
        return lax.ppermute((near.astype(F32) + far.astype(F32)).astype(BF), self.axes, self.corner)

    def with_corner(self, near, far, corner):
        corner = corner.astype(F32)
        to_x, to_y = (a.astype(F32) + b.astype(F32) for a, b in zip(near, far))
        to_x = (to_x + jnp.where(self.odd, 0.0, corner)).astype(BF)
        return to_x, (to_y + jnp.where(self.odd, corner, 0.0)).astype(BF)

    def scatter_last(self, own, to_x, to_y):
        return own + self.hop(to_x, 0, 2).astype(F32) + self.hop(to_y, 1, 0).astype(F32)

    def scatter_line_small(self, value):
        lines = self.shards // 4
        if lines != 4:
            return self.scatter_line(value).astype(F32)
        rows = value.shape[0] // lines
        value = value.astype(BF)
        line = self.fsdp // 4
        part = lambda d: lax.dynamic_slice_in_dim(value, (line ^ d) * rows, rows, axis=0)
        return sum([self.hop(part(d), 0, 4 * d).astype(F32) for d in range(1, 4)], part(0).astype(F32))

    def sum_small(self, value, bits):
        for bit, perm in self.doubling:
            if bit in bits:
                value = value + lax.ppermute(value, self.axes, perm)
        return value

    def both_halves(self, half, axis=0, other=None):
        if other is None:
            other = self.hop(half, 1, 0)
        first = self.rep == 0
        return jnp.concatenate(
            [jnp.where(first, half, other), jnp.where(first, other, half)], axis=axis
        ).astype(F32)

    def own_half(self, shard, rep=None):
        rows = shard.shape[0] // 2
        return lax.dynamic_slice_in_dim(shard, (self.rep if rep is None else rep) * rows, rows, axis=0)


def on_device(
    reps,
    shards,
    tokens,
    doc_ids,
    norm_gain,
    qkv_weight,
    group_gain,
    out_weight,
    ffn_gain,
    gate_weight,
    up_weight,
    down_weight,
    conv_kernel,
    head_mix,
    out_grad,
):
    net = Slice(reps, shards)
    lines = shards // 4
    n = tokens.shape[0]
    cols = 3 * D // shards // 2
    wide = gate_weight.shape[1] // 2

    half_out = D // shards // 2
    rows_of = lambda v: [v[b * n : (b + 1) * n] for b in range(v.shape[0] // n)]

    attn_half = jnp.concatenate([net.own_half(qkv_weight.T), net.own_half(out_weight.T)], axis=0)
    w_attn = net.gather_line(attn_half).reshape(lines, -1, D)
    ffn_half = jnp.concatenate(
        [net.own_half(v) for v in (gate_weight.T, up_weight.T, down_weight)], axis=0
    )
    w_ffn = net.gather_line(ffn_half).reshape(lines, -1, D)
    x_side = net.sides(tokens)
    d_low = out_grad.astype(BF)
    d_side = net.sides(d_low)
    taps = band_taps(conv_kernel, n)
    gains, *sides = fence(
        jnp.stack([norm_gain, group_gain, ffn_gain])[None], *x_side, *d_side, *taps
    )
    x_side, d_side, (taps_hi, taps_lo, taps_back) = sides[:2], sides[2:4], sides[4:]
    x_near = net.near_blocks(tokens, *x_side, net.far_corner(*x_side))
    x_far = net.hop(x_near, 0, 1)
    d_near = net.near_blocks(d_low, *d_side, net.far_corner(*d_side))
    gains = net.gather_small(gains)
    w_attn = fence(w_attn, time=100)[0]
    x_far = fence(x_far, time=40)[0]
    d_near = fence(d_near, time=60)[0]
    w_attn, d_near, x_far, gains = fence(w_attn, d_near, x_far, gains)
    gains = gains.transpose(1, 0, 2).reshape(3, D).astype(F32)
    w_cls = w_attn[:, cols:].reshape(-1, D)
    inputs = tokens.astype(F32)

    norm_near, parts = project(x_near, gains[0], w_attn, cols, n)
    norm_near, x_far, d_far, *parts = fence(norm_near, x_far, net.hop(d_near, 0, 1), *parts)
    norm_far, more = project(x_far, gains[0], w_attn, cols, n)
    pieces = [net.hop_block(p, b) for b, p in enumerate((*parts, *more))]
    pieces = fence(*pieces, time=45)
    w_qkv = w_attn[:, :cols].reshape(-1, D)
    *pieces, w_cls, d_far, w_qkv = fence(*pieces, w_cls, d_far, w_qkv)
    w_side = (*net.sides(w_cls), net.hop(w_cls, 1, 2))
    packed_t = join(pieces, net.place, lines, cols)
    group_col = gains[1].reshape(D, 1)
    *w_side, probs, attended, grouped = fence(
        *w_side,
        *attend(packed_t, doc_ids, taps_hi, taps_lo, head_mix, group_col, 0, PAIRS),
    )
    w_near = jnp.concatenate([w_cls, *w_side], axis=0)
    out_near, w_far = fence(out_blocks(grouped, w_near), net.hop(w_near, 0, 1))
    middle, second = out_project(
        grouped, w_near, w_far, out_near, inputs, gains[2], net.place, lines, half_out
    )
    w_near, w_far, second = fence(w_near, w_far, second)
    w_out = join([w_near, w_far], net.place, lines, half_out)
    *s_side, w_out = fence(*net.sides(second), w_out)
    s_corner = net.far_corner(*s_side)
    s_a = jnp.concatenate([second, s_side[0]], axis=0)
    far_a = net.hop(s_a, 0, 1)
    w_ffn = fence(w_ffn, time=40)[0]
    run_a = ffn([(s_a, d_near, 0, 0, 2)], w_ffn, n, 7)
    s_corner, far_a, w_qkv, *run_a = fence(s_corner, far_a, w_qkv, *run_a)
    w_side = net.sides(w_qkv)
    s_b = jnp.concatenate([s_side[1], s_corner], axis=0)
    far_b = net.hop(s_b, 0, 1)
    run_b = ffn([(s_b, d_near, 0, 2, 2)], w_ffn, n, 7)
    far_a, far_b, *run_b = fence(far_a, far_b, *run_b)
    run_f = ffn([(far_a, d_far, 0, 0, 2), (far_b, d_far, 0, 2, 2)], w_ffn, n, 2)
    ds_g, *w_side = fence(net.hop(run_f[4], 0, 1), *w_side)
    size_q = lines * cols // 2
    corner = net.send_corner(run_b[2][n:], ds_g[n:])
    ds_f, yo_f, yo_g = (net.hop(run_f[i], 0, 1) for i in (2, 3, 5))
    to_x, to_y = net.with_corner((run_a[2][n:], run_b[2][:n]), (ds_f[n:], ds_g[:n]), corner)
    last = (run_b[3][n:].astype(F32) + yo_g[n:].astype(F32)).astype(BF)
    to_x, to_y, last, *rest = fence(
        to_x, to_y, last, w_qkv, *w_side, w_side[1][:size_q], w_side[0][size_q:], *[r[i] for i in range(2) for r in (run_a, run_f, run_b)]
    )
    w_near, w_corner, acts = rest[:3], rest[3:5], rest[5:]
    w_far = [net.hop(w, 0, 1) for w in w_near]
    along_x, along_y = net.hop(to_x, 0, 2), net.hop(to_y, 1, 0)
    blocks = lambda a, f, b: [(a, 2 * n, 0), (f, 2 * n, 0), (f, 2 * n, 1), (b, 2 * n, 0)]
    g_ffn = ffn_grad(
        blocks(*acts[:3]),
        blocks(*acts[3:]),
        [(s_a, 2 * n, 0), (far_a, 2 * n, 0), (far_b, 2 * n, 0), (s_b, 2 * n, 0)],
        [(d_near, 2 * n, 0), (d_far, 2 * n, 0), (d_far, 2 * n, 1), (d_near, 2 * n, 1)],
        lines, wide,
    )
    along_x, along_y, last, g_ffn, *w_far = fence(along_x, along_y, last, g_ffn, *w_far)
    g_ffn = fence(net.scatter_line(g_ffn.reshape(-1, D)), time=80)[0]
    corner = lax.ppermute(last, net.axes, net.corner)
    d_middle, branch, d_grouped, g_ffn_gain = back_middle(
        run_a[2], ds_f, along_x, along_y, middle, out_grad, gains[2], w_out
    )
    to_x, to_y = net.with_corner((run_a[3][n:], run_b[3][:n]), (yo_f[n:], yo_g[:n]), corner)
    own = run_a[3][:n].astype(F32) + yo_f[:n].astype(F32)
    to_x, to_y, d_grouped, *w_corner = fence(to_x, to_y, d_grouped, *w_corner)
    w_corner = (net.hop(w_corner[0], 0, 2), net.hop(w_corner[1], 1, 0))
    along_x, along_y = net.hop(to_x, 0, 2), net.hop(to_y, 1, 0)
    d_packed, g_group, g_taps, g_mix = attend_back(
        packed_t, doc_ids, taps_back, head_mix, group_col, probs, attended, d_grouped
    )
    along_x, along_y, d_packed, *w_corner = fence(along_x, along_y, d_packed, *w_corner)
    w_near.append(jnp.concatenate(w_corner, axis=0))
    w_far.append(net.hop(w_near[3], 0, 1))
    layer_out = (middle + (own + along_x.astype(F32) + along_y.astype(F32))).astype(BF)
    pieces = cut(d_packed.reshape(3 * D, n), net.place, lines, cols)
    *cuts, branch = fence(*pieces, branch)
    pieces = [net.hop_block(p, b) for b, p in enumerate(cuts)]
    g_blocks = out_weight_grad(branch, grouped, net.place, lines, half_out)
    pieces = fence(*pieces, time=52)
    g_far, sums, w_near[3], w_far[3], *pieces = fence(
        net.hop(g_blocks[4], 0, 1), fold_sums(g_group, g_taps, g_mix), w_near[3], w_far[3], *pieces, *cuts
    )
    pieces, cuts = pieces[:8], pieces[8:]
    size = lines * half_out
    g_far = [g_far[b * size : (b + 1) * size] for b in range(4)]
    out_own, to_x, to_y = net.scatter_corner(g_blocks[:4], g_far)
    g_qkv, g_ffn, to_x, to_y, *cuts = fence(
        qkv_grad(pieces, norm_near, norm_far, cols), g_ffn, to_x, to_y, *cuts
    )
    g_qkv = fence(net.scatter_line(g_qkv), time=20)[0]
    g_other = net.hop(g_ffn, 1, 0)
    along_x, along_y = net.hop(to_x, 0, 2), net.hop(to_y, 1, 0)
    d_normed = normed_back([*cuts[:3], *cuts[4:7]], [*w_near[:3], *w_far[:3]])
    input_grad, g_norm = input_back([cuts[3], cuts[7]], [w_near[3], w_far[3]], d_normed, tokens, d_middle, gains[0])
    small = jnp.concatenate([g_norm[0], g_ffn_gain[0], sums])
    small = net.sum_small(small, [bit for bit, _ in net.doubling])
    along_x, along_y, g_other = fence(along_x, along_y, g_other, time=20)
    along_x, along_y, g_other, small, g_qkv = fence(along_x, along_y, g_other, small, g_qkv)
    q_other = net.hop(g_qkv, 1, 0)
    small = small + net.hop(small, 1, 0)
    g_out = net.scatter_line_small(out_own + along_x.astype(F32) + along_y.astype(F32)).astype(BF)
    g_out = net.both_halves(g_out).T
    shape = (3, wide, D)
    g_ffn = net.both_halves(g_ffn.reshape(shape), 1, g_other.reshape(shape))
    g_gate, g_up, g_down = g_ffn[0].T, g_ffn[1].T, g_ffn[2]
    g_qkv = net.both_halves(g_qkv, 0, q_other).T

    part = D // shards
    gain_grads = [
        lax.dynamic_slice_in_dim(small, b * D + net.fsdp * part, part) for b in (0, 2, 1)
    ]
    g_taps = small[3 * D : 3 * D + H * CQ * CK].reshape(H, CQ * CK)
    g_mix = small[3 * D + H * CQ * CK :].reshape(PAIRS, 2, 2)
    return (
        layer_out,
        input_grad,
        gain_grads[0],
        g_qkv,
        gain_grads[1],
        g_out,
        gain_grads[2],
        g_gate,
        g_up,
        g_down,
        g_taps,
        g_mix,
    )


def solution(mesh):
    placed = (
        P(("rep", "fsdp"), None),
        P(("rep", "fsdp")),
        P("fsdp"),
        P(None, "fsdp"),
        P("fsdp"),
        P(None, "fsdp"),
        P("fsdp"),
        P(None, "fsdp"),
        P(None, "fsdp"),
        P("fsdp", None),
        P(),
        P(),
        P(("rep", "fsdp"), None),
    )
    return jax.shard_map(
        functools.partial(on_device, mesh.shape["rep"], mesh.shape["fsdp"]),
        mesh=mesh,
        in_specs=placed,
        out_specs=(
            P(("rep", "fsdp"), None),
            P(("rep", "fsdp"), None),
            P("fsdp"),
            P(None, "fsdp"),
            P("fsdp"),
            P(None, "fsdp"),
            P("fsdp"),
            P(None, "fsdp"),
            P(None, "fsdp"),
            P("fsdp", None),
            P(),
            P(),
        ),
        check_vma=False,
    )
```

```python
import functools
import jax
import jax.numpy as jnp
from jax import lax
from jax.experimental import pallas as pl
from jax.experimental.pallas import tpu as pltpu
from jax.sharding import PartitionSpec as P

D = 1536
H = 16
HD = 96
CQ = 6
CK = 11
NEG = -1e30
PAIRS = H // 2
PW = 2 * HD
BF = jnp.bfloat16
F32 = jnp.float32


def cost(time):
    return pl.CostEstimate(flops=int(time * 5e8), bytes_accessed=0, transcendentals=0)


def dot(a, b, ca, cb):
    return lax.dot_general(a, b, (((ca,), (cb,)), ((), ())), preferred_element_type=F32)


def split(v):
    hi = v.astype(BF)
    return hi, (v - hi.astype(F32)).astype(BF)


def taps_kernel(fwd_ref, bwd_ref, th_ref, tl_ref, tt_ref):
    n = th_ref.shape[-1]
    row = lax.broadcasted_iota(jnp.int32, (n, n), 0)
    col = lax.broadcasted_iota(jnp.int32, (n, n), 1)
    near = jnp.abs(row - col) <= CK // 2
    for a in range(CQ):
        wide = jnp.broadcast_to(fwd_ref[0, a : a + 1, :], (n, n))
        band = jnp.where(near, pltpu.roll(wide, 0, 1, stride=1, stride_axis=0), 0.0)
        hi, lo = split(band)
        th_ref[0, a * n : (a + 1) * n, :] = hi
        tl_ref[0, a * n : (a + 1) * n, :] = lo
        wide = jnp.broadcast_to(bwd_ref[0, a : a + 1, :], (n, n))
        band = jnp.where(near, pltpu.roll(wide, 0, 1, stride=1, stride_axis=0), 0.0)
        tt_ref[0, a * n : (a + 1) * n, :] = band.astype(BF)


def band_taps(kernel, n):
    half = CK // 2

    def around(taps):
        gap = jnp.zeros((H, CQ, n - CK), F32)
        rows = jnp.concatenate([taps[:, :, half:], gap, taps[:, :, :half]], axis=2)
        return jnp.pad(rows, ((0, 0), (0, 8 - CQ), (0, 0)))

    taps = kernel.reshape(H, CQ, CK)
    fwd, bwd = around(taps), around(taps[:, :, ::-1])
    row = pl.BlockSpec((1, 8, n), lambda h: (h, 0, 0))
    out = pl.BlockSpec((1, CQ * n, n), lambda h: (h, 0, 0))
    shape = jax.ShapeDtypeStruct((H, CQ * n, n), BF)
    return pl.pallas_call(
        taps_kernel,
        cost_estimate=cost(16),
        grid=(H,),
        in_specs=[row, row],
        out_specs=[out, out, out],
        out_shape=[shape, shape, shape],
    )(fwd, bwd)


def fence_kernel(*refs):
    del refs


def fence(*values, time=0.1):
    return pl.pallas_call(
        fence_kernel,
        cost_estimate=cost(time),
        in_specs=[pl.BlockSpec(memory_space=pl.ANY)] * len(values),
        out_specs=[pl.BlockSpec(memory_space=pl.ANY)] * len(values),
        out_shape=[jax.ShapeDtypeStruct(v.shape, v.dtype) for v in values],
        input_output_aliases={i: i for i in range(len(values))},
    )(*values)


def project_kernel(x_ref, gain_ref, w_ref, normed_ref, *part_refs):
    cols = part_refs[0].shape[0] // w_ref.shape[0]
    x = x_ref[...].astype(F32)
    normed = rms_norm(x, gain_ref[...]).astype(BF)
    normed_ref[...] = normed
    w = w_ref[:, :cols, :].reshape(-1, D)
    part = dot(w, normed, 1, 1).astype(BF)
    for b, ref in enumerate(part_refs):

        @pl.when(pl.program_id(0) == b)
        def _():
            ref[...] = part


def project(blocks, gain, w_attn, cols, n):
    lines, count = w_attn.shape[0], blocks.shape[0] // n
    rows = lines * cols
    if cols % 16:
        normed = rms_norm(blocks.astype(F32), gain).astype(BF)
        part = dot(w_attn[:, :cols].reshape(rows, D), normed, 1, 1).astype(BF)
        return normed, [part[:, b * n : (b + 1) * n] for b in range(count)]
    out = pl.pallas_call(
        project_kernel,
        cost_estimate=cost(0),
        grid=(count,),
        in_specs=[
            pl.BlockSpec((n, D), lambda b: (b, 0)),
            pl.BlockSpec((1, D), lambda b: (0, 0)),
            pl.BlockSpec(w_attn.shape, lambda b: (0, 0, 0)),
        ],
        out_specs=[pl.BlockSpec((n, D), lambda b: (b, 0))]
        + [pl.BlockSpec((rows, n), lambda b: (0, 0))] * count,
        out_shape=[jax.ShapeDtypeStruct(blocks.shape, BF)]
        + [jax.ShapeDtypeStruct((rows, n), BF)] * count,
        compiler_params=pltpu.CompilerParams(vmem_limit_bytes=60 * 2**20),
    )(blocks, gain.reshape(1, D), w_attn)
    return out[0], out[1:]


def move_kernel(joins, count, cols, place_ref, *refs):
    *arrays, sems = refs
    if joins:
        *blocks, held = arrays
    else:
        whole, *blocks, held, sem = arrays
        first = pltpu.make_async_copy(whole, held, sem)
        first.start()
        first.wait()
    lines = held.shape[0]
    rows = lines * cols
    copies = []
    for b in range(8):
        other = place_ref[0] ^ order(b)
        for z in range(lines):
            part = blocks[b // count].at[pl.ds(b % count * rows + z * cols, cols)]
            spot = held.at[z, other & 3, other >> 2]
            pair = (part, spot) if joins else (spot, part)
            copies.append(pltpu.make_async_copy(*pair, sems.at[len(copies)]))
            copies[-1].start()
    for copy in copies:
        copy.wait()


def move(joins, values, place, lines, cols, n, count):
    anywhere = pl.BlockSpec(memory_space=pl.ANY)
    whole = (lines, 4, 2, cols, n)
    held = [pltpu.VMEM(whole, BF), pltpu.SemaphoreType.DMA(())]
    if joins:
        out_specs = pl.BlockSpec(memory_space=pltpu.VMEM)
        shape = jax.ShapeDtypeStruct(whole, BF)
    else:
        out_specs = [anywhere] * (8 // count)
        shape = [jax.ShapeDtypeStruct((lines * cols * count, n), BF)] * (8 // count)
    return pl.pallas_call(
        functools.partial(move_kernel, joins, count, cols),
        cost_estimate=cost(2),
        in_specs=[pl.BlockSpec(memory_space=pltpu.SMEM)] + [anywhere] * len(values),
        out_specs=out_specs,
        out_shape=shape,
        scratch_shapes=([] if joins else held) + [pltpu.SemaphoreType.DMA((8 * lines,))],
        compiler_params=pltpu.CompilerParams(vmem_limit_bytes=60 * 2**20),
    )(place.reshape(1), *values)


def out_blocks_kernel(grp_ref, w_ref, out_ref):
    out_ref[...] = dot(w_ref[...], grp_ref[...], 1, 0)


def out_blocks(grouped, w):
    n = grouped.shape[1]
    return pl.pallas_call(
        out_blocks_kernel,
        cost_estimate=cost(0),
        out_shape=jax.ShapeDtypeStruct((w.shape[0], n), F32),
        compiler_params=pltpu.CompilerParams(vmem_limit_bytes=60 * 2**20),
    )(grouped, w)


def out_project_kernel(half, place_ref, grp_ref, far_ref, near_ref, x_ref, gain_ref, mid_ref, sec_ref, held):
    size = far_ref.shape[0] // 4
    for b in range(8):
        other = place_ref[0] ^ order(b)
        rows = slice(b % 4 * size, (b % 4 + 1) * size)
        part = near_ref[rows, :] if b < 4 else dot(far_ref[rows, :], grp_ref[...], 1, 0)
        for z in range(size // half):
            start = pl.multiple_of((z * 8 + (other & 3) * 2 + (other >> 2)) * half, half)
            held[pl.ds(start, half), :] = part[z * half : (z + 1) * half, :]
    middle = x_ref[...] + held[...].T
    mid_ref[...] = middle
    sec_ref[...] = rms_norm(middle, gain_ref[...]).astype(BF)


def out_project(grouped, near, far, out_near, x, gain, place, lines, half):
    n = grouped.shape[1]
    if half % 16:
        w_out = join([near, far], place, lines, half)
        middle = x + dot(grouped, w_out, 0, 1)
        return middle, rms_norm(middle, gain).astype(BF)
    whole = lambda shape: pl.BlockSpec(shape, lambda t: (0, 0))
    return pl.pallas_call(
        functools.partial(out_project_kernel, half),
        cost_estimate=cost(0),
        grid=(1,),
        in_specs=[
            pl.BlockSpec(memory_space=pltpu.SMEM),
            whole((D, n)), whole(far.shape), whole(out_near.shape), whole((n, D)), whole((1, D)),
        ],
        out_specs=[whole((n, D)), whole((n, D))],
        out_shape=[jax.ShapeDtypeStruct((n, D), F32), jax.ShapeDtypeStruct((n, D), BF)],
        scratch_shapes=[pltpu.VMEM((D, n), F32)],
        compiler_params=pltpu.CompilerParams(vmem_limit_bytes=60 * 2**20),
    )(place.reshape(1), grouped, far, out_near, x, gain.reshape(1, D))


def back_middle_kernel(
    a_ref, f_ref, sx_ref, sy_ref, mid_ref, dy_ref, gain_ref, w_ref, dm_ref, branch_ref, dgrp_ref, dgain_ref
):
    d_second = sum(r[...].astype(F32) for r in (a_ref, f_ref, sx_ref, sy_ref))
    d_norm, dgain = rms_back(mid_ref[...], gain_ref[...], d_second)
    d_middle = dy_ref[...] + d_norm
    dm_ref[...] = d_middle
    branch = d_middle.astype(BF)
    branch_ref[...] = branch
    dgain_ref[...] = dgain[None]
    dgrp_ref[...] = dot(branch, w_ref[...], 1, 0).T


def back_middle(own, far, along_x, along_y, middle, out_grad, gain, w_out):
    n = middle.shape[0]
    block = pl.BlockSpec((n, D), lambda t: (0, 0))
    whole = lambda shape: pl.BlockSpec(shape, lambda t: (0, 0))
    return pl.pallas_call(
        back_middle_kernel,
        cost_estimate=cost(6),
        grid=(1,),
        in_specs=[block] * 6 + [whole((1, D)), whole((D, D))],
        out_specs=[block, block, whole((D, n)), whole((1, D))],
        out_shape=[
            jax.ShapeDtypeStruct((n, D), F32), jax.ShapeDtypeStruct((n, D), BF),
            jax.ShapeDtypeStruct((D, n), F32), jax.ShapeDtypeStruct((1, D), F32),
        ],
        compiler_params=pltpu.CompilerParams(vmem_limit_bytes=60 * 2**20),
    )(own, far, along_x, along_y, middle, out_grad, gain.reshape(1, D), w_out)


def out_grad_kernel(place_ref, branch_ref, grouped_ref, *refs):
    *outs, far_ref, held = refs
    wide, half = held.shape[0], held.shape[0] // 8
    size = outs[0].shape[0]
    lines = size // half
    for z in range(lines):
        held[...] = dot(branch_ref[:, z * wide : (z + 1) * wide], grouped_ref[...], 0, 1)
        for b in range(8):
            other = place_ref[0] ^ order(b)
            start = pl.multiple_of((other & 3) * 2 * half + (other >> 2) * half, half)
            ref, first = (outs[b], 0) if b < 4 else (far_ref, (b - 4) * size)
            ref[first + z * half : first + (z + 1) * half, :] = held[pl.ds(start, half), :].astype(BF)


def out_weight_grad(branch, grouped, place, lines, half):
    n = branch.shape[0]
    if half % 16:
        full = dot(branch, grouped, 0, 1).reshape(lines, 4, 2, half, D)
        blocks = []
        for b in range(8):
            other = place ^ order(b)
            block = lax.dynamic_slice(full, (0, other & 3, other >> 2, 0, 0), (lines, 1, 1, half, D))
            blocks.append(block.reshape(lines * half, D).astype(BF))
        return blocks[:4] + [jnp.concatenate(blocks[4:], axis=0)]
    return pl.pallas_call(
        out_grad_kernel,
        cost_estimate=cost(0),
        grid=(1,),
        in_specs=[
            pl.BlockSpec(memory_space=pltpu.SMEM),
            pl.BlockSpec((n, D), lambda t: (0, 0)),
            pl.BlockSpec((D, n), lambda t: (0, 0)),
        ],
        out_specs=[pl.BlockSpec((c * lines * half, D), lambda t: (0, 0)) for c in (1, 1, 1, 1, 4)],
        out_shape=[
            jax.ShapeDtypeStruct((c * lines * half, D), BF) for c in (1, 1, 1, 1, 4)
        ],
        scratch_shapes=[pltpu.VMEM((8 * half, D), F32)],
        compiler_params=pltpu.CompilerParams(vmem_limit_bytes=60 * 2**20),
    )(place.reshape(1), branch, grouped)


def join(values, place, lines, cols):
    count, n = 8 // len(values), values[0].shape[1]
    if cols % 16 == 0:
        return move(True, values, place, lines, cols, n, count).reshape(-1, n)
    out = jnp.zeros((lines, 4, 2, cols, n), BF)
    for b in range(8):
        source = place ^ order(b)
        block = values[b // count].reshape(count, lines, 1, 1, cols, n)[b % count]
        out = lax.dynamic_update_slice(out, block, (0, source & 3, source >> 2, 0, 0))
    return out.reshape(-1, n)


def cut(value, place, lines, cols):
    n = value.shape[1]
    value = value.reshape(lines, 4, 2, cols, n)
    if cols % 16 == 0:
        return move(False, [value], place, lines, cols, n, 1)
    pieces = []
    for b in range(8):
        target = place ^ order(b)
        piece = lax.dynamic_slice(value, (0, target & 3, target >> 2, 0, 0), (lines, 1, 1, cols, n))
        pieces.append(piece.reshape(lines * cols, n))
    return pieces


def order(b):
    return (b // 2 % 2) * 4 + (b % 2) * 2 + b // 4


def gated(gate, upper, d_hidden):
    sig = 1.0 / (1.0 + jnp.exp(-gate))
    act = gate * sig
    hidden = (act * upper).astype(BF)
    d_gate = (d_hidden * upper * (sig * (1.0 + gate * (1.0 - sig)))).astype(BF)
    return hidden, d_gate, (d_hidden * act).astype(BF)


def ffn_kernel(counts, *refs):
    runs = len(counts)
    w_ref, hid_ref, dgu_ref, *sums = refs[2 * runs : -2]
    t, ends = pl.program_id(0), [sum(counts[: r + 1]) for r in range(runs)]

    for r in range(runs if runs > 1 else 0):

        @pl.when((t >= ends[r] - counts[r]) & (t < ends[r]))
        def _():
            refs[-2][...] = refs[r][...]
            refs[-1][...] = refs[runs + r][...]

    lines, wide = w_ref.shape[0], w_ref.shape[1] // 3
    w_gu = w_ref[:, : 2 * wide, :].reshape(-1, D)
    w_down = w_ref[:, 2 * wide :, :].reshape(-1, D)
    s, o = (refs[-2][...], refs[-1][...]) if runs > 1 else (refs[0][...], refs[1][...])
    gu = dot(s, w_gu, 1, 1)
    dh = dot(o, w_down, 1, 1)
    for z in range(lines):
        lo, mid, hi = 2 * z * wide, (2 * z + 1) * wide, (2 * z + 2) * wide
        cut_h = slice(z * wide, (z + 1) * wide)
        hidden, d_gate, d_up = gated(gu[:, lo:mid], gu[:, mid:hi], dh[:, cut_h])
        hid_ref[:, cut_h] = hidden
        dgu_ref[:, lo:mid] = d_gate
        dgu_ref[:, mid:hi] = d_up
    ds = dot(dgu_ref[...], w_gu, 1, 0).astype(BF)
    yo = dot(hid_ref[...], w_down, 1, 0).astype(BF)
    for r in range(runs):

        @pl.when((t >= ends[r] - counts[r]) & (t < ends[r]))
        def _():
            sums[2 * r][...] = ds
            sums[2 * r + 1][...] = yo


def ffn(sources, w_ffn, n, time):
    counts = [count for _, _, _, _, count in sources]
    rows, lines, wide = sum(counts) * n, w_ffn.shape[0], w_ffn.shape[1] // 3
    if wide % 128:
        second, d_ffn = (
            jnp.concatenate([src[i][src[2 + i] * n : (src[2 + i] + src[4]) * n] for src in sources], axis=0)
            for i in range(2)
        )
        w_gu = w_ffn[:, : 2 * wide].reshape(-1, D)
        w_down = w_ffn[:, 2 * wide :].reshape(-1, D)
        gu = dot(second, w_gu, 1, 1).reshape(rows, lines, 2, wide)
        dh = dot(d_ffn, w_down, 1, 1).reshape(rows, lines, wide)
        hidden, d_gate, d_up = gated(gu[:, :, 0], gu[:, :, 1], dh)
        hidden = hidden.reshape(rows, lines * wide)
        d_gu = jnp.stack([d_gate, d_up], axis=2).reshape(rows, 2 * lines * wide)
        ds, yo = dot(d_gu, w_gu, 1, 0).astype(BF), dot(hidden, w_down, 1, 0).astype(BF)
        at, sums = 0, []
        for count in counts:
            sums += [v[at : at + count * n] for v in (ds, yo)]
            at += count * n
        return [hidden, d_gu] + sums

    def spec(part, first):
        start, count = sum(counts[:part]), counts[part]
        return pl.BlockSpec((n, D), lambda t: (jnp.clip(t - start, 0, count - 1) + first, 0))

    out = lambda width: pl.BlockSpec((n, width), lambda t: (t, 0))
    return pl.pallas_call(
        functools.partial(ffn_kernel, counts),
        cost_estimate=cost(time),
        grid=(rows // n,),
        in_specs=[spec(p, src[2 + i]) for i in range(2) for p, src in enumerate(sources)]
        + [pl.BlockSpec(memory_space=pltpu.VMEM)],
        out_specs=[out(lines * wide), out(2 * lines * wide)]
        + [spec(p, 0) for p in range(len(sources)) for _ in range(2)],
        out_shape=[
            jax.ShapeDtypeStruct((rows, lines * wide), BF),
            jax.ShapeDtypeStruct((rows, 2 * lines * wide), BF),
        ]
        + [jax.ShapeDtypeStruct((src[4] * n, D), BF) for src in sources for _ in range(2)],
        scratch_shapes=[pltpu.VMEM((n, D), BF)] * 2,
        compiler_params=pltpu.CompilerParams(vmem_limit_bytes=58 * 2**20),
    )(*(src[i] for i in range(2) for src in sources), w_ffn)


def ffn_grad_kernel(runs, *refs):
    hid, dgu, sec, dff = (refs[i * runs : (i + 1) * runs] for i in range(4))
    out_ref, gu_ref, down_ref = refs[4 * runs :]

    @pl.when(pl.program_id(0) == 0)
    def _():
        start = 0
        for h, d in zip(hid, dgu):
            rows = h.shape[0]
            gu_ref[:, start : start + rows] = d[...].T
            down_ref[:, start : start + rows] = h[...].T
            start += rows

    lines, wide = out_ref.shape[0], out_ref.shape[1] // 3
    gu, down, start = 0.0, 0.0, 0
    for a, b in zip(sec, dff):
        rows = slice(start, start + a.shape[0])
        gu = gu + dot(gu_ref[:, rows], a[...], 1, 0)
        down = down + dot(down_ref[:, rows], b[...], 1, 0)
        start += a.shape[0]
    for z in range(lines):
        out_ref[z, : 2 * wide, :] = gu[2 * z * wide : 2 * (z + 1) * wide, :].astype(BF)
        out_ref[z, 2 * wide :, :] = down[z * wide : (z + 1) * wide, :].astype(BF)


def ffn_grad(hidden, d_gu, second, d_ffn, lines, wide):
    if wide % 128:
        rows = lambda group: [v[f * c : (f + 1) * c] for v, c, f in group]
        gu = sum(dot(a, b, 0, 0) for a, b in zip(rows(d_gu), rows(second))).reshape(lines, 2 * wide, D)
        down = sum(dot(a, b, 0, 0) for a, b in zip(rows(hidden), rows(d_ffn))).reshape(lines, wide, D)
        return jnp.concatenate([gu, down], axis=1).astype(BF)
    step = 256
    whole = [
        pl.BlockSpec((c, v.shape[1]), lambda t, f=f: (f, 0)) for v, c, f in (*hidden, *d_gu)
    ]
    slab = [pl.BlockSpec((c, step), lambda t, f=f: (f, t)) for _, c, f in (*second, *d_ffn)]
    out, tall = (lines, 3 * wide), sum(c for _, c, _ in hidden)
    return pl.pallas_call(
        functools.partial(ffn_grad_kernel, len(hidden)),
        cost_estimate=cost(14),
        grid=(D // step,),
        in_specs=whole + slab,
        out_specs=pl.BlockSpec(out + (step,), lambda t: (0, 0, t)),
        out_shape=jax.ShapeDtypeStruct(out + (D,), BF),
        scratch_shapes=[
            pltpu.VMEM((2 * lines * wide, tall), BF),
            pltpu.VMEM((lines * wide, tall), BF),
        ],
        compiler_params=pltpu.CompilerParams(vmem_limit_bytes=60 * 2**20),
    )(*(v for group in (hidden, d_gu, second, d_ffn) for v, _, _ in group))


def qkv_grad_kernel(count, *refs):
    parts, (near_ref, far_ref, out_ref, held) = refs[:count], refs[count:]
    n = parts[0].shape[1]

    @pl.when(pl.program_id(0) == 0)
    def _():
        for b, part in enumerate(parts):
            held[:, b * n : (b + 1) * n] = part[...]

    rows = near_ref.shape[0]
    out_ref[...] = (
        dot(held[:, :rows], near_ref[...], 1, 0) + dot(held[:, rows:], far_ref[...], 1, 0)
    ).astype(BF)


def qkv_grad(parts, near, far, cols):
    rows, n = parts[0].shape
    if cols % 16:
        half = len(parts) // 2
        grads = (jnp.concatenate(p, axis=1) for p in (parts[:half], parts[half:]))
        return sum(dot(g, v, 1, 0) for g, v in zip(grads, (near, far))).astype(BF)
    step = 256
    slab = pl.BlockSpec((near.shape[0], step), lambda t: (0, t))
    return pl.pallas_call(
        functools.partial(qkv_grad_kernel, len(parts)),
        cost_estimate=cost(6),
        grid=(D // step,),
        in_specs=[pl.BlockSpec((rows, n), lambda t: (0, 0))] * len(parts) + [slab, slab],
        out_specs=pl.BlockSpec((rows, step), lambda t: (0, t)),
        out_shape=jax.ShapeDtypeStruct((rows, D), BF),
        scratch_shapes=[pltpu.VMEM((rows, len(parts) * n), BF)],
        compiler_params=pltpu.CompilerParams(vmem_limit_bytes=60 * 2**20),
    )(*parts, near, far)


def normed_back_kernel(*refs):
    count = len(refs) // 2
    refs[-1][...] = sum(dot(p[...], w[...], 0, 0) for p, w in zip(refs[:count], refs[count:-1]))


def normed_back(parts, weights):
    vmem = pl.BlockSpec(memory_space=pltpu.VMEM)
    return pl.pallas_call(
        normed_back_kernel,
        cost_estimate=cost(1),
        in_specs=[vmem] * (2 * len(parts)),
        out_specs=vmem,
        out_shape=jax.ShapeDtypeStruct((parts[0].shape[1], D), F32),
        compiler_params=pltpu.CompilerParams(vmem_limit_bytes=60 * 2**20),
    )(*parts, *weights)


def input_back_kernel(*refs):
    p_ref, p2_ref, w_ref, w2_ref, before_ref, x_ref, dm_ref, gain_ref, out_ref, dgain_ref = refs
    d_normed = before_ref[...] + dot(p_ref[...], w_ref[...], 0, 0) + dot(p2_ref[...], w2_ref[...], 0, 0)
    d_in, dgain = rms_back(x_ref[...].astype(F32), gain_ref[...], d_normed)
    out_ref[...] = dm_ref[...] + d_in
    dgain_ref[...] = dgain[None]


def input_back(parts, weights, before, x, d_middle, gain):
    vmem = pl.BlockSpec(memory_space=pltpu.VMEM)
    return pl.pallas_call(
        input_back_kernel,
        cost_estimate=cost(5),
        in_specs=[vmem] * 8,
        out_specs=[vmem] * 2,
        out_shape=[jax.ShapeDtypeStruct(x.shape, F32), jax.ShapeDtypeStruct((1, D), F32)],
        compiler_params=pltpu.CompilerParams(vmem_limit_bytes=60 * 2**20),
    )(*parts, *weights, before, x, d_middle, gain.reshape(1, D))


def doc_masks(drow_ref, dcol_ref, allow_ref, same_ref):
    n = allow_ref.shape[0]
    row = lax.broadcasted_iota(jnp.int32, (n, n), 0)
    col = lax.broadcasted_iota(jnp.int32, (n, n), 1)
    same = dcol_ref[...] == drow_ref[...]
    same_ref[...] = jnp.where(same, 1.0, 0.0)
    allow_ref[...] = jnp.where(same & (col <= row), 1.0, 0.0)


def attend_kernel(
    mix_ref, q_ref, k_ref, v_ref, th_ref, tl_ref, drow_ref, dcol_ref, gain_ref, *refs
):
    prob_ref, att_ref, grp_ref, allow_ref, same_ref, pad_ref, xh_ref, xl_ref = refs[-8:]
    g = pl.program_id(0)
    n = q_ref.shape[1]

    @pl.when(g == 0)
    def _():
        doc_masks(drow_ref, dcol_ref, allow_ref, same_ref)
        pad_ref[:, 0:8, :] = jnp.zeros((2, 8, n), F32)

    for e in range(2):
        q = q_ref[e * HD : (e + 1) * HD, :]
        k = k_ref[e * HD : (e + 1) * HD, :]
        logits = dot(q, k, 0, 0) * (HD ** (-0.5))
        pad_ref[e, 8 : 8 + n, :] = jnp.where(allow_ref[...] > 0, logits, 0.0)
        for a in range(CQ):
            part = jnp.where(same_ref[...] > 0, pad_ref[e, 8 - a : 8 - a + n, :], 0.0)
            hi, lo = split(part)
            xh_ref[e, :, a * n : (a + 1) * n] = hi
            xl_ref[e, :, a * n : (a + 1) * n] = lo
        conv = (
            dot(xh_ref[e], th_ref[e], 1, 0)
            + dot(xh_ref[e], tl_ref[e], 1, 0)
            + dot(xl_ref[e], th_ref[e], 1, 0)
        )
        scores = jnp.where(allow_ref[...] > 0, conv, NEG)
        weights = jnp.exp(scores - jnp.max(scores, axis=1, keepdims=True))
        prob_ref[e] = weights * (1.0 / jnp.sum(weights, axis=1, keepdims=True))
    for c in range(2):
        mixed = (mix_ref[g, 2 * c] * prob_ref[0] + mix_ref[g, 2 * c + 1] * prob_ref[1]).astype(BF)
        att = dot(v_ref[c * HD : (c + 1) * HD, :], mixed, 1, 1)
        att_ref[c * HD : (c + 1) * HD, :] = att
        centre = att - jnp.mean(att, axis=0, keepdims=True)
        spread = jnp.mean(centre * centre, axis=0, keepdims=True)
        grp_ref[c * HD : (c + 1) * HD, :] = (
            centre * lax.rsqrt(spread + 1e-05) * gain_ref[c * HD : (c + 1) * HD, :]
        ).astype(BF)


def attend(packed_t, docs, th, tl, mix, gain, start, count, before=()):
    n = packed_t.shape[1]
    blk = lambda off: pl.BlockSpec((PW, n), lambda g: (g + off, 0))
    tap = pl.BlockSpec((2, CQ * n, n), lambda g: (g + start, 0, 0))
    whole = lambda s: pl.BlockSpec(s, lambda g: (0, 0))
    return pl.pallas_call(
        attend_kernel,
        cost_estimate=cost(0),
        grid=(count,),
        in_specs=[
            pl.BlockSpec(memory_space=pltpu.SMEM),
            blk(start), blk(PAIRS + start), blk(2 * PAIRS + start), tap, tap,
            whole((1, n)), whole((n, 1)),
            pl.BlockSpec((PW, 1), lambda g: (g + start, 0)),
        ]
        + [pl.BlockSpec(memory_space=pl.ANY)] * len(before),
        out_specs=[pl.BlockSpec((2, n, n), lambda g: (g, 0, 0)), blk(0), blk(start)],
        out_shape=[
            jax.ShapeDtypeStruct((2 * count, n, n), F32),
            jax.ShapeDtypeStruct((count * PW, n), F32),
            jax.ShapeDtypeStruct((D, n), BF),
        ],
        input_output_aliases={9: 2} if before else {},
        scratch_shapes=[
            pltpu.VMEM((n, n), F32), pltpu.VMEM((n, n), F32), pltpu.VMEM((2, n + 8, n), F32),
            pltpu.VMEM((2, n, CQ * n), BF), pltpu.VMEM((2, n, CQ * n), BF),
        ],
        compiler_params=pltpu.CompilerParams(vmem_limit_bytes=60 * 2**20),
    )(
        mix[start : start + count].reshape(count, 4), packed_t, packed_t, packed_t, th, tl,
        docs.reshape(1, n), docs.reshape(n, 1), gain, *before,
    )


def attend_back_kernel(
    mix_ref, q_ref, k_ref, v_ref, tt_ref, drow_ref, dcol_ref, gain_ref, prob_ref, att_ref, dgrp_ref,
    d_ref, dgain_ref, dtap_ref, dmix_ref,
    allow_ref, same_ref, pad_ref, y_ref, dm_ref,
):
    g = pl.program_id(0)
    n = q_ref.shape[1]
    scale = HD ** (-0.5)

    @pl.when(g == 0)
    def _():
        doc_masks(drow_ref, dcol_ref, allow_ref, same_ref)
        pad_ref[:, n : n + 8, :] = jnp.zeros((2, 8, n), F32)

    for c in range(2):
        rows = slice(c * HD, (c + 1) * HD)
        att = att_ref[rows, :]
        centre = att - jnp.mean(att, axis=0, keepdims=True)
        rstd = lax.rsqrt(jnp.mean(centre * centre, axis=0, keepdims=True) + 1e-05)
        hat = centre * rstd
        dgrp = dgrp_ref[rows, :]
        dgain_ref[rows, :] = jnp.sum(dgrp * hat, axis=1, keepdims=True)
        dhat = dgrp * gain_ref[rows, :]
        datt = rstd * (
            dhat
            - jnp.mean(dhat, axis=0, keepdims=True)
            - hat * jnp.mean(dhat * hat, axis=0, keepdims=True)
        )
        datt = datt.astype(BF)
        mixed = (mix_ref[g, 2 * c] * prob_ref[0] + mix_ref[g, 2 * c + 1] * prob_ref[1]).astype(BF)
        d_ref[2, rows, :] = dot(datt, mixed, 1, 0).astype(BF)
        dmixed = dot(datt, v_ref[rows, :], 0, 0)
        dm_ref[c] = dmixed
        for e in range(2):
            dmix_ref[0, 2 * c + e : 2 * c + e + 1, :] = jnp.sum(dmixed * prob_ref[e], axis=0, keepdims=True)
    dmix_ref[0, 4:8, :] = jnp.zeros((4, n), F32)
    row = lax.broadcasted_iota(jnp.int32, (128, 128), 0)
    col = lax.broadcasted_iota(jnp.int32, (128, 128), 1)
    off = col - row
    half = CK // 2
    for e in range(2):
        rows = slice(e * HD, (e + 1) * HD)
        q = q_ref[rows, :]
        k = k_ref[rows, :]
        allowed = allow_ref[...] > 0
        masked_t = dot(k, q, 0, 0) * scale
        prob = prob_ref[e]
        dprob = mix_ref[g, e] * dm_ref[0] + mix_ref[g, 2 + e] * dm_ref[1]
        pad_ref[e, 0:n, :] = prob * (dprob - jnp.sum(prob * dprob, axis=1, keepdims=True))
        for a in range(CQ):
            y_ref[e, :, a * n : (a + 1) * n] = jnp.where(same_ref[...] > 0, pad_ref[e, a : a + n, :], 0.0).astype(BF)
        dlog = jnp.where(allowed, dot(y_ref[e], tt_ref[e], 1, 0), 0.0).astype(BF)
        d_ref[0, rows, :] = (dot(k, dlog, 1, 1) * scale).astype(BF)
        d_ref[1, rows, :] = (dot(q, dlog, 1, 0) * scale).astype(BF)
        krow = lax.broadcasted_iota(jnp.int32, (n, n), 0)
        qcol = lax.broadcasted_iota(jnp.int32, (n, n), 1)
        masked_t = jnp.where((same_ref[...] > 0) & (krow <= qcol), masked_t, 0.0).astype(BF)
        for a in range(CQ):
            full = dot(masked_t, y_ref[e, :, a * n : (a + 1) * n], 1, 0)
            fold = jnp.zeros((128, 128), F32)
            blocks = n // 128
            for r in range(blocks):
                fold = fold + full[r * 128 : (r + 1) * 128, r * 128 : (r + 1) * 128]
            fold = jnp.where(jnp.abs(off) <= half, fold, 0.0)
            for r in range(blocks - 1):
                up = full[r * 128 : (r + 1) * 128, (r + 1) * 128 : (r + 2) * 128]
                down = full[(r + 1) * 128 : (r + 2) * 128, r * 128 : (r + 1) * 128]
                fold = fold + jnp.where(off <= half - 128, up, 0.0) + jnp.where(off >= 128 - half, down, 0.0)
            lined = fold[0:8, :]
            for t in range(1, 16):
                lined = lined + pltpu.roll(fold[8 * t : 8 * t + 8, :], 128 - 8 * t, 1)
            dtap_ref[e, 8 * a : 8 * a + 8, :] = lined


def attend_back(packed_t, docs, tt, mix, gain, prob, att, dgrp):
    n = packed_t.shape[1]
    blk = lambda off: pl.BlockSpec((PW, n), lambda g: (g + off, 0))
    whole = lambda s: pl.BlockSpec(s, lambda g: (0, 0))
    thin = pl.BlockSpec((PW, 1), lambda g: (g, 0))
    return pl.pallas_call(
        attend_back_kernel,
        cost_estimate=cost(24),
        grid=(PAIRS,),
        in_specs=[
            pl.BlockSpec(memory_space=pltpu.SMEM),
            blk(0), blk(PAIRS), blk(2 * PAIRS),
            pl.BlockSpec((2, CQ * n, n), lambda g: (g, 0, 0)),
            whole((1, n)), whole((n, 1)), thin,
            pl.BlockSpec((2, n, n), lambda g: (g, 0, 0)),
            blk(0), blk(0),
        ],
        out_specs=[
            pl.BlockSpec((3, PW, n), lambda g: (0, g, 0)), thin,
            pl.BlockSpec((2, 8 * CQ, 128), lambda g: (g, 0, 0)),
            pl.BlockSpec((1, 8, n), lambda g: (g, 0, 0)),
        ],
        out_shape=[
            jax.ShapeDtypeStruct((3, D, n), BF),
            jax.ShapeDtypeStruct((D, 1), F32),
            jax.ShapeDtypeStruct((H, 8 * CQ, 128), F32),
            jax.ShapeDtypeStruct((PAIRS, 8, n), F32),
        ],
        scratch_shapes=[
            pltpu.VMEM((n, n), F32), pltpu.VMEM((n, n), F32), pltpu.VMEM((2, n + 8, n), F32),
            pltpu.VMEM((2, n, CQ * n), BF), pltpu.VMEM((2, n, n), F32),
        ],
        compiler_params=pltpu.CompilerParams(vmem_limit_bytes=60 * 2**20),
    )(
        mix.reshape(PAIRS, 4), packed_t, packed_t, packed_t, tt,
        docs.reshape(1, n), docs.reshape(n, 1), gain, prob, att, dgrp,
    )


def fold_sums(dgain, dtap, dmix):
    lane = jnp.arange(128)[None, None, :] - jnp.arange(8)[None, :, None]
    tap = jnp.arange(CK)[:, None, None] - CK // 2
    pick = (jnp.remainder(lane - tap, 128) == 0).astype(F32)
    dtap = jnp.sum(dtap.reshape(H, CQ, 1, 8, 128) * pick, axis=(3, 4))
    dmix = jnp.sum(dmix[:, :4, :], axis=2)
    return jnp.concatenate([dgain[:, 0], dtap.reshape(-1), dmix.reshape(-1)])


def rms_norm(values, gain):
    return values * lax.rsqrt(jnp.mean(values * values, axis=-1, keepdims=True) + 1e-05) * gain


def rms_back(values, gain, grad):
    rstd = lax.rsqrt(jnp.mean(values * values, axis=-1, keepdims=True) + 1e-05)
    hat = values * rstd
    dhat = grad * gain
    dvalues = rstd * (dhat - hat * jnp.mean(dhat * hat, axis=-1, keepdims=True))
    return dvalues, jnp.sum(grad * hat, axis=0)


class Slice:
    def __init__(self, reps, shards):
        self.axes = ("rep", "fsdp")
        self.shards = shards
        self.lines = [[4 * o + i for o in range(shards // 4)] for i in range(4)]
        places = [(y, f) for y in range(reps) for f in range(shards)]

        def perm(move):
            out = []
            for y, f in places:
                to = move(y, f)
                out.append((y * shards + f, to[0] * shards + to[1]))
            return out

        self.hops = {
            (dy, di): perm(lambda y, f, dy=dy, di=di: (y ^ dy, f ^ di))
            for dy in range(2)
            for di in (range(16) if shards == 16 else range(4))
        }
        self.corner = perm(lambda y, f: (y, f ^ 2) if f & 1 else (1 - y, f))
        self.doubling = []
        bit = 1
        while bit < shards:
            self.doubling.append((bit, perm(lambda y, f, bit=bit: (y, f ^ bit))))
            bit *= 2
        self.rep = lax.axis_index("rep")
        self.fsdp = lax.axis_index("fsdp")
        self.odd = (self.fsdp & 1) == 1
        self.place = self.rep * 4 + (self.fsdp & 3)

    def hop(self, value, dy, di):
        return lax.ppermute(value, self.axes, self.hops[dy, di])

    def hop_block(self, value, b):
        return self.hop(value, order(b) >> 2, order(b) & 3) if b else value

    def gather_line(self, value):
        return lax.all_gather(value, "fsdp", axis=0, tiled=True, axis_index_groups=self.lines)

    def scatter_line(self, value):
        return lax.psum_scatter(
            value.astype(BF), "fsdp", scatter_dimension=0, tiled=True, axis_index_groups=self.lines
        )

    def gather_small(self, value):
        for bit, perm in self.doubling:
            other = lax.ppermute(value, self.axes, perm)
            high = (self.fsdp & bit) != 0
            value = jnp.concatenate(
                [jnp.where(high, other, value), jnp.where(high, value, other)], axis=0
            )
        return value

    def sides(self, value):
        return self.hop(value, 0, 2), self.hop(value, 1, 0)

    def far_corner(self, along_x, along_y):
        return lax.ppermute(jnp.where(self.odd, along_y, along_x), self.axes, self.corner)

    def near_blocks(self, value, along_x, along_y, corner):
        near = jnp.concatenate([value, along_x, along_y, jnp.zeros_like(value)], axis=0)
        return lax.dynamic_update_slice(near, corner, (3 * value.shape[0], 0))

    def scatter_corner(self, near, far):
        own, to_x, to_y, last = (a.astype(F32) + b.astype(F32) for a, b in zip(near, far))
        corner = lax.ppermute(last.astype(BF), self.axes, self.corner).astype(F32)
        to_x = (to_x + jnp.where(self.odd, 0.0, corner)).astype(BF)
        to_y = (to_y + jnp.where(self.odd, corner, 0.0)).astype(BF)
        return own, to_x, to_y

    def send_corner(self, near, far):
        return lax.ppermute((near.astype(F32) + far.astype(F32)).astype(BF), self.axes, self.corner)

    def with_corner(self, near, far, corner):
        corner = corner.astype(F32)
        to_x, to_y = (a.astype(F32) + b.astype(F32) for a, b in zip(near, far))
        to_x = (to_x + jnp.where(self.odd, 0.0, corner)).astype(BF)
        return to_x, (to_y + jnp.where(self.odd, corner, 0.0)).astype(BF)

    def scatter_last(self, own, to_x, to_y):
        return own + self.hop(to_x, 0, 2).astype(F32) + self.hop(to_y, 1, 0).astype(F32)

    def scatter_line_small(self, value):
        lines = self.shards // 4
        if lines != 4:
            return self.scatter_line(value).astype(F32)
        rows = value.shape[0] // lines
        value = value.astype(BF)
        line = self.fsdp // 4
        part = lambda d: lax.dynamic_slice_in_dim(value, (line ^ d) * rows, rows, axis=0)
        return sum([self.hop(part(d), 0, 4 * d).astype(F32) for d in range(1, 4)], part(0).astype(F32))

    def sum_small(self, value, bits):
        for bit, perm in self.doubling:
            if bit in bits:
                value = value + lax.ppermute(value, self.axes, perm)
        return value

    def both_halves(self, half, axis=0, other=None):
        if other is None:
            other = self.hop(half, 1, 0)
        first = self.rep == 0
        return jnp.concatenate(
            [jnp.where(first, half, other), jnp.where(first, other, half)], axis=axis
        ).astype(F32)

    def own_half(self, shard, rep=None):
        rows = shard.shape[0] // 2
        return lax.dynamic_slice_in_dim(shard, (self.rep if rep is None else rep) * rows, rows, axis=0)


def on_device(
    reps,
    shards,
    tokens,
    doc_ids,
    norm_gain,
    qkv_weight,
    group_gain,
    out_weight,
    ffn_gain,
    gate_weight,
    up_weight,
    down_weight,
    conv_kernel,
    head_mix,
    out_grad,
):
    net = Slice(reps, shards)
    lines = shards // 4
    n = tokens.shape[0]
    cols = 3 * D // shards // 2
    wide = gate_weight.shape[1] // 2

    half_out = D // shards // 2
    rows_of = lambda v: [v[b * n : (b + 1) * n] for b in range(v.shape[0] // n)]

    attn_half = jnp.concatenate([net.own_half(qkv_weight.T), net.own_half(out_weight.T)], axis=0)
    w_attn = net.gather_line(attn_half).reshape(lines, -1, D)
    ffn_half = jnp.concatenate(
        [net.own_half(v) for v in (gate_weight.T, up_weight.T, down_weight)], axis=0
    )
    w_ffn = net.gather_line(ffn_half).reshape(lines, -1, D)
    x_side = net.sides(tokens)
    d_low = out_grad.astype(BF)
    d_side = net.sides(d_low)
    taps = band_taps(conv_kernel, n)
    gains, *sides = fence(
        jnp.stack([norm_gain, group_gain, ffn_gain])[None], *x_side, *d_side, *taps
    )
    x_side, d_side, (taps_hi, taps_lo, taps_back) = sides[:2], sides[2:4], sides[4:]
    x_near = net.near_blocks(tokens, *x_side, net.far_corner(*x_side))
    x_far = net.hop(x_near, 0, 1)
    d_near = net.near_blocks(d_low, *d_side, net.far_corner(*d_side))
    gains = net.gather_small(gains)
    w_attn = fence(w_attn, time=100)[0]
    x_far = fence(x_far, time=40)[0]
    d_near = fence(d_near, time=60)[0]
    w_attn, d_near, x_far, gains = fence(w_attn, d_near, x_far, gains)
    gains = gains.transpose(1, 0, 2).reshape(3, D).astype(F32)
    w_cls = w_attn[:, cols:].reshape(-1, D)
    inputs = tokens.astype(F32)

    norm_near, parts = project(x_near, gains[0], w_attn, cols, n)
    norm_near, x_far, d_far, *parts = fence(norm_near, x_far, net.hop(d_near, 0, 1), *parts)
    norm_far, more = project(x_far, gains[0], w_attn, cols, n)
    pieces = [net.hop_block(p, b) for b, p in enumerate((*parts, *more))]
    pieces = fence(*pieces, time=45)
    w_qkv = w_attn[:, :cols].reshape(-1, D)
    *pieces, w_cls, d_far, w_qkv = fence(*pieces, w_cls, d_far, w_qkv)
    w_side = (*net.sides(w_cls), net.hop(w_cls, 1, 2))
    packed_t = join(pieces, net.place, lines, cols)
    group_col = gains[1].reshape(D, 1)
    *w_side, probs, attended, grouped = fence(
        *w_side,
        *attend(packed_t, doc_ids, taps_hi, taps_lo, head_mix, group_col, 0, PAIRS),
    )
    w_near = jnp.concatenate([w_cls, *w_side], axis=0)
    out_near, w_far = fence(out_blocks(grouped, w_near), net.hop(w_near, 0, 1))
    middle, second = out_project(
        grouped, w_near, w_far, out_near, inputs, gains[2], net.place, lines, half_out
    )
    w_near, w_far, second = fence(w_near, w_far, second)
    w_out = join([w_near, w_far], net.place, lines, half_out)
    *s_side, w_out = fence(*net.sides(second), w_out)
    s_corner = net.far_corner(*s_side)
    s_a = jnp.concatenate([second, s_side[0]], axis=0)
    far_a = net.hop(s_a, 0, 1)
    w_ffn = fence(w_ffn, time=40)[0]
    run_a = ffn([(s_a, d_near, 0, 0, 2)], w_ffn, n, 7)
    s_corner, far_a, w_qkv, *run_a = fence(s_corner, far_a, w_qkv, *run_a)
    w_side = net.sides(w_qkv)
    s_b = jnp.concatenate([s_side[1], s_corner], axis=0)
    far_b = net.hop(s_b, 0, 1)
    run_b = ffn([(s_b, d_near, 0, 2, 2)], w_ffn, n, 7)
    far_a, far_b, *run_b = fence(far_a, far_b, *run_b)
    run_f = ffn([(far_a, d_far, 0, 0, 2), (far_b, d_far, 0, 2, 2)], w_ffn, n, 2)
    ds_g, *w_side = fence(net.hop(run_f[4], 0, 1), *w_side)
    size_q = lines * cols // 2
    corner = net.send_corner(run_b[2][n:], ds_g[n:])
    ds_f, yo_f, yo_g = (net.hop(run_f[i], 0, 1) for i in (2, 3, 5))
    to_x, to_y = net.with_corner((run_a[2][n:], run_b[2][:n]), (ds_f[n:], ds_g[:n]), corner)
    last = (run_b[3][n:].astype(F32) + yo_g[n:].astype(F32)).astype(BF)
    to_x, to_y, last, *rest = fence(
        to_x, to_y, last, w_qkv, *w_side, w_side[1][:size_q], w_side[0][size_q:], *[r[i] for i in range(2) for r in (run_a, run_f, run_b)]
    )
    w_near, w_corner, acts = rest[:3], rest[3:5], rest[5:]
    w_far = [net.hop(w, 0, 1) for w in w_near]
    along_x, along_y = net.hop(to_x, 0, 2), net.hop(to_y, 1, 0)
    blocks = lambda a, f, b: [(a, 2 * n, 0), (f, 2 * n, 0), (f, 2 * n, 1), (b, 2 * n, 0)]
    g_ffn = ffn_grad(
        blocks(*acts[:3]),
        blocks(*acts[3:]),
        [(s_a, 2 * n, 0), (far_a, 2 * n, 0), (far_b, 2 * n, 0), (s_b, 2 * n, 0)],
        [(d_near, 2 * n, 0), (d_far, 2 * n, 0), (d_far, 2 * n, 1), (d_near, 2 * n, 1)],
        lines, wide,
    )
    along_x, along_y, last, g_ffn, *w_far = fence(along_x, along_y, last, g_ffn, *w_far)
    g_ffn = fence(net.scatter_line(g_ffn.reshape(-1, D)), time=80)[0]
    corner = lax.ppermute(last, net.axes, net.corner)
    d_middle, branch, d_grouped, g_ffn_gain = back_middle(
        run_a[2], ds_f, along_x, along_y, middle, out_grad, gains[2], w_out
    )
    d_grouped, *w_corner = fence(d_grouped, *w_corner)
    w_corner = (net.hop(w_corner[0], 0, 2), net.hop(w_corner[1], 1, 0))
    d_packed, g_group, g_taps, g_mix = attend_back(
        packed_t, doc_ids, taps_back, head_mix, group_col, probs, attended, d_grouped
    )
    d_packed, corner, *w_corner = fence(d_packed, corner, *w_corner)
    y_x, y_y = net.with_corner((run_a[3][n:], run_b[3][:n]), (yo_f[n:], yo_g[:n]), corner)
    w_near.append(jnp.concatenate(w_corner, axis=0))
    w_far.append(net.hop(w_near[3], 0, 1))
    pieces = cut(d_packed.reshape(3 * D, n), net.place, lines, cols)
    *cuts, branch = fence(*pieces, branch)
    pieces = [net.hop_block(p, b) for b, p in enumerate(cuts)]
    g_blocks = out_weight_grad(branch, grouped, net.place, lines, half_out)
    pieces = fence(*pieces, time=52)
    g_far, sums, w_near[3], w_far[3], y_x, y_y, *pieces = fence(
        net.hop(g_blocks[4], 0, 1), fold_sums(g_group, g_taps, g_mix), w_near[3], w_far[3], y_x, y_y, *pieces, *cuts
    )
    y_x, y_y = net.hop(y_x, 0, 2), net.hop(y_y, 1, 0)
    pieces, cuts = pieces[:8], pieces[8:]
    size = lines * half_out
    g_far = [g_far[b * size : (b + 1) * size] for b in range(4)]
    out_own, to_x, to_y = net.scatter_corner(g_blocks[:4], g_far)
    g_qkv, g_ffn, to_x, to_y, *cuts = fence(
        qkv_grad(pieces, norm_near, norm_far, cols), g_ffn, to_x, to_y, *cuts
    )
    g_qkv = fence(net.scatter_line(g_qkv), time=20)[0]
    g_other = net.hop(g_ffn, 1, 0)
    along_x, along_y = net.hop(to_x, 0, 2), net.hop(to_y, 1, 0)
    d_normed = normed_back([*cuts[:3], *cuts[4:7]], [*w_near[:3], *w_far[:3]])
    input_grad, g_norm = input_back([cuts[3], cuts[7]], [w_near[3], w_far[3]], d_normed, tokens, d_middle, gains[0])
    small = jnp.concatenate([g_norm[0], g_ffn_gain[0], sums])
    small = net.sum_small(small, [bit for bit, _ in net.doubling])
    g_other, y_x, y_y = fence(g_other, y_x, y_y, time=20)
    g_out = net.scatter_line_small(out_own + along_x.astype(F32) + along_y.astype(F32)).astype(BF)
    own = run_a[3][:n].astype(F32) + yo_f[:n].astype(F32)
    layer_out = (middle + (own + y_x.astype(F32) + y_y.astype(F32))).astype(BF)
    g_out, g_other, small, g_qkv = fence(g_out, g_other, small, g_qkv)
    q_other = net.hop(g_qkv, 1, 0)
    small = small + net.hop(small, 1, 0)
    g_out = net.both_halves(g_out).T
    shape = (3, wide, D)
    g_ffn = net.both_halves(g_ffn.reshape(shape), 1, g_other.reshape(shape))
    g_gate, g_up, g_down = g_ffn[0].T, g_ffn[1].T, g_ffn[2]
    g_qkv = net.both_halves(g_qkv, 0, q_other).T

    part = D // shards
    gain_grads = [
        lax.dynamic_slice_in_dim(small, b * D + net.fsdp * part, part) for b in (0, 2, 1)
    ]
    g_taps = small[3 * D : 3 * D + H * CQ * CK].reshape(H, CQ * CK)
    g_mix = small[3 * D + H * CQ * CK :].reshape(PAIRS, 2, 2)
    return (
        layer_out,
        input_grad,
        gain_grads[0],
        g_qkv,
        gain_grads[1],
        g_out,
        gain_grads[2],
        g_gate,
        g_up,
        g_down,
        g_taps,
        g_mix,
    )


def solution(mesh):
    placed = (
        P(("rep", "fsdp"), None),
        P(("rep", "fsdp")),
        P("fsdp"),
        P(None, "fsdp"),
        P("fsdp"),
        P(None, "fsdp"),
        P("fsdp"),
        P(None, "fsdp"),
        P(None, "fsdp"),
        P("fsdp", None),
        P(),
        P(),
        P(("rep", "fsdp"), None),
    )
    return jax.shard_map(
        functools.partial(on_device, mesh.shape["rep"], mesh.shape["fsdp"]),
        mesh=mesh,
        in_specs=placed,
        out_specs=(
            P(("rep", "fsdp"), None),
            P(("rep", "fsdp"), None),
            P("fsdp"),
            P(None, "fsdp"),
            P("fsdp"),
            P(None, "fsdp"),
            P("fsdp"),
            P(None, "fsdp"),
            P(None, "fsdp"),
            P("fsdp", None),
            P(),
            P(),
        ),
        check_vma=False,
    )
```

```python
import functools
import jax
import jax.numpy as jnp
from jax import lax
from jax.experimental import pallas as pl
from jax.experimental.pallas import tpu as pltpu
from jax.sharding import PartitionSpec as P

D = 1536
H = 16
HD = 96
CQ = 6
CK = 11
NEG = -1e30
PAIRS = H // 2
PW = 2 * HD
BF = jnp.bfloat16
F32 = jnp.float32


def cost(time):
    return pl.CostEstimate(flops=int(time * 5e8), bytes_accessed=0, transcendentals=0)


def dot(a, b, ca, cb):
    return lax.dot_general(a, b, (((ca,), (cb,)), ((), ())), preferred_element_type=F32)


def split(v):
    hi = v.astype(BF)
    return hi, (v - hi.astype(F32)).astype(BF)


def taps_kernel(fwd_ref, bwd_ref, th_ref, tl_ref, tt_ref):
    n = th_ref.shape[-1]
    row = lax.broadcasted_iota(jnp.int32, (n, n), 0)
    col = lax.broadcasted_iota(jnp.int32, (n, n), 1)
    near = jnp.abs(row - col) <= CK // 2
    for a in range(CQ):
        wide = jnp.broadcast_to(fwd_ref[0, a : a + 1, :], (n, n))
        band = jnp.where(near, pltpu.roll(wide, 0, 1, stride=1, stride_axis=0), 0.0)
        hi, lo = split(band)
        th_ref[0, a * n : (a + 1) * n, :] = hi
        tl_ref[0, a * n : (a + 1) * n, :] = lo
        wide = jnp.broadcast_to(bwd_ref[0, a : a + 1, :], (n, n))
        band = jnp.where(near, pltpu.roll(wide, 0, 1, stride=1, stride_axis=0), 0.0)
        tt_ref[0, a * n : (a + 1) * n, :] = band.astype(BF)


def band_taps(kernel, n):
    half = CK // 2

    def around(taps):
        gap = jnp.zeros((H, CQ, n - CK), F32)
        rows = jnp.concatenate([taps[:, :, half:], gap, taps[:, :, :half]], axis=2)
        return jnp.pad(rows, ((0, 0), (0, 8 - CQ), (0, 0)))

    taps = kernel.reshape(H, CQ, CK)
    fwd, bwd = around(taps), around(taps[:, :, ::-1])
    row = pl.BlockSpec((1, 8, n), lambda h: (h, 0, 0))
    out = pl.BlockSpec((1, CQ * n, n), lambda h: (h, 0, 0))
    shape = jax.ShapeDtypeStruct((H, CQ * n, n), BF)
    return pl.pallas_call(
        taps_kernel,
        cost_estimate=cost(16),
        grid=(H,),
        in_specs=[row, row],
        out_specs=[out, out, out],
        out_shape=[shape, shape, shape],
    )(fwd, bwd)


def fence_kernel(*refs):
    del refs


def fence(*values, time=0.1):
    return pl.pallas_call(
        fence_kernel,
        cost_estimate=cost(time),
        in_specs=[pl.BlockSpec(memory_space=pl.ANY)] * len(values),
        out_specs=[pl.BlockSpec(memory_space=pl.ANY)] * len(values),
        out_shape=[jax.ShapeDtypeStruct(v.shape, v.dtype) for v in values],
        input_output_aliases={i: i for i in range(len(values))},
    )(*values)


def project_kernel(x_ref, gain_ref, w_ref, normed_ref, *part_refs):
    cols = part_refs[0].shape[0] // w_ref.shape[0]
    x = x_ref[...].astype(F32)
    normed = rms_norm(x, gain_ref[...]).astype(BF)
    normed_ref[...] = normed
    w = w_ref[:, :cols, :].reshape(-1, D)
    part = dot(w, normed, 1, 1).astype(BF)
    for b, ref in enumerate(part_refs):

        @pl.when(pl.program_id(0) == b)
        def _():
            ref[...] = part


def project(blocks, gain, w_attn, cols, n):
    lines, count = w_attn.shape[0], blocks.shape[0] // n
    rows = lines * cols
    if cols % 16:
        normed = rms_norm(blocks.astype(F32), gain).astype(BF)
        part = dot(w_attn[:, :cols].reshape(rows, D), normed, 1, 1).astype(BF)
        return normed, [part[:, b * n : (b + 1) * n] for b in range(count)]
    out = pl.pallas_call(
        project_kernel,
        cost_estimate=cost(0),
        grid=(count,),
        in_specs=[
            pl.BlockSpec((n, D), lambda b: (b, 0)),
            pl.BlockSpec((1, D), lambda b: (0, 0)),
            pl.BlockSpec(w_attn.shape, lambda b: (0, 0, 0)),
        ],
        out_specs=[pl.BlockSpec((n, D), lambda b: (b, 0))]
        + [pl.BlockSpec((rows, n), lambda b: (0, 0))] * count,
        out_shape=[jax.ShapeDtypeStruct(blocks.shape, BF)]
        + [jax.ShapeDtypeStruct((rows, n), BF)] * count,
        compiler_params=pltpu.CompilerParams(vmem_limit_bytes=60 * 2**20),
    )(blocks, gain.reshape(1, D), w_attn)
    return out[0], out[1:]


def move_kernel(joins, count, cols, place_ref, *refs):
    *arrays, sems = refs
    if joins:
        *blocks, held = arrays
    else:
        whole, *blocks, held, sem = arrays
        first = pltpu.make_async_copy(whole, held, sem)
        first.start()
        first.wait()
    lines = held.shape[0]
    rows = lines * cols
    copies = []
    for b in range(8):
        other = place_ref[0] ^ order(b)
        for z in range(lines):
            part = blocks[b // count].at[pl.ds(b % count * rows + z * cols, cols)]
            spot = held.at[z, other & 3, other >> 2]
            pair = (part, spot) if joins else (spot, part)
            copies.append(pltpu.make_async_copy(*pair, sems.at[len(copies)]))
            copies[-1].start()
    for copy in copies:
        copy.wait()


def move(joins, values, place, lines, cols, n, count):
    anywhere = pl.BlockSpec(memory_space=pl.ANY)
    whole = (lines, 4, 2, cols, n)
    held = [pltpu.VMEM(whole, BF), pltpu.SemaphoreType.DMA(())]
    if joins:
        out_specs = pl.BlockSpec(memory_space=pltpu.VMEM)
        shape = jax.ShapeDtypeStruct(whole, BF)
    else:
        out_specs = [anywhere] * (8 // count)
        shape = [jax.ShapeDtypeStruct((lines * cols * count, n), BF)] * (8 // count)
    return pl.pallas_call(
        functools.partial(move_kernel, joins, count, cols),
        cost_estimate=cost(2),
        in_specs=[pl.BlockSpec(memory_space=pltpu.SMEM)] + [anywhere] * len(values),
        out_specs=out_specs,
        out_shape=shape,
        scratch_shapes=([] if joins else held) + [pltpu.SemaphoreType.DMA((8 * lines,))],
        compiler_params=pltpu.CompilerParams(vmem_limit_bytes=60 * 2**20),
    )(place.reshape(1), *values)


def out_blocks_kernel(grp_ref, w_ref, out_ref):
    out_ref[...] = dot(w_ref[...], grp_ref[...], 1, 0)


def out_blocks(grouped, w):
    n = grouped.shape[1]
    return pl.pallas_call(
        out_blocks_kernel,
        cost_estimate=cost(0),
        out_shape=jax.ShapeDtypeStruct((w.shape[0], n), F32),
        compiler_params=pltpu.CompilerParams(vmem_limit_bytes=60 * 2**20),
    )(grouped, w)


def out_project_kernel(half, place_ref, grp_ref, far_ref, near_ref, x_ref, gain_ref, mid_ref, sec_ref, held):
    size = far_ref.shape[0] // 4
    for b in range(8):
        other = place_ref[0] ^ order(b)
        rows = slice(b % 4 * size, (b % 4 + 1) * size)
        part = near_ref[rows, :] if b < 4 else dot(far_ref[rows, :], grp_ref[...], 1, 0)
        for z in range(size // half):
            start = pl.multiple_of((z * 8 + (other & 3) * 2 + (other >> 2)) * half, half)
            held[pl.ds(start, half), :] = part[z * half : (z + 1) * half, :]
    middle = x_ref[...] + held[...].T
    mid_ref[...] = middle
    sec_ref[...] = rms_norm(middle, gain_ref[...]).astype(BF)


def out_project(grouped, near, far, out_near, x, gain, place, lines, half):
    n = grouped.shape[1]
    if half % 16:
        w_out = join([near, far], place, lines, half)
        middle = x + dot(grouped, w_out, 0, 1)
        return middle, rms_norm(middle, gain).astype(BF)
    whole = lambda shape: pl.BlockSpec(shape, lambda t: (0, 0))
    return pl.pallas_call(
        functools.partial(out_project_kernel, half),
        cost_estimate=cost(0),
        grid=(1,),
        in_specs=[
            pl.BlockSpec(memory_space=pltpu.SMEM),
            whole((D, n)), whole(far.shape), whole(out_near.shape), whole((n, D)), whole((1, D)),
        ],
        out_specs=[whole((n, D)), whole((n, D))],
        out_shape=[jax.ShapeDtypeStruct((n, D), F32), jax.ShapeDtypeStruct((n, D), BF)],
        scratch_shapes=[pltpu.VMEM((D, n), F32)],
        compiler_params=pltpu.CompilerParams(vmem_limit_bytes=60 * 2**20),
    )(place.reshape(1), grouped, far, out_near, x, gain.reshape(1, D))


def back_middle_kernel(
    a_ref, f_ref, sx_ref, sy_ref, mid_ref, dy_ref, gain_ref, w_ref, dm_ref, branch_ref, dgrp_ref, dgain_ref
):
    d_second = sum(r[...].astype(F32) for r in (a_ref, f_ref, sx_ref, sy_ref))
    d_norm, dgain = rms_back(mid_ref[...], gain_ref[...], d_second)
    d_middle = dy_ref[...] + d_norm
    dm_ref[...] = d_middle
    branch = d_middle.astype(BF)
    branch_ref[...] = branch
    dgain_ref[...] = dgain[None]
    dgrp_ref[...] = dot(branch, w_ref[...], 1, 0).T


def back_middle(own, far, along_x, along_y, middle, out_grad, gain, w_out):
    n = middle.shape[0]
    block = pl.BlockSpec((n, D), lambda t: (0, 0))
    whole = lambda shape: pl.BlockSpec(shape, lambda t: (0, 0))
    return pl.pallas_call(
        back_middle_kernel,
        cost_estimate=cost(6),
        grid=(1,),
        in_specs=[block] * 6 + [whole((1, D)), whole((D, D))],
        out_specs=[block, block, whole((D, n)), whole((1, D))],
        out_shape=[
            jax.ShapeDtypeStruct((n, D), F32), jax.ShapeDtypeStruct((n, D), BF),
            jax.ShapeDtypeStruct((D, n), F32), jax.ShapeDtypeStruct((1, D), F32),
        ],
        compiler_params=pltpu.CompilerParams(vmem_limit_bytes=60 * 2**20),
    )(own, far, along_x, along_y, middle, out_grad, gain.reshape(1, D), w_out)


def out_grad_kernel(place_ref, branch_ref, grouped_ref, *refs):
    *outs, far_ref, held = refs
    wide, half = held.shape[0], held.shape[0] // 8
    size = outs[0].shape[0]
    lines = size // half
    for z in range(lines):
        held[...] = dot(branch_ref[:, z * wide : (z + 1) * wide], grouped_ref[...], 0, 1)
        for b in range(8):
            other = place_ref[0] ^ order(b)
            start = pl.multiple_of((other & 3) * 2 * half + (other >> 2) * half, half)
            ref, first = (outs[b], 0) if b < 4 else (far_ref, (b - 4) * size)
            ref[first + z * half : first + (z + 1) * half, :] = held[pl.ds(start, half), :].astype(BF)


def out_weight_grad(branch, grouped, place, lines, half):
    n = branch.shape[0]
    if half % 16:
        full = dot(branch, grouped, 0, 1).reshape(lines, 4, 2, half, D)
        blocks = []
        for b in range(8):
            other = place ^ order(b)
            block = lax.dynamic_slice(full, (0, other & 3, other >> 2, 0, 0), (lines, 1, 1, half, D))
            blocks.append(block.reshape(lines * half, D).astype(BF))
        return blocks[:4] + [jnp.concatenate(blocks[4:], axis=0)]
    return pl.pallas_call(
        out_grad_kernel,
        cost_estimate=cost(0),
        grid=(1,),
        in_specs=[
            pl.BlockSpec(memory_space=pltpu.SMEM),
            pl.BlockSpec((n, D), lambda t: (0, 0)),
            pl.BlockSpec((D, n), lambda t: (0, 0)),
        ],
        out_specs=[pl.BlockSpec((c * lines * half, D), lambda t: (0, 0)) for c in (1, 1, 1, 1, 4)],
        out_shape=[
            jax.ShapeDtypeStruct((c * lines * half, D), BF) for c in (1, 1, 1, 1, 4)
        ],
        scratch_shapes=[pltpu.VMEM((8 * half, D), F32)],
        compiler_params=pltpu.CompilerParams(vmem_limit_bytes=60 * 2**20),
    )(place.reshape(1), branch, grouped)


def join(values, place, lines, cols):
    count, n = 8 // len(values), values[0].shape[1]
    if cols % 16 == 0:
        return move(True, values, place, lines, cols, n, count).reshape(-1, n)
    out = jnp.zeros((lines, 4, 2, cols, n), BF)
    for b in range(8):
        source = place ^ order(b)
        block = values[b // count].reshape(count, lines, 1, 1, cols, n)[b % count]
        out = lax.dynamic_update_slice(out, block, (0, source & 3, source >> 2, 0, 0))
    return out.reshape(-1, n)


def cut(value, place, lines, cols):
    n = value.shape[1]
    value = value.reshape(lines, 4, 2, cols, n)
    if cols % 16 == 0:
        return move(False, [value], place, lines, cols, n, 1)
    pieces = []
    for b in range(8):
        target = place ^ order(b)
        piece = lax.dynamic_slice(value, (0, target & 3, target >> 2, 0, 0), (lines, 1, 1, cols, n))
        pieces.append(piece.reshape(lines * cols, n))
    return pieces


def order(b):
    return (b // 2 % 2) * 4 + (b % 2) * 2 + b // 4


def gated(gate, upper, d_hidden):
    sig = 1.0 / (1.0 + jnp.exp(-gate))
    act = gate * sig
    hidden = (act * upper).astype(BF)
    d_gate = (d_hidden * upper * (sig * (1.0 + gate * (1.0 - sig)))).astype(BF)
    return hidden, d_gate, (d_hidden * act).astype(BF)


def ffn_kernel(counts, *refs):
    runs = len(counts)
    w_ref, hid_ref, dgu_ref, *sums = refs[2 * runs : -2]
    t, ends = pl.program_id(0), [sum(counts[: r + 1]) for r in range(runs)]

    for r in range(runs if runs > 1 else 0):

        @pl.when((t >= ends[r] - counts[r]) & (t < ends[r]))
        def _():
            refs[-2][...] = refs[r][...]
            refs[-1][...] = refs[runs + r][...]

    lines, wide = w_ref.shape[0], w_ref.shape[1] // 3
    w_gu = w_ref[:, : 2 * wide, :].reshape(-1, D)
    w_down = w_ref[:, 2 * wide :, :].reshape(-1, D)
    s, o = (refs[-2][...], refs[-1][...]) if runs > 1 else (refs[0][...], refs[1][...])
    gu = dot(s, w_gu, 1, 1)
    dh = dot(o, w_down, 1, 1)
    for z in range(lines):
        lo, mid, hi = 2 * z * wide, (2 * z + 1) * wide, (2 * z + 2) * wide
        cut_h = slice(z * wide, (z + 1) * wide)
        hidden, d_gate, d_up = gated(gu[:, lo:mid], gu[:, mid:hi], dh[:, cut_h])
        hid_ref[:, cut_h] = hidden
        dgu_ref[:, lo:mid] = d_gate
        dgu_ref[:, mid:hi] = d_up
    ds = dot(dgu_ref[...], w_gu, 1, 0).astype(BF)
    yo = dot(hid_ref[...], w_down, 1, 0).astype(BF)
    for r in range(runs):

        @pl.when((t >= ends[r] - counts[r]) & (t < ends[r]))
        def _():
            sums[2 * r][...] = ds
            sums[2 * r + 1][...] = yo


def ffn(sources, w_ffn, n, time):
    counts = [count for _, _, _, _, count in sources]
    rows, lines, wide = sum(counts) * n, w_ffn.shape[0], w_ffn.shape[1] // 3
    if wide % 128:
        second, d_ffn = (
            jnp.concatenate([src[i][src[2 + i] * n : (src[2 + i] + src[4]) * n] for src in sources], axis=0)
            for i in range(2)
        )
        w_gu = w_ffn[:, : 2 * wide].reshape(-1, D)
        w_down = w_ffn[:, 2 * wide :].reshape(-1, D)
        gu = dot(second, w_gu, 1, 1).reshape(rows, lines, 2, wide)
        dh = dot(d_ffn, w_down, 1, 1).reshape(rows, lines, wide)
        hidden, d_gate, d_up = gated(gu[:, :, 0], gu[:, :, 1], dh)
        hidden = hidden.reshape(rows, lines * wide)
        d_gu = jnp.stack([d_gate, d_up], axis=2).reshape(rows, 2 * lines * wide)
        ds, yo = dot(d_gu, w_gu, 1, 0).astype(BF), dot(hidden, w_down, 1, 0).astype(BF)
        at, sums = 0, []
        for count in counts:
            sums += [v[at : at + count * n] for v in (ds, yo)]
            at += count * n
        return [hidden, d_gu] + sums

    def spec(part, first):
        start, count = sum(counts[:part]), counts[part]
        return pl.BlockSpec((n, D), lambda t: (jnp.clip(t - start, 0, count - 1) + first, 0))

    out = lambda width: pl.BlockSpec((n, width), lambda t: (t, 0))
    return pl.pallas_call(
        functools.partial(ffn_kernel, counts),
        cost_estimate=cost(time),
        grid=(rows // n,),
        in_specs=[spec(p, src[2 + i]) for i in range(2) for p, src in enumerate(sources)]
        + [pl.BlockSpec(memory_space=pltpu.VMEM)],
        out_specs=[out(lines * wide), out(2 * lines * wide)]
        + [spec(p, 0) for p in range(len(sources)) for _ in range(2)],
        out_shape=[
            jax.ShapeDtypeStruct((rows, lines * wide), BF),
            jax.ShapeDtypeStruct((rows, 2 * lines * wide), BF),
        ]
        + [jax.ShapeDtypeStruct((src[4] * n, D), BF) for src in sources for _ in range(2)],
        scratch_shapes=[pltpu.VMEM((n, D), BF)] * 2,
        compiler_params=pltpu.CompilerParams(vmem_limit_bytes=58 * 2**20),
    )(*(src[i] for i in range(2) for src in sources), w_ffn)


def ffn_grad_kernel(runs, *refs):
    hid, dgu, sec, dff = (refs[i * runs : (i + 1) * runs] for i in range(4))
    out_ref, gu_ref, down_ref = refs[4 * runs :]

    @pl.when(pl.program_id(0) == 0)
    def _():
        start = 0
        for h, d in zip(hid, dgu):
            rows = h.shape[0]
            gu_ref[:, start : start + rows] = d[...].T
            down_ref[:, start : start + rows] = h[...].T
            start += rows

    lines, wide = out_ref.shape[0], out_ref.shape[1] // 3
    gu, down, start = 0.0, 0.0, 0
    for a, b in zip(sec, dff):
        rows = slice(start, start + a.shape[0])
        gu = gu + dot(gu_ref[:, rows], a[...], 1, 0)
        down = down + dot(down_ref[:, rows], b[...], 1, 0)
        start += a.shape[0]
    for z in range(lines):
        out_ref[z, : 2 * wide, :] = gu[2 * z * wide : 2 * (z + 1) * wide, :].astype(BF)
        out_ref[z, 2 * wide :, :] = down[z * wide : (z + 1) * wide, :].astype(BF)


def ffn_grad(hidden, d_gu, second, d_ffn, lines, wide):
    if wide % 128:
        rows = lambda group: [v[f * c : (f + 1) * c] for v, c, f in group]
        gu = sum(dot(a, b, 0, 0) for a, b in zip(rows(d_gu), rows(second))).reshape(lines, 2 * wide, D)
        down = sum(dot(a, b, 0, 0) for a, b in zip(rows(hidden), rows(d_ffn))).reshape(lines, wide, D)
        return jnp.concatenate([gu, down], axis=1).astype(BF)
    step = 256
    whole = [
        pl.BlockSpec((c, v.shape[1]), lambda t, f=f: (f, 0)) for v, c, f in (*hidden, *d_gu)
    ]
    slab = [pl.BlockSpec((c, step), lambda t, f=f: (f, t)) for _, c, f in (*second, *d_ffn)]
    out, tall = (lines, 3 * wide), sum(c for _, c, _ in hidden)
    return pl.pallas_call(
        functools.partial(ffn_grad_kernel, len(hidden)),
        cost_estimate=cost(14),
        grid=(D // step,),
        in_specs=whole + slab,
        out_specs=pl.BlockSpec(out + (step,), lambda t: (0, 0, t)),
        out_shape=jax.ShapeDtypeStruct(out + (D,), BF),
        scratch_shapes=[
            pltpu.VMEM((2 * lines * wide, tall), BF),
            pltpu.VMEM((lines * wide, tall), BF),
        ],
        compiler_params=pltpu.CompilerParams(vmem_limit_bytes=60 * 2**20),
    )(*(v for group in (hidden, d_gu, second, d_ffn) for v, _, _ in group))


def qkv_grad_kernel(count, *refs):
    parts, (near_ref, far_ref, out_ref, held) = refs[:count], refs[count:]
    n = parts[0].shape[1]

    @pl.when(pl.program_id(0) == 0)
    def _():
        for b, part in enumerate(parts):
            held[:, b * n : (b + 1) * n] = part[...]

    rows = near_ref.shape[0]
    out_ref[...] = (
        dot(held[:, :rows], near_ref[...], 1, 0) + dot(held[:, rows:], far_ref[...], 1, 0)
    ).astype(BF)


def qkv_grad(parts, near, far, cols):
    rows, n = parts[0].shape
    if cols % 16:
        half = len(parts) // 2
        grads = (jnp.concatenate(p, axis=1) for p in (parts[:half], parts[half:]))
        return sum(dot(g, v, 1, 0) for g, v in zip(grads, (near, far))).astype(BF)
    step = 256
    slab = pl.BlockSpec((near.shape[0], step), lambda t: (0, t))
    return pl.pallas_call(
        functools.partial(qkv_grad_kernel, len(parts)),
        cost_estimate=cost(6),
        grid=(D // step,),
        in_specs=[pl.BlockSpec((rows, n), lambda t: (0, 0))] * len(parts) + [slab, slab],
        out_specs=pl.BlockSpec((rows, step), lambda t: (0, t)),
        out_shape=jax.ShapeDtypeStruct((rows, D), BF),
        scratch_shapes=[pltpu.VMEM((rows, len(parts) * n), BF)],
        compiler_params=pltpu.CompilerParams(vmem_limit_bytes=60 * 2**20),
    )(*parts, near, far)


def normed_back_kernel(*refs):
    count = len(refs) // 2
    refs[-1][...] = sum(dot(p[...], w[...], 0, 0) for p, w in zip(refs[:count], refs[count:-1]))


def normed_back(parts, weights):
    vmem = pl.BlockSpec(memory_space=pltpu.VMEM)
    return pl.pallas_call(
        normed_back_kernel,
        cost_estimate=cost(1),
        in_specs=[vmem] * (2 * len(parts)),
        out_specs=vmem,
        out_shape=jax.ShapeDtypeStruct((parts[0].shape[1], D), F32),
        compiler_params=pltpu.CompilerParams(vmem_limit_bytes=60 * 2**20),
    )(*parts, *weights)


def input_back_kernel(*refs):
    p_ref, p2_ref, w_ref, w2_ref, before_ref, x_ref, dm_ref, gain_ref, out_ref, dgain_ref = refs
    d_normed = before_ref[...] + dot(p_ref[...], w_ref[...], 0, 0) + dot(p2_ref[...], w2_ref[...], 0, 0)
    d_in, dgain = rms_back(x_ref[...].astype(F32), gain_ref[...], d_normed)
    out_ref[...] = dm_ref[...] + d_in
    dgain_ref[...] = dgain[None]


def input_back(parts, weights, before, x, d_middle, gain):
    vmem = pl.BlockSpec(memory_space=pltpu.VMEM)
    return pl.pallas_call(
        input_back_kernel,
        cost_estimate=cost(5),
        in_specs=[vmem] * 8,
        out_specs=[vmem] * 2,
        out_shape=[jax.ShapeDtypeStruct(x.shape, F32), jax.ShapeDtypeStruct((1, D), F32)],
        compiler_params=pltpu.CompilerParams(vmem_limit_bytes=60 * 2**20),
    )(*parts, *weights, before, x, d_middle, gain.reshape(1, D))


def doc_masks(drow_ref, dcol_ref, allow_ref, same_ref):
    n = allow_ref.shape[0]
    row = lax.broadcasted_iota(jnp.int32, (n, n), 0)
    col = lax.broadcasted_iota(jnp.int32, (n, n), 1)
    same = dcol_ref[...] == drow_ref[...]
    same_ref[...] = jnp.where(same, 1.0, 0.0)
    allow_ref[...] = jnp.where(same & (col <= row), 1.0, 0.0)


def attend_kernel(
    mix_ref, q_ref, k_ref, v_ref, th_ref, tl_ref, drow_ref, dcol_ref, gain_ref, *refs
):
    prob_ref, att_ref, grp_ref, allow_ref, same_ref, pad_ref, xh_ref, xl_ref = refs[-8:]
    g = pl.program_id(0)
    n = q_ref.shape[1]

    @pl.when(g == 0)
    def _():
        doc_masks(drow_ref, dcol_ref, allow_ref, same_ref)
        pad_ref[:, 0:8, :] = jnp.zeros((2, 8, n), F32)

    for e in range(2):
        q = q_ref[e * HD : (e + 1) * HD, :]
        k = k_ref[e * HD : (e + 1) * HD, :]
        logits = dot(q, k, 0, 0) * (HD ** (-0.5))
        pad_ref[e, 8 : 8 + n, :] = jnp.where(allow_ref[...] > 0, logits, 0.0)
        for a in range(CQ):
            part = jnp.where(same_ref[...] > 0, pad_ref[e, 8 - a : 8 - a + n, :], 0.0)
            hi, lo = split(part)
            xh_ref[e, :, a * n : (a + 1) * n] = hi
            xl_ref[e, :, a * n : (a + 1) * n] = lo
        conv = (
            dot(xh_ref[e], th_ref[e], 1, 0)
            + dot(xh_ref[e], tl_ref[e], 1, 0)
            + dot(xl_ref[e], th_ref[e], 1, 0)
        )
        scores = jnp.where(allow_ref[...] > 0, conv, NEG)
        weights = jnp.exp(scores - jnp.max(scores, axis=1, keepdims=True))
        prob_ref[e] = weights * (1.0 / jnp.sum(weights, axis=1, keepdims=True))
    for c in range(2):
        mixed = (mix_ref[g, 2 * c] * prob_ref[0] + mix_ref[g, 2 * c + 1] * prob_ref[1]).astype(BF)
        att = dot(v_ref[c * HD : (c + 1) * HD, :], mixed, 1, 1)
        att_ref[c * HD : (c + 1) * HD, :] = att
        centre = att - jnp.mean(att, axis=0, keepdims=True)
        spread = jnp.mean(centre * centre, axis=0, keepdims=True)
        grp_ref[c * HD : (c + 1) * HD, :] = (
            centre * lax.rsqrt(spread + 1e-05) * gain_ref[c * HD : (c + 1) * HD, :]
        ).astype(BF)


def attend(packed_t, docs, th, tl, mix, gain, start, count, before=()):
    n = packed_t.shape[1]
    blk = lambda off: pl.BlockSpec((PW, n), lambda g: (g + off, 0))
    tap = pl.BlockSpec((2, CQ * n, n), lambda g: (g + start, 0, 0))
    whole = lambda s: pl.BlockSpec(s, lambda g: (0, 0))
    return pl.pallas_call(
        attend_kernel,
        cost_estimate=cost(0),
        grid=(count,),
        in_specs=[
            pl.BlockSpec(memory_space=pltpu.SMEM),
            blk(start), blk(PAIRS + start), blk(2 * PAIRS + start), tap, tap,
            whole((1, n)), whole((n, 1)),
            pl.BlockSpec((PW, 1), lambda g: (g + start, 0)),
        ]
        + [pl.BlockSpec(memory_space=pl.ANY)] * len(before),
        out_specs=[pl.BlockSpec((2, n, n), lambda g: (g, 0, 0)), blk(0), blk(start)],
        out_shape=[
            jax.ShapeDtypeStruct((2 * count, n, n), F32),
            jax.ShapeDtypeStruct((count * PW, n), F32),
            jax.ShapeDtypeStruct((D, n), BF),
        ],
        input_output_aliases={9: 2} if before else {},
        scratch_shapes=[
            pltpu.VMEM((n, n), F32), pltpu.VMEM((n, n), F32), pltpu.VMEM((2, n + 8, n), F32),
            pltpu.VMEM((2, n, CQ * n), BF), pltpu.VMEM((2, n, CQ * n), BF),
        ],
        compiler_params=pltpu.CompilerParams(vmem_limit_bytes=60 * 2**20),
    )(
        mix[start : start + count].reshape(count, 4), packed_t, packed_t, packed_t, th, tl,
        docs.reshape(1, n), docs.reshape(n, 1), gain, *before,
    )


def attend_back_kernel(
    mix_ref, q_ref, k_ref, v_ref, tt_ref, drow_ref, dcol_ref, gain_ref, prob_ref, att_ref, dgrp_ref,
    d_ref, dgain_ref, dtap_ref, dmix_ref,
    allow_ref, same_ref, pad_ref, y_ref, dm_ref,
):
    g = pl.program_id(0)
    n = q_ref.shape[1]
    scale = HD ** (-0.5)

    @pl.when(g == 0)
    def _():
        doc_masks(drow_ref, dcol_ref, allow_ref, same_ref)
        pad_ref[:, n : n + 8, :] = jnp.zeros((2, 8, n), F32)

    for c in range(2):
        rows = slice(c * HD, (c + 1) * HD)
        att = att_ref[rows, :]
        centre = att - jnp.mean(att, axis=0, keepdims=True)
        rstd = lax.rsqrt(jnp.mean(centre * centre, axis=0, keepdims=True) + 1e-05)
        hat = centre * rstd
        dgrp = dgrp_ref[rows, :]
        dgain_ref[rows, :] = jnp.sum(dgrp * hat, axis=1, keepdims=True)
        dhat = dgrp * gain_ref[rows, :]
        datt = rstd * (
            dhat
            - jnp.mean(dhat, axis=0, keepdims=True)
            - hat * jnp.mean(dhat * hat, axis=0, keepdims=True)
        )
        datt = datt.astype(BF)
        mixed = (mix_ref[g, 2 * c] * prob_ref[0] + mix_ref[g, 2 * c + 1] * prob_ref[1]).astype(BF)
        d_ref[2, rows, :] = dot(datt, mixed, 1, 0).astype(BF)
        dmixed = dot(datt, v_ref[rows, :], 0, 0)
        dm_ref[c] = dmixed
        for e in range(2):
            dmix_ref[0, 2 * c + e : 2 * c + e + 1, :] = jnp.sum(dmixed * prob_ref[e], axis=0, keepdims=True)
    dmix_ref[0, 4:8, :] = jnp.zeros((4, n), F32)
    row = lax.broadcasted_iota(jnp.int32, (128, 128), 0)
    col = lax.broadcasted_iota(jnp.int32, (128, 128), 1)
    off = col - row
    half = CK // 2
    for e in range(2):
        rows = slice(e * HD, (e + 1) * HD)
        q = q_ref[rows, :]
        k = k_ref[rows, :]
        allowed = allow_ref[...] > 0
        masked_t = dot(k, q, 0, 0) * scale
        prob = prob_ref[e]
        dprob = mix_ref[g, e] * dm_ref[0] + mix_ref[g, 2 + e] * dm_ref[1]
        pad_ref[e, 0:n, :] = prob * (dprob - jnp.sum(prob * dprob, axis=1, keepdims=True))
        for a in range(CQ):
            y_ref[e, :, a * n : (a + 1) * n] = jnp.where(same_ref[...] > 0, pad_ref[e, a : a + n, :], 0.0).astype(BF)
        dlog = jnp.where(allowed, dot(y_ref[e], tt_ref[e], 1, 0), 0.0).astype(BF)
        d_ref[0, rows, :] = (dot(k, dlog, 1, 1) * scale).astype(BF)
        d_ref[1, rows, :] = (dot(q, dlog, 1, 0) * scale).astype(BF)
        krow = lax.broadcasted_iota(jnp.int32, (n, n), 0)
        qcol = lax.broadcasted_iota(jnp.int32, (n, n), 1)
        masked_t = jnp.where((same_ref[...] > 0) & (krow <= qcol), masked_t, 0.0).astype(BF)
        for a in range(CQ):
            full = dot(masked_t, y_ref[e, :, a * n : (a + 1) * n], 1, 0)
            fold = jnp.zeros((128, 128), F32)
            blocks = n // 128
            for r in range(blocks):
                fold = fold + full[r * 128 : (r + 1) * 128, r * 128 : (r + 1) * 128]
            fold = jnp.where(jnp.abs(off) <= half, fold, 0.0)
            for r in range(blocks - 1):
                up = full[r * 128 : (r + 1) * 128, (r + 1) * 128 : (r + 2) * 128]
                down = full[(r + 1) * 128 : (r + 2) * 128, r * 128 : (r + 1) * 128]
                fold = fold + jnp.where(off <= half - 128, up, 0.0) + jnp.where(off >= 128 - half, down, 0.0)
            lined = fold[0:8, :]
            for t in range(1, 16):
                lined = lined + pltpu.roll(fold[8 * t : 8 * t + 8, :], 128 - 8 * t, 1)
            dtap_ref[e, 8 * a : 8 * a + 8, :] = lined


def attend_back(packed_t, docs, tt, mix, gain, prob, att, dgrp):
    n = packed_t.shape[1]
    blk = lambda off: pl.BlockSpec((PW, n), lambda g: (g + off, 0))
    whole = lambda s: pl.BlockSpec(s, lambda g: (0, 0))
    thin = pl.BlockSpec((PW, 1), lambda g: (g, 0))
    return pl.pallas_call(
        attend_back_kernel,
        cost_estimate=cost(24),
        grid=(PAIRS,),
        in_specs=[
            pl.BlockSpec(memory_space=pltpu.SMEM),
            blk(0), blk(PAIRS), blk(2 * PAIRS),
            pl.BlockSpec((2, CQ * n, n), lambda g: (g, 0, 0)),
            whole((1, n)), whole((n, 1)), thin,
            pl.BlockSpec((2, n, n), lambda g: (g, 0, 0)),
            blk(0), blk(0),
        ],
        out_specs=[
            pl.BlockSpec((3, PW, n), lambda g: (0, g, 0)), thin,
            pl.BlockSpec((2, 8 * CQ, 128), lambda g: (g, 0, 0)),
            pl.BlockSpec((1, 8, n), lambda g: (g, 0, 0)),
        ],
        out_shape=[
            jax.ShapeDtypeStruct((3, D, n), BF),
            jax.ShapeDtypeStruct((D, 1), F32),
            jax.ShapeDtypeStruct((H, 8 * CQ, 128), F32),
            jax.ShapeDtypeStruct((PAIRS, 8, n), F32),
        ],
        scratch_shapes=[
            pltpu.VMEM((n, n), F32), pltpu.VMEM((n, n), F32), pltpu.VMEM((2, n + 8, n), F32),
            pltpu.VMEM((2, n, CQ * n), BF), pltpu.VMEM((2, n, n), F32),
        ],
        compiler_params=pltpu.CompilerParams(vmem_limit_bytes=60 * 2**20),
    )(
        mix.reshape(PAIRS, 4), packed_t, packed_t, packed_t, tt,
        docs.reshape(1, n), docs.reshape(n, 1), gain, prob, att, dgrp,
    )


def fold_sums(dgain, dtap, dmix):
    lane = jnp.arange(128)[None, None, :] - jnp.arange(8)[None, :, None]
    tap = jnp.arange(CK)[:, None, None] - CK // 2
    pick = (jnp.remainder(lane - tap, 128) == 0).astype(F32)
    dtap = jnp.sum(dtap.reshape(H, CQ, 1, 8, 128) * pick, axis=(3, 4))
    dmix = jnp.sum(dmix[:, :4, :], axis=2)
    return jnp.concatenate([dgain[:, 0], dtap.reshape(-1), dmix.reshape(-1)])


def rms_norm(values, gain):
    return values * lax.rsqrt(jnp.mean(values * values, axis=-1, keepdims=True) + 1e-05) * gain


def rms_back(values, gain, grad):
    rstd = lax.rsqrt(jnp.mean(values * values, axis=-1, keepdims=True) + 1e-05)
    hat = values * rstd
    dhat = grad * gain
    dvalues = rstd * (dhat - hat * jnp.mean(dhat * hat, axis=-1, keepdims=True))
    return dvalues, jnp.sum(grad * hat, axis=0)


class Slice:
    def __init__(self, reps, shards):
        self.axes = ("rep", "fsdp")
        self.shards = shards
        self.lines = [[4 * o + i for o in range(shards // 4)] for i in range(4)]
        places = [(y, f) for y in range(reps) for f in range(shards)]

        def perm(move):
            out = []
            for y, f in places:
                to = move(y, f)
                out.append((y * shards + f, to[0] * shards + to[1]))
            return out

        self.hops = {
            (dy, di): perm(lambda y, f, dy=dy, di=di: (y ^ dy, f ^ di))
            for dy in range(2)
            for di in (range(16) if shards == 16 else range(4))
        }
        self.corner = perm(lambda y, f: (y, f ^ 2) if f & 1 else (1 - y, f))
        self.doubling = []
        bit = 1
        while bit < shards:
            self.doubling.append((bit, perm(lambda y, f, bit=bit: (y, f ^ bit))))
            bit *= 2
        self.rep = lax.axis_index("rep")
        self.fsdp = lax.axis_index("fsdp")
        self.odd = (self.fsdp & 1) == 1
        self.place = self.rep * 4 + (self.fsdp & 3)

    def hop(self, value, dy, di):
        return lax.ppermute(value, self.axes, self.hops[dy, di])

    def hop_block(self, value, b):
        return self.hop(value, order(b) >> 2, order(b) & 3) if b else value

    def gather_line(self, value):
        return lax.all_gather(value, "fsdp", axis=0, tiled=True, axis_index_groups=self.lines)

    def scatter_line(self, value):
        return lax.psum_scatter(
            value.astype(BF), "fsdp", scatter_dimension=0, tiled=True, axis_index_groups=self.lines
        )

    def gather_small(self, value):
        for bit, perm in self.doubling:
            other = lax.ppermute(value, self.axes, perm)
            high = (self.fsdp & bit) != 0
            value = jnp.concatenate(
                [jnp.where(high, other, value), jnp.where(high, value, other)], axis=0
            )
        return value

    def sides(self, value):
        return self.hop(value, 0, 2), self.hop(value, 1, 0)

    def far_corner(self, along_x, along_y):
        return lax.ppermute(jnp.where(self.odd, along_y, along_x), self.axes, self.corner)

    def near_blocks(self, value, along_x, along_y, corner):
        near = jnp.concatenate([value, along_x, along_y, jnp.zeros_like(value)], axis=0)
        return lax.dynamic_update_slice(near, corner, (3 * value.shape[0], 0))

    def scatter_corner(self, near, far):
        own, to_x, to_y, last = (a.astype(F32) + b.astype(F32) for a, b in zip(near, far))
        corner = lax.ppermute(last.astype(BF), self.axes, self.corner).astype(F32)
        to_x = (to_x + jnp.where(self.odd, 0.0, corner)).astype(BF)
        to_y = (to_y + jnp.where(self.odd, corner, 0.0)).astype(BF)
        return own, to_x, to_y

    def send_corner(self, near, far):
        return lax.ppermute((near.astype(F32) + far.astype(F32)).astype(BF), self.axes, self.corner)

    def with_corner(self, near, far, corner):
        corner = corner.astype(F32)
        to_x, to_y = (a.astype(F32) + b.astype(F32) for a, b in zip(near, far))
        to_x = (to_x + jnp.where(self.odd, 0.0, corner)).astype(BF)
        return to_x, (to_y + jnp.where(self.odd, corner, 0.0)).astype(BF)

    def scatter_last(self, own, to_x, to_y):
        return own + self.hop(to_x, 0, 2).astype(F32) + self.hop(to_y, 1, 0).astype(F32)

    def scatter_line_small(self, value):
        lines = self.shards // 4
        if lines != 4:
            return self.scatter_line(value).astype(F32)
        rows = value.shape[0] // lines
        value = value.astype(BF)
        line = self.fsdp // 4
        part = lambda d: lax.dynamic_slice_in_dim(value, (line ^ d) * rows, rows, axis=0)
        return sum([self.hop(part(d), 0, 4 * d).astype(F32) for d in range(1, 4)], part(0).astype(F32))

    def sum_small(self, value, bits):
        for bit, perm in self.doubling:
            if bit in bits:
                value = value + lax.ppermute(value, self.axes, perm)
        return value

    def both_halves(self, half, axis=0, other=None):
        if other is None:
            other = self.hop(half, 1, 0)
        first = self.rep == 0
        return jnp.concatenate(
            [jnp.where(first, half, other), jnp.where(first, other, half)], axis=axis
        ).astype(F32)

    def own_half(self, shard, rep=None):
        rows = shard.shape[0] // 2
        return lax.dynamic_slice_in_dim(shard, (self.rep if rep is None else rep) * rows, rows, axis=0)


def on_device(
    reps,
    shards,
    tokens,
    doc_ids,
    norm_gain,
    qkv_weight,
    group_gain,
    out_weight,
    ffn_gain,
    gate_weight,
    up_weight,
    down_weight,
    conv_kernel,
    head_mix,
    out_grad,
):
    net = Slice(reps, shards)
    lines = shards // 4
    n = tokens.shape[0]
    cols = 3 * D // shards // 2
    wide = gate_weight.shape[1] // 2

    half_out = D // shards // 2
    rows_of = lambda v: [v[b * n : (b + 1) * n] for b in range(v.shape[0] // n)]

    attn_half = jnp.concatenate([net.own_half(qkv_weight.T), net.own_half(out_weight.T)], axis=0)
    w_attn = net.gather_line(attn_half).reshape(lines, -1, D)
    ffn_half = jnp.concatenate(
        [net.own_half(v) for v in (gate_weight.T, up_weight.T, down_weight)], axis=0
    )
    w_ffn = net.gather_line(ffn_half).reshape(lines, -1, D)
    x_side = net.sides(tokens)
    d_low = out_grad.astype(BF)
    d_side = net.sides(d_low)
    taps = band_taps(conv_kernel, n)
    gains, *sides = fence(
        jnp.stack([norm_gain, group_gain, ffn_gain])[None], *x_side, *d_side, *taps
    )
    x_side, d_side, (taps_hi, taps_lo, taps_back) = sides[:2], sides[2:4], sides[4:]
    x_near = net.near_blocks(tokens, *x_side, net.far_corner(*x_side))
    x_far = net.hop(x_near, 0, 1)
    d_near = net.near_blocks(d_low, *d_side, net.far_corner(*d_side))
    gains = net.gather_small(gains)
    w_attn = fence(w_attn, time=100)[0]
    x_far = fence(x_far, time=40)[0]
    d_near = fence(d_near, time=60)[0]
    w_attn, d_near, gains = fence(w_attn, d_near, gains)
    gains = gains.transpose(1, 0, 2).reshape(3, D).astype(F32)
    w_cls = w_attn[:, cols:].reshape(-1, D)
    inputs = tokens.astype(F32)

    norm_near, parts = project(x_near, gains[0], w_attn, cols, n)
    norm_near, x_far, d_far, *parts = fence(norm_near, x_far, net.hop(d_near, 0, 1), *parts)
    norm_far, more = project(x_far, gains[0], w_attn, cols, n)
    pieces = [net.hop_block(p, b) for b, p in enumerate((*parts, *more))]
    pieces = fence(*pieces, time=45)
    w_qkv = w_attn[:, :cols].reshape(-1, D)
    *pieces, w_cls, d_far, w_qkv = fence(*pieces, w_cls, d_far, w_qkv)
    w_side = (*net.sides(w_cls), net.hop(w_cls, 1, 2))
    packed_t = join(pieces, net.place, lines, cols)
    group_col = gains[1].reshape(D, 1)
    *w_side, probs, attended, grouped = fence(
        *w_side,
        *attend(packed_t, doc_ids, taps_hi, taps_lo, head_mix, group_col, 0, PAIRS),
    )
    w_near = jnp.concatenate([w_cls, *w_side], axis=0)
    out_near, w_far = fence(out_blocks(grouped, w_near), net.hop(w_near, 0, 1))
    middle, second = out_project(
        grouped, w_near, w_far, out_near, inputs, gains[2], net.place, lines, half_out
    )
    w_near, w_far, second = fence(w_near, w_far, second)
    w_out = join([w_near, w_far], net.place, lines, half_out)
    *s_side, w_out = fence(*net.sides(second), w_out)
    s_corner = net.far_corner(*s_side)
    s_a = jnp.concatenate([second, s_side[0]], axis=0)
    far_a = net.hop(s_a, 0, 1)
    w_ffn = fence(w_ffn, time=40)[0]
    run_a = ffn([(s_a, d_near, 0, 0, 2)], w_ffn, n, 7)
    s_corner, far_a, w_qkv, *run_a = fence(s_corner, far_a, w_qkv, *run_a)
    w_side = net.sides(w_qkv)
    s_b = jnp.concatenate([s_side[1], s_corner], axis=0)
    far_b = net.hop(s_b, 0, 1)
    run_b = ffn([(s_b, d_near, 0, 2, 2)], w_ffn, n, 7)
    far_a, far_b, *run_b = fence(far_a, far_b, *run_b)
    run_f = ffn([(far_a, d_far, 0, 0, 2), (far_b, d_far, 0, 2, 2)], w_ffn, n, 2)
    ds_g, *w_side = fence(net.hop(run_f[4], 0, 1), *w_side)
    size_q = lines * cols // 2
    corner = net.send_corner(run_b[2][n:], ds_g[n:])
    ds_f, yo_f, yo_g = (net.hop(run_f[i], 0, 1) for i in (2, 3, 5))
    to_x, to_y = net.with_corner((run_a[2][n:], run_b[2][:n]), (ds_f[n:], ds_g[:n]), corner)
    last = (run_b[3][n:].astype(F32) + yo_g[n:].astype(F32)).astype(BF)
    to_x, to_y, last, *rest = fence(
        to_x, to_y, last, w_qkv, *w_side, w_side[1][:size_q], w_side[0][size_q:], *[r[i] for i in range(2) for r in (run_a, run_f, run_b)]
    )
    w_near, w_corner, acts = rest[:3], rest[3:5], rest[5:]
    w_far = [net.hop(w, 0, 1) for w in w_near]
    along_x, along_y = net.hop(to_x, 0, 2), net.hop(to_y, 1, 0)
    blocks = lambda a, f, b: [(a, 2 * n, 0), (f, 2 * n, 0), (f, 2 * n, 1), (b, 2 * n, 0)]
    g_ffn = ffn_grad(
        blocks(*acts[:3]),
        blocks(*acts[3:]),
        [(s_a, 2 * n, 0), (far_a, 2 * n, 0), (far_b, 2 * n, 0), (s_b, 2 * n, 0)],
        [(d_near, 2 * n, 0), (d_far, 2 * n, 0), (d_far, 2 * n, 1), (d_near, 2 * n, 1)],
        lines, wide,
    )
    along_x, along_y, last, g_ffn, *w_far = fence(along_x, along_y, last, g_ffn, *w_far)
    g_ffn = fence(net.scatter_line(g_ffn.reshape(-1, D)), time=80)[0]
    corner = lax.ppermute(last, net.axes, net.corner)
    d_middle, branch, d_grouped, g_ffn_gain = back_middle(
        run_a[2], ds_f, along_x, along_y, middle, out_grad, gains[2], w_out
    )
    d_grouped, *w_corner = fence(d_grouped, *w_corner)
    w_corner = (net.hop(w_corner[0], 0, 2), net.hop(w_corner[1], 1, 0))
    d_packed, g_group, g_taps, g_mix = attend_back(
        packed_t, doc_ids, taps_back, head_mix, group_col, probs, attended, d_grouped
    )
    d_packed, corner, *w_corner = fence(d_packed, corner, *w_corner)
    y_x, y_y = net.with_corner((run_a[3][n:], run_b[3][:n]), (yo_f[n:], yo_g[:n]), corner)
    w_near.append(jnp.concatenate(w_corner, axis=0))
    w_far.append(net.hop(w_near[3], 0, 1))
    pieces = cut(d_packed.reshape(3 * D, n), net.place, lines, cols)
    *cuts, branch = fence(*pieces, branch)
    pieces = [net.hop_block(p, b) for b, p in enumerate(cuts)]
    g_blocks = out_weight_grad(branch, grouped, net.place, lines, half_out)
    pieces = fence(*pieces, time=52)
    g_far, sums, w_near[3], w_far[3], y_x, y_y, *pieces = fence(
        net.hop(g_blocks[4], 0, 1), fold_sums(g_group, g_taps, g_mix), w_near[3], w_far[3], y_x, y_y, *pieces, *cuts
    )
    y_x, y_y = net.hop(y_x, 0, 2), net.hop(y_y, 1, 0)
    pieces, cuts = pieces[:8], pieces[8:]
    size = lines * half_out
    g_far = [g_far[b * size : (b + 1) * size] for b in range(4)]
    out_own, to_x, to_y = net.scatter_corner(g_blocks[:4], g_far)
    g_qkv, g_ffn, to_x, to_y, *cuts = fence(
        qkv_grad(pieces, norm_near, norm_far, cols), g_ffn, to_x, to_y, *cuts
    )
    g_qkv = fence(net.scatter_line(g_qkv), time=20)[0]
    g_other = net.hop(g_ffn, 1, 0)
    along_x, along_y = net.hop(to_x, 0, 2), net.hop(to_y, 1, 0)
    d_normed = normed_back([*cuts[:3], *cuts[4:7]], [*w_near[:3], *w_far[:3]])
    input_grad, g_norm = input_back([cuts[3], cuts[7]], [w_near[3], w_far[3]], d_normed, tokens, d_middle, gains[0])
    small = jnp.concatenate([g_norm[0], g_ffn_gain[0], sums])
    small = net.sum_small(small, [bit for bit, _ in net.doubling])
    g_other, y_x, y_y = fence(g_other, y_x, y_y, time=20)
    g_out = net.scatter_line_small(out_own + along_x.astype(F32) + along_y.astype(F32)).astype(BF)
    own = run_a[3][:n].astype(F32) + yo_f[:n].astype(F32)
    layer_out = (middle + (own + y_x.astype(F32) + y_y.astype(F32))).astype(BF)
    g_out, g_other, small, g_qkv = fence(g_out, g_other, small, g_qkv)
    q_other = net.hop(g_qkv, 1, 0)
    small = small + net.hop(small, 1, 0)
    g_out = net.both_halves(g_out).T
    shape = (3, wide, D)
    g_ffn = net.both_halves(g_ffn.reshape(shape), 1, g_other.reshape(shape))
    g_gate, g_up, g_down = g_ffn[0].T, g_ffn[1].T, g_ffn[2]
    g_qkv = net.both_halves(g_qkv, 0, q_other).T

    part = D // shards
    gain_grads = [
        lax.dynamic_slice_in_dim(small, b * D + net.fsdp * part, part) for b in (0, 2, 1)
    ]
    g_taps = small[3 * D : 3 * D + H * CQ * CK].reshape(H, CQ * CK)
    g_mix = small[3 * D + H * CQ * CK :].reshape(PAIRS, 2, 2)
    return (
        layer_out,
        input_grad,
        gain_grads[0],
        g_qkv,
        gain_grads[1],
        g_out,
        gain_grads[2],
        g_gate,
        g_up,
        g_down,
        g_taps,
        g_mix,
    )


def solution(mesh):
    placed = (
        P(("rep", "fsdp"), None),
        P(("rep", "fsdp")),
        P("fsdp"),
        P(None, "fsdp"),
        P("fsdp"),
        P(None, "fsdp"),
        P("fsdp"),
        P(None, "fsdp"),
        P(None, "fsdp"),
        P("fsdp", None),
        P(),
        P(),
        P(("rep", "fsdp"), None),
    )
    return jax.shard_map(
        functools.partial(on_device, mesh.shape["rep"], mesh.shape["fsdp"]),
        mesh=mesh,
        in_specs=placed,
        out_specs=(
            P(("rep", "fsdp"), None),
            P(("rep", "fsdp"), None),
            P("fsdp"),
            P(None, "fsdp"),
            P("fsdp"),
            P(None, "fsdp"),
            P("fsdp"),
            P(None, "fsdp"),
            P(None, "fsdp"),
            P("fsdp", None),
            P(),
            P(),
        ),
        check_vma=False,
    )
```
